256 devices in a mesh: gx: 16 (over y, z_lo), gy: 8 (over x, z_hi), gz: 2 (over core).
Axes of the slice: x: 4, y: 4, z: 8 (z_hi: 2, z_lo: 4; z = z_hi * 4 + z_lo), core: 2. Of those that a mesh axis runs over, the one named last changes fastest.
Arguments:
- adjoint_start: float32 [5, 125, 32768], P(None, None, ('gx', 'gy', 'gz')), may hold values from -6 to 6
- adjoint_source: float32 [5, 125, 32768], P(None, None, ('gx', 'gy', 'gz')), may hold values from -24 to 24
- density: float32 [125, 32768], P(None, ('gx', 'gy', 'gz')), may hold values from 0.5 to 2
- velocity: float32 [3, 125, 32768], P(None, None, ('gx', 'gy', 'gz')), may hold values from -2.5 to 2.5
- pressure: float32 [125, 32768], P(None, ('gx', 'gy', 'gz')), may hold values from 0.5 to 2
- pseudo_shift: float32 [32, 64, 16], P('gx', 'gy', 'gz'), may hold values from 8 to 16
- block_inverse: float32 [5, 5, 32, 64, 16], P(None, None, 'gx', 'gy', 'gz'), may hold values from -0.02 to 0.12, as said below
Outputs:
- adjoint: float32 [5, 125, 32768], P(None, None, ('gx', 'gy', 'gz'))
The draws below stay inside these ranges and needn't reach their ends.
Inputs may be any that keep to these rules, and one draw needn't show every extreme that they name: `block_inverse`: diagonal entries lie in 0.06 to 0.12, the others within 0.02 of zero.
All inputs are finite; a program needn't handle non-finite values.
Results may differ from the reference program's by a relative error of at most 0.0001.
Values sent between devices are 32-bit elements; how exact they have to be, the bound alone decides.
A program may use at most 64 MiB of HBM per device.

```python
import math
import jax
import jax.numpy as jnp
import numpy as np
from jax import lax

VARS = 5
FINE_NODES = 5
EX = 2
EY = 8
EZ = 8
NX = 32
NY = 64
NZ = 16
N_GX = 16
N_GY = 8
N_GZ = 2


def draw_block_inverse(key, part):
    key = jax.random.fold_in(key, 7)
    first_key, second_key = jax.random.split(key)
    diagonal = jnp.exp(jax.random.uniform(first_key, (VARS, NX, NY, NZ), jnp.float32, math.log(0.06), math.log(0.12)))
    others = jax.random.uniform(second_key, (VARS, VARS, NX, NY, NZ), jnp.float32, -0.02, 0.02)
    identity = jnp.eye(VARS, dtype=jnp.float32)[:, :, None, None, None]
    return others * (1.0 - identity) + identity * diagonal[:, None]


def block_levels(stream_key, dims, pieces, smallest, top_value):
    def one(dim, blocks):
        draws = jax.random.uniform(jax.random.fold_in(jax.random.fold_in(stream_key, 6), dim), (blocks,), jnp.float32, smallest / len(pieces), top_value / len(pieces))
        return jnp.repeat(jnp.exp(draws), dims[dim] // blocks).reshape((-1,) + (1,) * (len(dims) - dim - 1))

    gain = one(*pieces[0])
    for cut in pieces[1:]:
        gain = gain * one(*cut)
    return gain


def scatter_about(key, extent, spread, limit, pieces=(), kind=jnp.bfloat16):
    loudness = block_levels(key, extent, pieces, -0.22, 0.18) if pieces else 1.0
    values = jax.random.normal(key, extent, jnp.float32) * spread * loudness
    return jnp.minimum(jnp.maximum(values, -limit), limit).astype(kind)


def setup_inputs(seed: int = 0) -> dict:
    arg_keys = jax.random.split(jax.random.key(seed), 8)
    return {
        "adjoint_start": scatter_about(arg_keys[0], (VARS, FINE_NODES ** 3, NX * NY * NZ), 1.0, 6.0, ((2, 256),), jnp.float32),
        "adjoint_source": scatter_about(arg_keys[1], (VARS, FINE_NODES ** 3, NX * NY * NZ), 4.0, 24.0, ((2, 256),), jnp.float32),
        "density": jnp.clip(jnp.exp(math.log(2.0) - 1.3862944 * jax.random.uniform(arg_keys[2], (FINE_NODES ** 3, NX * NY * NZ), jnp.float32) ** block_levels(arg_keys[2], (FINE_NODES ** 3, NX * NY * NZ), ((1, 256),), -0.2, 0.2)), 0.5, 2.0),
        "velocity": scatter_about(arg_keys[3], (3, FINE_NODES ** 3, NX * NY * NZ), 0.4, 2.5, ((2, 256),), jnp.float32),
        "pressure": jnp.clip(jnp.exp(math.log(2.0) - 1.3862944 * jax.random.uniform(arg_keys[4], (FINE_NODES ** 3, NX * NY * NZ), jnp.float32) ** block_levels(arg_keys[4], (FINE_NODES ** 3, NX * NY * NZ), ((1, 256),), -0.2, 0.2)), 0.5, 2.0),
        "pseudo_shift": jnp.clip(jnp.exp(math.log(16.0) - 0.6931472 * jax.random.uniform(arg_keys[5], (NX, NY, NZ), jnp.float32) ** block_levels(arg_keys[5], (NX, NY, NZ), ((0, 16), (1, 8), (2, 2)), -0.2, 0.2)), 8.0, 16.0),
        "block_inverse": draw_block_inverse(jax.random.fold_in(arg_keys[7], 71), 0),
    }


GAMMA = 1.4
OMEGA = 0.7
METRIC = 0.25

def diff_table(nodes):
    count = len(nodes)
    weights = np.array([1.0 / np.prod([nodes[j] - nodes[k] for k in range(count) if k != j]) for j in range(count)])
    table = np.zeros((count, count))
    for i in range(count):
        for j in range(count):
            if i != j:
                table[i, j] = weights[j] / weights[i] / (nodes[i] - nodes[j])
        table[i, i] = -np.sum(table[i])
    return table.astype(np.float32)

def fine_points():
    return np.array([-1.0, -np.sqrt(3.0 / 7.0), 0.0, np.sqrt(3.0 / 7.0), 1.0])

def interp_table():
    points = fine_points()
    return np.stack([points * (points - 1.0) / 2.0, 1.0 - points ** 2, points * (points + 1.0) / 2.0], axis=1).astype(np.float32)

def to_grid(field, groups_x, groups_y, groups_z, elem_x, elem_y, elem_z):
    lead = field.shape[:-2]
    k = len(lead)
    split = field.reshape(lead + (5, 5, 5, groups_x, groups_y, groups_z, elem_x, elem_y, elem_z))
    order = tuple(range(k)) + (k + 3, k + 6, k, k + 4, k + 7, k + 1, k + 5, k + 8, k + 2)
    moved = jnp.transpose(split, order)
    return moved.reshape(lead + (groups_x * elem_x * 5, groups_y * elem_y * 5, groups_z * elem_z * 5))

def from_grid(field, groups_x, groups_y, groups_z, elem_x, elem_y, elem_z):
    lead = field.shape[:-3]
    k = len(lead)
    split = field.reshape(lead + (groups_x, elem_x, 5, groups_y, elem_y, 5, groups_z, elem_z, 5))
    order = tuple(range(k)) + (k + 2, k + 5, k + 8, k, k + 3, k + 6, k + 1, k + 4, k + 7)
    moved = jnp.transpose(split, order)
    return moved.reshape(lead + (125, groups_x * groups_y * groups_z * elem_x * elem_y * elem_z))

def along(field, matrix, axis, count):
    shape = field.shape
    split = shape[:axis] + (shape[axis] // count, count) + shape[axis + 1:]
    moved = jnp.tensordot(field.reshape(split), jnp.asarray(matrix), axes=([axis + 1], [0]), precision=lax.Precision.HIGHEST)
    moved = jnp.moveaxis(moved, -1, axis + 1)
    return moved.reshape(shape[:axis] + (moved.shape[axis] * moved.shape[axis + 1],) + shape[axis + 1:])

def inject(field, axis, count):
    shape = field.shape
    split = field.reshape(shape[:axis] + (shape[axis] // count, count) + shape[axis + 1:])
    taken = lax.slice_in_dim(split, 0, count, 2, axis + 1)
    return taken.reshape(shape[:axis] + (taken.shape[axis] * taken.shape[axis + 1],) + shape[axis + 1:])

def conserved(density, velocity, pressure):
    kinetic = 0.5 * density * lax.optimization_barrier(jnp.sum(velocity * velocity, axis=0))
    return jnp.concatenate([density[None], density[None] * velocity, (pressure / (GAMMA - 1.0) + kinetic)[None]], axis=0)

def flux_all(state):
    dens = state[0]
    speeds = state[1:4] / dens
    press = (GAMMA - 1.0) * (state[4] - 0.5 * dens * lax.optimization_barrier(jnp.sum(speeds * speeds, axis=0)))
    result = []
    for axis_id in range(3):
        parts = [state[1 + axis_id]]
        for comp in range(3):
            extra = press if comp == axis_id else 0.0
            parts.append(state[1 + comp] * speeds[axis_id] + extra)
        parts.append((state[4] + press) * speeds[axis_id])
        result.append(jnp.stack(parts))
    return tuple(result)

def expand(values, count):
    ex, ey, ez = values.shape
    wide = jnp.broadcast_to(values[:, None, :, None, :, None], (ex, count, ey, count, ez, count))
    return wide.reshape(ex * count, ey * count, ez * count)

def precondition(resid, inverse, count):
    vars_n, lx, ly, lz = resid.shape
    blocks = resid.reshape(vars_n, lx // count, count, ly // count, count, lz // count, count)
    out = jnp.einsum('baxyz,bxiyjzk->axiyjzk', inverse, blocks, precision=lax.Precision.HIGHEST)
    return out.reshape(resid.shape)

def operate(field, state, shift_nodes, count, neighbours):
    table = diff_table(fine_points() if count == 5 else np.array([-1.0, 0.0, 1.0]))
    face = 0.25 / (0.1 if count == 5 else 1.0 / 3.0)
    dens = state[0]
    speeds = state[1:4] / dens
    press = (GAMMA - 1.0) * (state[4] - 0.5 * dens * lax.optimization_barrier(jnp.sum(speeds * speeds, axis=0)))
    sound = jnp.sqrt(GAMMA * press / dens)
    cotangents = []
    penalty = jnp.zeros_like(field)
    for axis_id in range(3):
        axis = axis_id + 1
        after, before = neighbours[axis_id]
        length = field.shape[axis]
        place = jnp.arange(length) % count
        bshape = [1, 1, 1, 1]
        bshape[axis] = length
        upper = (place == count - 1).astype(jnp.float32).reshape(bshape)
        lower = (place == 0).astype(jnp.float32).reshape(bshape)
        jump_up = upper * (field - after)
        jump_low = lower * (field - before)
        cotangents.append(-METRIC * along(field, table, axis, count) + 0.5 * face * (jump_up - jump_low))
        speed_max = jnp.abs(speeds[axis_id]) + sound
        penalty = penalty + 0.5 * face * speed_max[None] * (jump_up + jump_low)
    _, pull = jax.vjp(flux_all, state)
    adjoint_part, = pull(tuple(cotangents))
    return shift_nodes[None] * field + adjoint_part + penalty

def local_neighbours(field):
    padded = jnp.pad(field, ((0, 0), (1, 1), (1, 1), (1, 1)))
    return ((padded[:, 2:, 1:-1, 1:-1], padded[:, :-2, 1:-1, 1:-1]), (padded[:, 1:-1, 2:, 1:-1], padded[:, 1:-1, :-2, 1:-1]), (padded[:, 1:-1, 1:-1, 2:], padded[:, 1:-1, 1:-1, :-2]))

def reference(adjoint_start, adjoint_source, density, velocity, pressure, pseudo_shift, block_inverse):

    def grid(field):
        return to_grid(field, N_GX, N_GY, N_GZ, EX, EY, EZ)
    adjoint_start = grid(adjoint_start)
    adjoint_source = grid(adjoint_source)
    state = conserved(grid(density), grid(velocity), grid(pressure))
    shift_fine = expand(pseudo_shift, 5)
    shift_coarse = expand(pseudo_shift, 3)
    prolong = interp_table()

    def fine_op(field):
        return operate(field, state, shift_fine, 5, local_neighbours(field))
    first = adjoint_start + OMEGA * precondition(adjoint_source - fine_op(adjoint_start), block_inverse, 5)
    resid = adjoint_source - fine_op(first)
    coarse_rhs = along(along(along(resid, prolong, 1, 5), prolong, 2, 5), prolong, 3, 5)
    coarse_state = inject(inject(inject(state, 1, 5), 2, 5), 3, 5)
    coarse_one = OMEGA * precondition(coarse_rhs, block_inverse, 3)
    coarse_res = coarse_rhs - operate(coarse_one, coarse_state, shift_coarse, 3, local_neighbours(coarse_one))
    coarse_two = coarse_one + OMEGA * precondition(coarse_res, block_inverse, 3)
    back = prolong.T
    second = first + along(along(along(coarse_two, back, 1, 3), back, 2, 3), back, 3, 3)
    result = second + OMEGA * precondition(adjoint_source - fine_op(second), block_inverse, 5)
    return from_grid(result, N_GX, N_GY, N_GZ, EX, EY, EZ)
```

```python
import itertools

import jax
import jax.numpy as jnp
import ml_dtypes
import numpy as np
from jax import lax
from jax.experimental import pallas as pl
from jax.experimental.pallas import tpu as pltpu
from jax.sharding import PartitionSpec as P

OMEGA = 0.7
METRIC = 0.25
FINE_FACE = 0.5 * 0.25 / 0.1
COARSE_FACE = 0.5 * 0.25 * 3.0
MESH = pl.DeviceIdType.MESH
AXES = ("gx", "gy", "gz")
COUNTS = (2, 8, 8)
STRIDES = (64, 8, 1)
F32 = jnp.float32
BF16 = jnp.bfloat16


def diff_table(nodes):
    count = len(nodes)
    weights = np.array(
        [1.0 / np.prod([nodes[j] - nodes[k] for k in range(count) if k != j]) for j in range(count)]
    )
    table = np.zeros((count, count))
    for i in range(count):
        for j in range(count):
            if i != j:
                table[i, j] = weights[j] / weights[i] / (nodes[i] - nodes[j])
        table[i, i] = -np.sum(table[i])
    return table.astype(np.float32).astype(np.float64)


def fine_points():
    return np.array([-1.0, -np.sqrt(3.0 / 7.0), 0.0, np.sqrt(3.0 / 7.0), 1.0])


def interp_table():
    points = fine_points()
    table = np.stack(
        [points * (points - 1.0) / 2.0, 1.0 - points**2, points * (points + 1.0) / 2.0], axis=1
    )
    return table.astype(np.float32).astype(np.float64)


def triple(a, b, c):
    return np.kron(np.kron(a, b), c)


def padded(matrix, rows, columns):
    result = np.zeros((rows, columns))
    result[: matrix.shape[0], : matrix.shape[1]] = matrix
    return result


def face_tables(count, rows, width):
    take = np.zeros((6 * rows, width))
    give = np.zeros((width, 6 * rows))
    for dim in range(3):
        for side in range(2):
            face = 2 * dim + side
            for row in range(rows):
                a, b = divmod(min(row, count * count - 1), count)
                place = [a, b]
                place.insert(dim, side * (count - 1))
                node = (place[0] * count + place[1]) * count + place[2]
                take[face * rows + row, node] = 1.0
                if row < count * count:
                    give[node, face * rows + row] = 1.0
    return take, give


def volume_table(count, width):
    table = diff_table(fine_points() if count == 5 else np.array([-1.0, 0.0, 1.0]))
    unit = np.eye(count)
    parts = []
    for dim in range(3):
        mats = [unit, unit, unit]
        mats[dim] = -METRIC * table.T
        parts.append(padded(triple(*mats), width, width))
    return np.concatenate(parts)


def two(matrix):
    high = matrix.astype(ml_dtypes.bfloat16)
    return np.concatenate([high, high], axis=1)


def three(matrix):
    high = matrix.astype(ml_dtypes.bfloat16)
    low = (matrix - high.astype(np.float64)).astype(ml_dtypes.bfloat16)
    return np.concatenate([high, high, low], axis=1)


def tables():
    prolong = interp_table()
    take, give = face_tables(5, 32, 128)
    take_c, give_c = face_tables(3, 16, 32)
    pick = np.zeros((32, 128))
    for n, (a, b, c) in enumerate(itertools.product(range(3), repeat=3)):
        pick[n, (2 * a * 5 + 2 * b) * 5 + 2 * c] = 1.0
    restrict = padded(triple(prolong.T, prolong.T, prolong.T), 32, 128)
    restrict = np.concatenate([restrict, take_c @ restrict])
    extend = padded(triple(prolong, prolong, prolong), 128, 32)
    flat = np.kron(prolong, prolong)
    flat = np.concatenate([flat, np.repeat(flat[24:25], 7, axis=0)])
    face_extend = np.zeros((192, 96))
    for face in range(6):
        face_extend[32 * face : 32 * face + 32, 16 * face : 16 * face + 9] = flat
    return {
        "take": two(np.concatenate([take, pick, take_c @ pick])),
        "volume": three(volume_table(5, 128)),
        "give": two(-FINE_FACE * np.concatenate([take @ give, give])),
        "restrict": three(restrict),
        "restrict_give": three(-FINE_FACE * restrict @ give),
        "volume_c": two(np.concatenate([volume_table(3, 32), take_c])),
        "give_c": two(-COARSE_FACE * np.concatenate([take_c @ give_c, give_c])),
        "extend": three(extend),
        "face_extend": three(face_extend),
    }


def dot(matrix, field):
    return jnp.dot(matrix, field, preferred_element_type=F32)


def split(value):
    high = value.astype(BF16)
    low = (value - high.astype(F32)).astype(BF16)
    return high, low


def lanes(var):
    return slice(128 * var, 128 * var + 128)


def rows_of(step, size=16):
    return pl.ds(pl.multiple_of(step * size, size), size)


def load(ref, rows):
    return [ref[rows, lanes(v)] for v in range(5)]


def store(ref, rows, values):
    for v in range(5):
        ref[rows, lanes(v)] = values[v]


def store_split(ref, step, height, values, pieces):
    for v in range(5):
        parts = split(values[v])
        for piece in range(pieces):
            ref[rows_of(step + piece * (height // 16)), lanes(v)] = parts[piece % 2]


def pull_all(cot, state):
    w = state[:3]
    enthalpy = state[3]
    crossed = [w[0] * c[1] + w[1] * c[2] + w[2] * c[3] + enthalpy * c[4] for c in cot]
    ends = [w[d] * cot[d][4] for d in range(3)]
    energy = ends[0] + ends[1] + ends[2]
    total = 0.4 * (cot[0][1] + cot[1][2] + cot[2][3] + energy)
    half_square = 0.5 * (w[0] * w[0] + w[1] * w[1] + w[2] * w[2])
    first = half_square * total - (w[0] * crossed[0] + w[1] * crossed[1] + w[2] * crossed[2])
    middle = []
    for j in range(3):
        drift = w[0] * cot[0][1 + j] + w[1] * cot[1][1 + j] + w[2] * cot[2][1 + j]
        middle.append(drift + cot[j][0] + crossed[j] - w[j] * total)
    return [first, *middle, total + energy]


def pull_face(jump, state, speed, normal, pick, sign):
    w = state[:3]
    crossed = w[0] * jump[1] + w[1] * jump[2] + w[2] * jump[3] + state[3] * jump[4]
    end = speed * jump[4]
    total = 0.4 * (normal + end)
    half_square = 0.5 * (w[0] * w[0] + w[1] * w[1] + w[2] * w[2])
    turned = jump[0] + crossed
    out = [half_square * total - speed * crossed]
    for j in range(3):
        out.append(speed * jump[1 + j] - w[j] * total + pick[j] * turned)
    out.append(total + end)
    top = jnp.abs(speed) + state[4]
    return [sign * out[v] + top * jump[v] for v in range(5)]


def apply_blocks(blocks, values):
    result = []
    for a in range(5):
        total = blocks[a] * values[0]
        for b in range(1, 5):
            total = total + blocks[b * 5 + a] * values[b]
        result.append(total)
    return result


def kernel(start_h, source_h, density_h, velocity_h, pressure_h, shift_h, inverse_h, *rest):
    tables_h, rest = rest[:9], rest[9:]
    out_h, rest = rest[0], rest[1:]
    (start_r, source_r, density_r, velocity_r, pressure_r, shift_r, inverse_r), rest = rest[:7], rest[7:]
    tables_r, rest = rest[:9], rest[9:]
    (take, volume, give, restrict, restrict_give, volume_c, give_c, extend, face_extend) = tables_r
    (
        field, source, state, base, split_n, cot,
        face_state, face_field, jump, split_f, compact, own,
        state_c, field_c, base_c, split_c, split_cf, cot_c, jump_c, compact_c, own_c,
        blocks, shift, out_r,
    ), rest = rest[:24], rest[24:]
    send_fine, recv_fine, send_coarse, recv_coarse, rest = rest[:6], rest[6:12], rest[12:18], rest[18:24], rest[24:]
    in_sems, out_sem, send_sems, recv_sems = rest

    place = [lax.axis_index(axis) for axis in AXES]
    size = [lax.axis_size(axis) for axis in AXES]
    has = [place[f // 2] > 0 if f % 2 == 0 else place[f // 2] < size[f // 2] - 1 for f in range(6)]

    def partner(f):
        target = list(place)
        target[f // 2] = target[f // 2] + (1 if f % 2 else -1)
        return tuple(target)

    barrier = pltpu.get_barrier_semaphore()
    for f in range(6):
        @pl.when(has[f])
        def _(f=f):
            pl.semaphore_signal(barrier, inc=1, device_id=partner(f), device_id_type=MESH)

    field[120:128, :] = jnp.zeros((8, 640), F32)
    source[120:128, :] = jnp.zeros((8, 640), F32)
    order = [
        (start_h, start_r), (tables_h[0], take), (velocity_h, velocity_r), (density_h, density_r),
        (pressure_h, pressure_r), (tables_h[1], volume), (source_h, source_r), (shift_h, shift_r),
        (inverse_h, inverse_r), (tables_h[2], give),
    ] + [(tables_h[n], tables_r[n]) for n in range(3, 9)]
    inward = [pltpu.make_async_copy(a, b, in_sems.at[n]) for n, (a, b) in enumerate(order)]
    for copy in inward:
        copy.start()

    def lane_place(rows, dim):
        lane = lax.broadcasted_iota(jnp.int32, (rows, 128), 1)
        return (lane // STRIDES[dim]) % COUNTS[dim]

    def gather_faces(source_ref, offset, rows, whole, target):
        sub = lax.broadcasted_iota(jnp.int32, (8, 128), 0)

        def one(f, _):
            top = offset + f * rows
            last = source_ref[pl.ds(pl.multiple_of(top + whole, 8), 8), lanes(0)]
            for v in range(5):
                target[f, whole * v : whole * v + whole, :] = source_ref[
                    pl.ds(pl.multiple_of(top, 8), whole), lanes(v)
                ]
                if v:
                    here = source_ref[pl.ds(pl.multiple_of(top + whole, 8), 8), lanes(v)]
                    last = jnp.where(sub == v, here, last)
            target[f, 5 * whole : 5 * whole + 8, :] = last
            return 0

        lax.fori_loop(0, 6, one, 0)

    def scatter_faces(source_ref, rows, whole, target):
        def one(f, _):
            top = f * rows
            for v in range(5):
                target[pl.ds(pl.multiple_of(top, 8), whole), lanes(v)] = source_ref[
                    f, whole * v : whole * v + whole, :
                ]
                target[pl.ds(pl.multiple_of(top + whole, 8), 8), lanes(v)] = jnp.broadcast_to(
                    source_ref[f, pl.ds(5 * whole + v, 1), :], (8, 128)
                )
            return 0

        lax.fori_loop(0, 6, one, 0)

    def turn(value, amount):
        amount %= 128
        return pltpu.roll(value, amount, 1) if amount else value

    def copies(exchange, sends, receives):
        row = exchange + (2 if sends is send_coarse else 0)
        return [
            pltpu.make_async_remote_copy(
                src_ref=sends[f].at[exchange],
                dst_ref=receives[f ^ 1].at[exchange],
                send_sem=send_sems.at[row, f],
                recv_sem=recv_sems.at[row, f ^ 1],
                device_id=partner(f),
                device_id_type=MESH,
            )
            for f in range(6)
        ]

    def send(exchange, faces, sends, remote):
        for f in range(6):
            dim, side = divmod(f, 2)
            count, stride = COUNTS[dim], STRIDES[dim]
            slot = sends[f].shape[1]
            where = lane_place(slot, dim)
            packed = None
            for g in range(faces.shape[1] // slot):
                block = turn(faces[f, g * slot : g * slot + slot, :], (g - side * (count - 1)) * stride)
                packed = block if packed is None else jnp.where(where == g, block, packed)
            sends[f][exchange] = packed
            if exchange == 0 and sends is send_fine and f == 0:
                pl.semaphore_wait(barrier, sum(h.astype(jnp.int32) for h in has))

            @pl.when(has[f])
            def _():
                remote[f].start()

    def own_part(faces, result):
        for f in range(6):
            dim, side = divmod(f, 2)
            count, stride = COUNTS[dim], STRIDES[dim]
            inside = lane_place(faces.shape[1], dim) != side * (count - 1)
            other = turn(faces[f ^ 1], -stride if side else stride)
            result[f] = faces[f] - jnp.where(inside, other, 0.0)

    def receive(exchange, receives, remote, result, target):
        for f in range(6):
            dim, side = divmod(f, 2)
            count, stride = COUNTS[dim], STRIDES[dim]
            slot = receives[f].shape[1]
            edge = lane_place(slot, dim) == side * (count - 1)

            @pl.when(has[f])
            def _():
                remote[f ^ 1].wait_recv()
                packed = receives[f][exchange]
                for g in range(result.shape[1] // slot):
                    here = slice(g * slot, g * slot + slot)
                    there = turn(packed, (side * (count - 1) - g) * stride)
                    target[f, here, :] = result[f, here, :] - jnp.where(edge, there, 0.0)

            @pl.when(jnp.logical_not(has[f]))
            def _():
                target[f] = result[f]

    def face_pull(step, values, state_ref, offset, per_face):
        f = lax.div(step, per_face)
        d = lax.div(f, 2)
        sign = (2 * (f - 2 * d) - 1).astype(F32)
        pick = [(d == j).astype(F32) for j in range(3)]
        rows = rows_of(step + offset)
        local = load(state_ref, rows)
        speed = state_ref[rows, pl.ds(pl.multiple_of(d * 128, 128), 128)]
        normal = pick[0] * values[1] + pick[1] * values[2] + pick[2] * values[3]
        return pull_face(values, local, speed, normal, pick, sign)

    def block_rows():
        return [blocks[n] for n in range(25)]

    inward[0].wait()
    for v in range(5):
        field[0:125, lanes(v)] = start_r[v]

    def split_field(step, _):
        store_split(split_n, step, 128, load(field, rows_of(step)), 3)
        return 0

    lax.fori_loop(0, 8, split_field, 0)
    inward[1].wait()
    face_field[...] = dot(take[0:192, :], split_n[0:256, :])
    gather_faces(face_field, 0, 32, 24, compact)
    fine_0 = copies(0, send_fine, recv_fine)
    send(0, compact, send_fine, fine_0)

    for n in (2, 3, 4):
        inward[n].wait()
    state[120:128, :] = jnp.zeros((8, 640), F32)
    for part in ((0, 64), (64, 125)):
        here = slice(*part)
        w = [velocity_r[d, here, :] for d in range(3)]
        sound_2 = 1.4 * pressure_r[here, :] / density_r[here, :]
        for d in range(3):
            state[here, lanes(d)] = w[d]
        state[here, lanes(3)] = 2.5 * sound_2 + 0.5 * (w[0] * w[0] + w[1] * w[1] + w[2] * w[2])
        state[here, lanes(4)] = jnp.sqrt(sound_2)

    def split_state(step, _):
        store_split(split_f, step, 128, load(state, rows_of(step)), 2)
        return 0

    lax.fori_loop(0, 8, split_state, 0)
    face_state[...] = dot(take[0:192, :], split_f[0:256, :])
    state_c[...] = dot(take[192:320, :], split_f[0:256, :])
    own_part(compact, own)

    for n in (7, 8):
        inward[n].wait()
    spread = (
        lax.broadcasted_iota(jnp.int32, (8, 128), 1) % 8 == lax.broadcasted_iota(jnp.int32, (8, 128), 0)
    ).astype(F32)

    def to_lanes(value, count):
        wide = jnp.dot(
            value.reshape(16 * count, 8), spread,
            precision=lax.Precision.HIGHEST, preferred_element_type=F32,
        ).reshape(count, 16, 128)
        row = lax.broadcasted_iota(jnp.int32, (count, 16, 128), 1)
        lane = lax.broadcasted_iota(jnp.int32, (count, 16, 128), 2)
        kept = jnp.where(lane // 8 == row, wide, 0.0)
        return jnp.broadcast_to(jnp.sum(kept, axis=1, keepdims=True), (count, 16, 128))

    shift[...] = to_lanes(shift_r[...], 1)[0]
    blocks[...] = OMEGA * to_lanes(inverse_r[...], 25)

    inward[5].wait()
    inward[6].wait()
    for v in range(5):
        source[0:125, lanes(v)] = source_r[v]

    def residual(step, height, cot_ref, values, right, state_ref):
        rows = rows_of(step)
        cots = [load(cot_ref, rows_of(step + d * (height // 16))) for d in range(3)]
        pulled = pull_all(cots, load(state_ref, rows))
        return [right[v] - shift[...] * values[v] - pulled[v] for v in range(5)]

    def smooth_volume(step, _, keep_split):
        rows = rows_of(step)
        values = load(field, rows)
        resid = residual(step, 128, cot, values, load(source, rows), state)
        change = apply_blocks(block_rows(), resid)
        values = [values[v] + change[v] for v in range(5)]
        store(base, rows, values)
        if keep_split:
            store_split(split_n, step, 128, values, 2)
        return 0

    cot[...] = dot(volume[...], split_n[...])
    lax.fori_loop(0, 8, lambda s, c: smooth_volume(s, c, True), 0)
    face_field[...] = dot(take[0:192, :], split_n[0:256, :])

    def smooth_faces(step, _):
        values = face_pull(step, load(jump, rows_of(step)), face_state, 0, 2)
        store_split(split_f, step, 192, apply_blocks(block_rows(), values), 2)
        return 0

    receive(0, recv_fine, fine_0, own, compact)
    scatter_faces(compact, 32, 24, jump)
    lax.fori_loop(0, 12, smooth_faces, 0)
    inward[9].wait()
    face_field[...] += dot(give[0:192, :], split_f[0:384, :])
    gather_faces(face_field, 0, 32, 24, compact)
    fine_1 = copies(1, send_fine, recv_fine)
    send(1, compact, send_fine, fine_1)

    for n in range(10, 16):
        inward[n].wait()
    field[...] = base[...] + dot(give[192:320, :], split_f[0:384, :])
    own_part(compact, own)
    lax.fori_loop(0, 8, split_field, 0)
    cot[...] = dot(volume[...], split_n[...])

    def residual_volume(step, _):
        rows = rows_of(step)
        resid = residual(step, 128, cot, load(field, rows), load(source, rows), state)
        store_split(split_n, step, 128, resid, 3)
        return 0

    lax.fori_loop(0, 8, residual_volume, 0)
    field_c[...] = dot(restrict[...], split_n[...])

    def residual_faces(step, _):
        values = face_pull(step, load(jump, rows_of(step)), face_state, 0, 2)
        store_split(split_f, step, 192, values, 3)
        return 0

    receive(1, recv_fine, fine_1, own, compact)
    scatter_faces(compact, 32, 24, jump)
    lax.fori_loop(0, 12, residual_faces, 0)
    field_c[...] += dot(restrict_give[...], split_f[...])

    def coarse_first(step, _):
        rows = rows_of(step)
        store(base_c, rows, apply_blocks(block_rows(), load(field_c, rows)))
        return 0

    lax.fori_loop(0, 8, coarse_first, 0)
    gather_faces(base_c, 32, 16, 8, compact_c)
    coarse_0 = copies(0, send_coarse, recv_coarse)
    send(0, compact_c, send_coarse, coarse_0)
    own_part(compact_c, own_c)

    def split_coarse(step, _):
        store_split(split_c, step, 32, load(base_c, rows_of(step)), 2)
        return 0

    lax.fori_loop(0, 2, split_coarse, 0)
    cot_c[...] = dot(volume_c[0:96, :], split_c[0:64, :])

    def coarse_volume(step, _):
        rows = rows_of(step)
        values = load(base_c, rows)
        resid = residual(step, 32, cot_c, values, load(field_c, rows), state_c)
        change = apply_blocks(block_rows(), resid)
        values = [values[v] + change[v] for v in range(5)]
        store(field_c, rows, values)
        store_split(split_c, step, 32, values, 2)
        return 0

    lax.fori_loop(0, 2, coarse_volume, 0)
    base_c[32:128, :] = dot(volume_c[96:192, :], split_c[0:64, :])

    def coarse_faces(step, _):
        values = face_pull(step, load(jump_c, rows_of(step)), state_c, 2, 1)
        store_split(split_cf, step, 96, apply_blocks(block_rows(), values), 2)
        return 0

    receive(0, recv_coarse, coarse_0, own_c, compact_c)
    scatter_faces(compact_c, 16, 8, jump_c)
    lax.fori_loop(0, 6, coarse_faces, 0)
    base_c[32:128, :] += dot(give_c[0:96, :], split_cf[0:192, :])
    gather_faces(base_c, 32, 16, 8, compact_c)
    coarse_1 = copies(1, send_coarse, recv_coarse)
    send(1, compact_c, send_coarse, coarse_1)

    base_c[0:32, :] = field_c[0:32, :] + dot(give_c[96:128, :], split_cf[0:192, :])
    own_part(compact_c, own_c)

    def split_coarse_3(step, _):
        store_split(split_c, step, 32, load(base_c, rows_of(step)), 3)
        return 0

    lax.fori_loop(0, 2, split_coarse_3, 0)
    field[...] += dot(extend[...], split_c[...])
    lax.fori_loop(0, 8, split_field, 0)
    cot[...] = dot(volume[...], split_n[...])
    lax.fori_loop(0, 8, lambda s, c: smooth_volume(s, c, False), 0)

    def split_jump(step, _):
        store_split(split_cf, step, 96, load(jump_c, rows_of(step)), 3)
        return 0

    receive(1, recv_coarse, coarse_1, own_c, compact_c)
    scatter_faces(compact_c, 16, 8, jump_c)
    lax.fori_loop(0, 6, split_jump, 0)
    jump[...] += dot(face_extend[...], split_cf[...])
    lax.fori_loop(0, 12, smooth_faces, 0)
    base[...] += dot(give[192:320, :], split_f[0:384, :])
    for v in range(5):
        out_r[v] = base[0:125, lanes(v)]
    outward = pltpu.make_async_copy(out_r, out_h, out_sem)
    outward.start()
    for n, remote in enumerate((fine_0, fine_1, coarse_0, coarse_1)):
        for f in range(6):
            @pl.when(has[f])
            def _(remote=remote, f=f):
                remote[f].wait_send()
    outward.wait()


def body(*args):
    constants = [jnp.asarray(table) for table in tables().values()]
    vmem = pltpu.VMEM
    raw = [vmem(a.shape, a.dtype) for a in args]
    held = [vmem(t.shape, t.dtype) for t in constants]
    work = [
        vmem((128, 640), F32), vmem((128, 640), F32), vmem((128, 640), F32), vmem((128, 640), F32),
        vmem((384, 640), BF16), vmem((384, 640), F32),
        vmem((192, 640), F32), vmem((192, 640), F32), vmem((192, 640), F32), vmem((576, 640), BF16),
        vmem((6, 128, 128), F32), vmem((6, 128, 128), F32),
        vmem((128, 640), F32), vmem((128, 640), F32), vmem((128, 640), F32), vmem((96, 640), BF16),
        vmem((288, 640), BF16), vmem((96, 640), F32), vmem((96, 640), F32),
        vmem((6, 48, 128), F32), vmem((6, 48, 128), F32),
        vmem((25, 16, 128), F32), vmem((16, 128), F32), vmem(args[0].shape, F32),
    ]
    fine = [vmem((2, rows, 128), F32) for rows in (64, 64, 16, 16, 16, 16)]
    coarse = [vmem((2, rows, 128), F32) for rows in (24, 24, 8, 8, 8, 8)]
    sems = [
        pltpu.SemaphoreType.DMA((16,)),
        pltpu.SemaphoreType.DMA,
        pltpu.SemaphoreType.DMA((4, 6)),
        pltpu.SemaphoreType.DMA((4, 6)),
    ]
    anywhere = pl.BlockSpec(memory_space=pl.ANY)
    return pl.pallas_call(
        kernel,
        out_shape=jax.ShapeDtypeStruct(args[0].shape, F32),
        in_specs=[anywhere] * (len(args) + len(constants)),
        out_specs=anywhere,
        scratch_shapes=raw + held + work + fine + fine + coarse + coarse + sems,
        compiler_params=pltpu.CompilerParams(
            collective_id=0, has_side_effects=True, vmem_limit_bytes=40 * 1024 * 1024
        ),
    )(*args, *constants)


def solution(mesh):
    in_specs = (
        P(None, None, AXES),
        P(None, None, AXES),
        P(None, AXES),
        P(None, None, AXES),
        P(None, AXES),
        P(*AXES),
        P(None, None, *AXES),
    )
    return jax.shard_map(
        body, mesh=mesh, in_specs=in_specs, out_specs=P(None, None, AXES), check_vma=False
    )
```

```python
import itertools

import jax
import jax.numpy as jnp
import ml_dtypes
import numpy as np
from jax import lax
from jax.experimental import pallas as pl
from jax.experimental.pallas import tpu as pltpu
from jax.sharding import PartitionSpec as P

OMEGA = 0.7
METRIC = 0.25
FINE_FACE = 0.5 * 0.25 / 0.1
COARSE_FACE = 0.5 * 0.25 * 3.0
MESH = pl.DeviceIdType.MESH
AXES = ("gx", "gy", "gz")
COUNTS = (2, 8, 8)
STRIDES = (64, 8, 1)
F32 = jnp.float32
BF16 = jnp.bfloat16


def diff_table(nodes):
    count = len(nodes)
    weights = np.array(
        [1.0 / np.prod([nodes[j] - nodes[k] for k in range(count) if k != j]) for j in range(count)]
    )
    table = np.zeros((count, count))
    for i in range(count):
        for j in range(count):
            if i != j:
                table[i, j] = weights[j] / weights[i] / (nodes[i] - nodes[j])
        table[i, i] = -np.sum(table[i])
    return table.astype(np.float32).astype(np.float64)


def fine_points():
    return np.array([-1.0, -np.sqrt(3.0 / 7.0), 0.0, np.sqrt(3.0 / 7.0), 1.0])


def interp_table():
    points = fine_points()
    table = np.stack(
        [points * (points - 1.0) / 2.0, 1.0 - points**2, points * (points + 1.0) / 2.0], axis=1
    )
    return table.astype(np.float32).astype(np.float64)


def triple(a, b, c):
    return np.kron(np.kron(a, b), c)


def padded(matrix, rows, columns):
    result = np.zeros((rows, columns))
    result[: matrix.shape[0], : matrix.shape[1]] = matrix
    return result


def face_tables(count, rows, width):
    take = np.zeros((6 * rows, width))
    give = np.zeros((width, 6 * rows))
    for dim in range(3):
        for side in range(2):
            face = 2 * dim + side
            for row in range(rows):
                a, b = divmod(min(row, count * count - 1), count)
                place = [a, b]
                place.insert(dim, side * (count - 1))
                node = (place[0] * count + place[1]) * count + place[2]
                take[face * rows + row, node] = 1.0
                if row < count * count:
                    give[node, face * rows + row] = 1.0
    return take, give


def volume_table(count, width):
    table = diff_table(fine_points() if count == 5 else np.array([-1.0, 0.0, 1.0]))
    unit = np.eye(count)
    parts = []
    for dim in range(3):
        mats = [unit, unit, unit]
        mats[dim] = -METRIC * table.T
        parts.append(padded(triple(*mats), width, width))
    return np.concatenate(parts)


def two(matrix):
    high = matrix.astype(ml_dtypes.bfloat16)
    return np.concatenate([high, high], axis=1)


def three(matrix):
    high = matrix.astype(ml_dtypes.bfloat16)
    low = (matrix - high.astype(np.float64)).astype(ml_dtypes.bfloat16)
    return np.concatenate([high, high, low], axis=1)


def tables():
    prolong = interp_table()
    take, give = face_tables(5, 32, 128)
    take_c, give_c = face_tables(3, 16, 32)
    pick = np.zeros((32, 128))
    for n, (a, b, c) in enumerate(itertools.product(range(3), repeat=3)):
        pick[n, (2 * a * 5 + 2 * b) * 5 + 2 * c] = 1.0
    restrict = padded(triple(prolong.T, prolong.T, prolong.T), 32, 128)
    restrict = np.concatenate([restrict, take_c @ restrict])
    extend = padded(triple(prolong, prolong, prolong), 128, 32)
    flat = np.kron(prolong, prolong)
    flat = np.concatenate([flat, np.repeat(flat[24:25], 7, axis=0)])
    face_extend = np.zeros((192, 96))
    for face in range(6):
        face_extend[32 * face : 32 * face + 32, 16 * face : 16 * face + 9] = flat
    return {
        "take": two(np.concatenate([take, pick, take_c @ pick])),
        "volume": three(volume_table(5, 128)),
        "give": two(-FINE_FACE * np.concatenate([take @ give, give])),
        "restrict": three(restrict),
        "restrict_give": three(-FINE_FACE * restrict @ give),
        "volume_c": two(np.concatenate([volume_table(3, 32), take_c])),
        "give_c": two(-COARSE_FACE * np.concatenate([take_c @ give_c, give_c])),
        "extend": three(extend),
        "face_extend": three(face_extend),
    }


def dot(matrix, field):
    return jnp.dot(matrix, field, preferred_element_type=F32)


def split(value):
    high = value.astype(BF16)
    low = (value - high.astype(F32)).astype(BF16)
    return high, low


def lanes(var):
    return slice(128 * var, 128 * var + 128)


def rows_of(step, size=16):
    return pl.ds(pl.multiple_of(step * size, size), size)


def load(ref, rows):
    return [ref[rows, lanes(v)] for v in range(5)]


def store(ref, rows, values):
    for v in range(5):
        ref[rows, lanes(v)] = values[v]


def store_split(ref, step, height, values, pieces):
    for v in range(5):
        parts = split(values[v])
        for piece in range(pieces):
            ref[rows_of(step + piece * (height // 16)), lanes(v)] = parts[piece % 2]


def pull_all(cot, state):
    w = state[:3]
    enthalpy = state[3]
    crossed = [w[0] * c[1] + w[1] * c[2] + w[2] * c[3] + enthalpy * c[4] for c in cot]
    ends = [w[d] * cot[d][4] for d in range(3)]
    energy = ends[0] + ends[1] + ends[2]
    total = 0.4 * (cot[0][1] + cot[1][2] + cot[2][3] + energy)
    half_square = 0.5 * (w[0] * w[0] + w[1] * w[1] + w[2] * w[2])
    first = half_square * total - (w[0] * crossed[0] + w[1] * crossed[1] + w[2] * crossed[2])
    middle = []
    for j in range(3):
        drift = w[0] * cot[0][1 + j] + w[1] * cot[1][1 + j] + w[2] * cot[2][1 + j]
        middle.append(drift + cot[j][0] + crossed[j] - w[j] * total)
    return [first, *middle, total + energy]


def pull_face(jump, state, speed, normal, pick, sign):
    w = state[:3]
    crossed = w[0] * jump[1] + w[1] * jump[2] + w[2] * jump[3] + state[3] * jump[4]
    end = speed * jump[4]
    total = 0.4 * (normal + end)
    half_square = 0.5 * (w[0] * w[0] + w[1] * w[1] + w[2] * w[2])
    turned = jump[0] + crossed
    out = [half_square * total - speed * crossed]
    for j in range(3):
        out.append(speed * jump[1 + j] - w[j] * total + pick[j] * turned)
    out.append(total + end)
    top = jnp.abs(speed) + state[4]
    return [sign * out[v] + top * jump[v] for v in range(5)]


def apply_blocks(blocks, values):
    result = []
    for a in range(5):
        total = blocks[a] * values[0]
        for b in range(1, 5):
            total = total + blocks[b * 5 + a] * values[b]
        result.append(total)
    return result


def kernel(start_h, source_h, density_h, velocity_h, pressure_h, shift_h, inverse_h, *rest):
    tables_h, rest = rest[:9], rest[9:]
    out_h, rest = rest[0], rest[1:]
    (start_r, source_r, density_r, velocity_r, pressure_r, shift_r, inverse_r), rest = rest[:7], rest[7:]
    tables_r, rest = rest[:9], rest[9:]
    (take, volume, give, restrict, restrict_give, volume_c, give_c, extend, face_extend) = tables_r
    (
        field, source, state, base, split_n, cot,
        face_state, face_field, jump, split_f, compact, own,
        state_c, field_c, base_c, split_c, split_cf, cot_c, jump_c, compact_c, own_c,
        blocks, shift, out_r,
    ), rest = rest[:24], rest[24:]
    send_fine, recv_fine, send_coarse, recv_coarse, rest = rest[:6], rest[6:12], rest[12:18], rest[18:24], rest[24:]
    in_sems, out_sem, send_sems, recv_sems = rest

    place = [lax.axis_index(axis) for axis in AXES]
    size = [lax.axis_size(axis) for axis in AXES]
    has = [place[f // 2] > 0 if f % 2 == 0 else place[f // 2] < size[f // 2] - 1 for f in range(6)]

    def partner(f):
        target = list(place)
        target[f // 2] = target[f // 2] + (1 if f % 2 else -1)
        return tuple(target)

    barrier = pltpu.get_barrier_semaphore()
    for f in range(6):
        @pl.when(has[f])
        def _(f=f):
            pl.semaphore_signal(barrier, inc=1, device_id=partner(f), device_id_type=MESH)

    field[120:128, :] = jnp.zeros((8, 640), F32)
    source[120:128, :] = jnp.zeros((8, 640), F32)
    order = [
        (start_h, start_r), (tables_h[0], take), (velocity_h, velocity_r), (density_h, density_r),
        (pressure_h, pressure_r), (tables_h[1], volume), (source_h, source_r), (shift_h, shift_r),
        (inverse_h, inverse_r), (tables_h[2], give),
    ] + [(tables_h[n], tables_r[n]) for n in range(3, 9)]
    inward = [pltpu.make_async_copy(a, b, in_sems.at[n]) for n, (a, b) in enumerate(order)]
    for copy in inward:
        copy.start()

    def lane_place(rows, dim):
        lane = lax.broadcasted_iota(jnp.int32, (rows, 128), 1)
        return (lane // STRIDES[dim]) % COUNTS[dim]

    def gather_faces(source_ref, offset, rows, whole, target):
        sub = lax.broadcasted_iota(jnp.int32, (8, 128), 0)

        def one(f, _):
            top = offset + f * rows
            last = source_ref[pl.ds(pl.multiple_of(top + whole, 8), 8), lanes(0)]
            for v in range(5):
                target[f, whole * v : whole * v + whole, :] = source_ref[
                    pl.ds(pl.multiple_of(top, 8), whole), lanes(v)
                ]
                if v:
                    here = source_ref[pl.ds(pl.multiple_of(top + whole, 8), 8), lanes(v)]
                    last = jnp.where(sub == v, here, last)
            target[f, 5 * whole : 5 * whole + 8, :] = last
            return 0

        lax.fori_loop(0, 6, one, 0)

    def scatter_faces(source_ref, rows, whole, target):
        def one(f, _):
            top = f * rows
            for v in range(5):
                target[pl.ds(pl.multiple_of(top, 8), whole), lanes(v)] = source_ref[
                    f, whole * v : whole * v + whole, :
                ]
                target[pl.ds(pl.multiple_of(top + whole, 8), 8), lanes(v)] = jnp.broadcast_to(
                    source_ref[f, pl.ds(5 * whole + v, 1), :], (8, 128)
                )
            return 0

        lax.fori_loop(0, 6, one, 0)

    def turn(value, amount):
        amount %= 128
        return pltpu.roll(value, amount, 1) if amount else value

    def copies(exchange, sends, receives):
        row = exchange + (2 if sends is send_coarse else 0)
        return [
            pltpu.make_async_remote_copy(
                src_ref=sends[f].at[exchange],
                dst_ref=receives[f ^ 1].at[exchange],
                send_sem=send_sems.at[row, f],
                recv_sem=recv_sems.at[row, f ^ 1],
                device_id=partner(f),
                device_id_type=MESH,
            )
            for f in range(6)
        ]

    def send(exchange, faces, sends, remote):
        for f in range(6):
            dim, side = divmod(f, 2)
            count, stride = COUNTS[dim], STRIDES[dim]
            slot = sends[f].shape[1]
            where = lane_place(slot, dim)
            packed = None
            for g in range(faces.shape[1] // slot):
                block = turn(faces[f, g * slot : g * slot + slot, :], (g - side * (count - 1)) * stride)
                packed = block if packed is None else jnp.where(where == g, block, packed)
            sends[f][exchange] = packed
            if exchange == 0 and sends is send_fine and f == 0:
                pl.semaphore_wait(barrier, sum(h.astype(jnp.int32) for h in has))

            @pl.when(has[f])
            def _():
                remote[f].start()

    def own_part(faces, result):
        for f in range(6):
            dim, side = divmod(f, 2)
            count, stride = COUNTS[dim], STRIDES[dim]
            inside = lane_place(faces.shape[1], dim) != side * (count - 1)
            other = turn(faces[f ^ 1], -stride if side else stride)
            result[f] = faces[f] - jnp.where(inside, other, 0.0)

    def receive(exchange, receives, remote, result, target):
        for f in range(6):
            dim, side = divmod(f, 2)
            count, stride = COUNTS[dim], STRIDES[dim]
            slot = receives[f].shape[1]
            edge = lane_place(slot, dim) == side * (count - 1)

            @pl.when(has[f])
            def _():
                remote[f ^ 1].wait_recv()
                packed = receives[f][exchange]
                for g in range(result.shape[1] // slot):
                    here = slice(g * slot, g * slot + slot)
                    there = turn(packed, (side * (count - 1) - g) * stride)
                    target[f, here, :] = result[f, here, :] - jnp.where(edge, there, 0.0)

            @pl.when(jnp.logical_not(has[f]))
            def _():
                target[f] = result[f]

    def face_pull(step, values, state_ref, offset, per_face):
        f = lax.div(step, per_face)
        d = lax.div(f, 2)
        sign = (2 * (f - 2 * d) - 1).astype(F32)
        pick = [(d == j).astype(F32) for j in range(3)]
        rows = rows_of(step + offset)
        local = load(state_ref, rows)
        speed = state_ref[rows, pl.ds(pl.multiple_of(d * 128, 128), 128)]
        normal = pick[0] * values[1] + pick[1] * values[2] + pick[2] * values[3]
        return pull_face(values, local, speed, normal, pick, sign)

    def block_rows():
        return [blocks[n] for n in range(25)]

    inward[0].wait()
    for v in range(5):
        field[0:125, lanes(v)] = start_r[v]

    def split_field(step, _):
        store_split(split_n, step, 128, load(field, rows_of(step)), 3)
        return 0

    lax.fori_loop(0, 8, split_field, 0)
    inward[1].wait()
    face_field[...] = dot(take[0:192, :], split_n[0:256, :])
    gather_faces(face_field, 0, 32, 24, compact)
    fine_0 = copies(0, send_fine, recv_fine)
    send(0, compact, send_fine, fine_0)

    for n in (2, 3, 4):
        inward[n].wait()
    state[120:128, :] = jnp.zeros((8, 640), F32)
    for part in ((0, 64), (64, 125)):
        here = slice(*part)
        w = [velocity_r[d, here, :] for d in range(3)]
        sound_2 = 1.4 * pressure_r[here, :] / density_r[here, :]
        for d in range(3):
            state[here, lanes(d)] = w[d]
        state[here, lanes(3)] = 2.5 * sound_2 + 0.5 * (w[0] * w[0] + w[1] * w[1] + w[2] * w[2])
        state[here, lanes(4)] = jnp.sqrt(sound_2)

    def split_state(step, _):
        store_split(split_f, step, 128, load(state, rows_of(step)), 2)
        return 0

    lax.fori_loop(0, 8, split_state, 0)
    face_state[...] = dot(take[0:192, :], split_f[0:256, :])
    state_c[...] = dot(take[192:320, :], split_f[0:256, :])
    own_part(compact, own)

    for n in (7, 8):
        inward[n].wait()
    spread = (
        lax.broadcasted_iota(jnp.int32, (8, 128), 1) % 8 == lax.broadcasted_iota(jnp.int32, (8, 128), 0)
    ).astype(F32)

    def to_lanes(value, count):
        wide = jnp.dot(
            value.reshape(16 * count, 8), spread,
            precision=lax.Precision.HIGHEST, preferred_element_type=F32,
        ).reshape(count, 16, 128)
        row = lax.broadcasted_iota(jnp.int32, (count, 16, 128), 1)
        lane = lax.broadcasted_iota(jnp.int32, (count, 16, 128), 2)
        kept = jnp.where(lane // 8 == row, wide, 0.0)
        return jnp.broadcast_to(jnp.sum(kept, axis=1, keepdims=True), (count, 16, 128))

    shift[...] = to_lanes(shift_r[...], 1)[0]
    blocks[...] = OMEGA * to_lanes(inverse_r[...], 25)

    inward[5].wait()
    inward[6].wait()
    for v in range(5):
        source[0:125, lanes(v)] = source_r[v]

    def residual(step, height, cot_ref, values, right, state_ref):
        rows = rows_of(step)
        cots = [load(cot_ref, rows_of(step + d * (height // 16))) for d in range(3)]
        pulled = pull_all(cots, load(state_ref, rows))
        return [right[v] - shift[...] * values[v] - pulled[v] for v in range(5)]

    def smooth_volume(step, _, keep_split):
        rows = rows_of(step)
        values = load(field, rows)
        resid = residual(step, 128, cot, values, load(source, rows), state)
        change = apply_blocks(block_rows(), resid)
        values = [values[v] + change[v] for v in range(5)]
        store(base, rows, values)
        if keep_split:
            store_split(split_n, step, 128, values, 2)
        return 0

    cot[...] = dot(volume[...], split_n[...])
    lax.fori_loop(0, 8, lambda s, c: smooth_volume(s, c, True), 0)
    face_field[...] = dot(take[0:192, :], split_n[0:256, :])

    def smooth_faces(step, _):
        values = face_pull(step, load(jump, rows_of(step)), face_state, 0, 2)
        store_split(split_f, step, 192, apply_blocks(block_rows(), values), 2)
        return 0

    receive(0, recv_fine, fine_0, own, compact)
    scatter_faces(compact, 32, 24, jump)
    lax.fori_loop(0, 12, smooth_faces, 0)
    inward[9].wait()
    face_field[...] += dot(give[0:192, :], split_f[0:384, :])
    gather_faces(face_field, 0, 32, 24, compact)
    fine_1 = copies(1, send_fine, recv_fine)
    send(1, compact, send_fine, fine_1)

    for n in range(10, 16):
        inward[n].wait()
    field[...] = base[...] + dot(give[192:320, :], split_f[0:384, :])
    own_part(compact, own)
    lax.fori_loop(0, 8, split_field, 0)
    cot[...] = dot(volume[...], split_n[...])

    def residual_volume(step, _):
        rows = rows_of(step)
        resid = residual(step, 128, cot, load(field, rows), load(source, rows), state)
        store_split(split_n, step, 128, resid, 3)
        return 0

    lax.fori_loop(0, 8, residual_volume, 0)
    field_c[...] = dot(restrict[...], split_n[...])

    def residual_faces(step, _):
        values = face_pull(step, load(jump, rows_of(step)), face_state, 0, 2)
        store_split(split_f, step, 192, values, 3)
        return 0

    receive(1, recv_fine, fine_1, own, compact)
    scatter_faces(compact, 32, 24, jump)
    lax.fori_loop(0, 12, residual_faces, 0)
    field_c[...] += dot(restrict_give[...], split_f[...])

    def coarse_first(step, _):
        rows = rows_of(step)
        store(base_c, rows, apply_blocks(block_rows(), load(field_c, rows)))
        return 0

    lax.fori_loop(0, 8, coarse_first, 0)
    gather_faces(base_c, 32, 16, 8, compact_c)
    coarse_0 = copies(0, send_coarse, recv_coarse)
    send(0, compact_c, send_coarse, coarse_0)
    own_part(compact_c, own_c)

    def split_coarse(step, _):
        store_split(split_c, step, 32, load(base_c, rows_of(step)), 2)
        return 0

    lax.fori_loop(0, 2, split_coarse, 0)
    cot_c[...] = dot(volume_c[0:96, :], split_c[0:64, :])

    def coarse_volume(step, _):
        rows = rows_of(step)
        values = load(base_c, rows)
        resid = residual(step, 32, cot_c, values, load(field_c, rows), state_c)
        change = apply_blocks(block_rows(), resid)
        values = [values[v] + change[v] for v in range(5)]
        store(field_c, rows, values)
        store_split(split_c, step, 32, values, 2)
        return 0

    lax.fori_loop(0, 2, coarse_volume, 0)
    base_c[32:128, :] = dot(volume_c[96:192, :], split_c[0:64, :])

    def coarse_faces(step, _):
        values = face_pull(step, load(jump_c, rows_of(step)), state_c, 2, 1)
        store_split(split_cf, step, 96, apply_blocks(block_rows(), values), 2)
        return 0

    receive(0, recv_coarse, coarse_0, own_c, compact_c)
    scatter_faces(compact_c, 16, 8, jump_c)
    lax.fori_loop(0, 6, coarse_faces, 0)
    base_c[32:128, :] += dot(give_c[0:96, :], split_cf[0:192, :])
    gather_faces(base_c, 32, 16, 8, compact_c)
    coarse_1 = copies(1, send_coarse, recv_coarse)
    send(1, compact_c, send_coarse, coarse_1)

    base_c[0:32, :] = field_c[0:32, :] + dot(give_c[96:128, :], split_cf[0:192, :])
    own_part(compact_c, own_c)

    def split_coarse_3(step, _):
        store_split(split_c, step, 32, load(base_c, rows_of(step)), 3)
        return 0

    lax.fori_loop(0, 2, split_coarse_3, 0)
    field[...] += dot(extend[...], split_c[...])
    lax.fori_loop(0, 8, split_field, 0)
    cot[...] = dot(volume[...], split_n[...])
    lax.fori_loop(0, 8, lambda s, c: smooth_volume(s, c, False), 0)

    def split_jump(step, _):
        store_split(split_cf, step, 96, load(jump_c, rows_of(step)), 3)
        return 0

    receive(1, recv_coarse, coarse_1, own_c, compact_c)
    scatter_faces(compact_c, 16, 8, jump_c)
    lax.fori_loop(0, 6, split_jump, 0)
    jump[...] += dot(face_extend[...], split_cf[...])
    lax.fori_loop(0, 12, smooth_faces, 0)
    base[...] += dot(give[192:320, :], split_f[0:384, :])
    for v in range(5):
        out_r[v] = base[0:125, lanes(v)]
    outward = pltpu.make_async_copy(out_r, out_h, out_sem)
    outward.start()
    for n, remote in enumerate((fine_0, fine_1, coarse_0, coarse_1)):
        for f in range(6):
            @pl.when(has[f])
            def _(remote=remote, f=f):
                remote[f].wait_send()
    outward.wait()


def body(*args):
    constants = [jnp.asarray(table) for table in tables().values()]
    vmem = pltpu.VMEM
    raw = [vmem(a.shape, a.dtype) for a in args]
    held = [vmem(t.shape, t.dtype) for t in constants]
    work = [
        vmem((128, 640), F32), vmem((128, 640), F32), vmem((128, 640), F32), vmem((128, 640), F32),
        vmem((384, 640), BF16), vmem((384, 640), F32),
        vmem((192, 640), F32), vmem((192, 640), F32), vmem((192, 640), F32), vmem((576, 640), BF16),
        vmem((6, 128, 128), F32), vmem((6, 128, 128), F32),
        vmem((128, 640), F32), vmem((128, 640), F32), vmem((128, 640), F32), vmem((96, 640), BF16),
        vmem((288, 640), BF16), vmem((96, 640), F32), vmem((96, 640), F32),
        vmem((6, 48, 128), F32), vmem((6, 48, 128), F32),
        vmem((25, 16, 128), F32), vmem((16, 128), F32), vmem(args[0].shape, F32),
    ]
    fine = [vmem((2, rows, 128), F32) for rows in (64, 64, 16, 16, 16, 16)]
    coarse = [vmem((2, rows, 128), F32) for rows in (24, 24, 8, 8, 8, 8)]
    sems = [
        pltpu.SemaphoreType.DMA((16,)),
        pltpu.SemaphoreType.DMA,
        pltpu.SemaphoreType.DMA((4, 6)),
        pltpu.SemaphoreType.DMA((4, 6)),
    ]
    anywhere = pl.BlockSpec(memory_space=pl.ANY)
    return pl.pallas_call(
        kernel,
        out_shape=jax.ShapeDtypeStruct(args[0].shape, F32),
        in_specs=[anywhere] * (len(args) + len(constants)),
        out_specs=anywhere,
        scratch_shapes=raw + held + work + fine + fine + coarse + coarse + sems,
        compiler_params=pltpu.CompilerParams(
            collective_id=0, has_side_effects=True, vmem_limit_bytes=60 * 1024 * 1024
        ),
    )(*args, *constants)


def solution(mesh):
    in_specs = (
        P(None, None, AXES),
        P(None, None, AXES),
        P(None, AXES),
        P(None, None, AXES),
        P(None, AXES),
        P(*AXES),
        P(None, None, *AXES),
    )
    return jax.shard_map(
        body, mesh=mesh, in_specs=in_specs, out_specs=P(None, None, AXES), check_vma=False
    )
```

```python
import itertools

import jax
import jax.numpy as jnp
import ml_dtypes
import numpy as np
from jax import lax
from jax.experimental import pallas as pl
from jax.experimental.pallas import tpu as pltpu
from jax.sharding import PartitionSpec as P

OMEGA = 0.7
METRIC = 0.25
FINE_FACE = 0.5 * 0.25 / 0.1
COARSE_FACE = 0.5 * 0.25 * 3.0
MESH = pl.DeviceIdType.MESH
AXES = ("gx", "gy", "gz")
COUNTS = (2, 8, 8)
STRIDES = (64, 8, 1)
LINES = [(i, j, s, t) for i, j in ((0, 1), (0, 2), (1, 2)) for s in range(2) for t in range(2)]
F32 = jnp.float32
BF16 = jnp.bfloat16


def diff_table(nodes):
    count = len(nodes)
    weights = np.array(
        [1.0 / np.prod([nodes[j] - nodes[k] for k in range(count) if k != j]) for j in range(count)]
    )
    table = np.zeros((count, count))
    for i in range(count):
        for j in range(count):
            if i != j:
                table[i, j] = weights[j] / weights[i] / (nodes[i] - nodes[j])
        table[i, i] = -np.sum(table[i])
    return table.astype(np.float32).astype(np.float64)


def fine_points():
    return np.array([-1.0, -np.sqrt(3.0 / 7.0), 0.0, np.sqrt(3.0 / 7.0), 1.0])


def interp_table():
    points = fine_points()
    table = np.stack(
        [points * (points - 1.0) / 2.0, 1.0 - points**2, points * (points + 1.0) / 2.0], axis=1
    )
    return table.astype(np.float32).astype(np.float64)


def triple(a, b, c):
    return np.kron(np.kron(a, b), c)


def padded(matrix, rows, columns):
    result = np.zeros((rows, columns))
    result[: matrix.shape[0], : matrix.shape[1]] = matrix
    return result


def face_tables(count, rows, width):
    take = np.zeros((6 * rows, width))
    give = np.zeros((width, 6 * rows))
    for dim in range(3):
        for side in range(2):
            face = 2 * dim + side
            for row in range(rows):
                a, b = divmod(min(row, count * count - 1), count)
                place = [a, b]
                place.insert(dim, side * (count - 1))
                node = (place[0] * count + place[1]) * count + place[2]
                take[face * rows + row, node] = 1.0
                if row < count * count:
                    give[node, face * rows + row] = 1.0
    return take, give


def line_table(count, width):
    take = np.zeros((96, width))
    for line, (i, j, s, t) in enumerate(LINES):
        for node in range(count):
            place = [node] * 3
            place[i], place[j] = s * (count - 1), t * (count - 1)
            take[8 * line + node, (place[0] * count + place[1]) * count + place[2]] = 1.0
    return take


def line_faces(count, rows):
    result = np.zeros((2, 6 * rows, 96))
    for dim in range(3):
        for side in range(2):
            for row in range(rows):
                pair = divmod(min(row, count * count - 1), count)
                others = [d for d in range(3) if d != dim]
                for n in range(2):
                    if pair[n] % (count - 1) == 0:
                        sides = {dim: side, others[n]: pair[n] // (count - 1)}
                        i, j = sorted(sides)
                        line = LINES.index((i, j, sides[i], sides[j]))
                        result[n, (2 * dim + side) * rows + row, 8 * line + pair[1 - n]] = -1.0
    return result.reshape(12 * rows, 96)


def volume_table(count, width):
    table = diff_table(fine_points() if count == 5 else np.array([-1.0, 0.0, 1.0]))
    unit = np.eye(count)
    parts = []
    for dim in range(3):
        mats = [unit, unit, unit]
        mats[dim] = -METRIC * table.T
        parts.append(padded(triple(*mats), width, width))
    return np.concatenate(parts)


def two(matrix):
    high = matrix.astype(ml_dtypes.bfloat16)
    return np.concatenate([high, high], axis=1)


def three(matrix):
    high = matrix.astype(ml_dtypes.bfloat16)
    low = (matrix - high.astype(np.float64)).astype(ml_dtypes.bfloat16)
    return np.concatenate([high, high, low], axis=1)


def tables():
    prolong = interp_table()
    take, give = face_tables(5, 32, 128)
    take_c, give_c = face_tables(3, 16, 32)
    pick = np.zeros((32, 128))
    for n, (a, b, c) in enumerate(itertools.product(range(3), repeat=3)):
        pick[n, (2 * a * 5 + 2 * b) * 5 + 2 * c] = 1.0
    restrict = padded(triple(prolong.T, prolong.T, prolong.T), 32, 128)
    restrict = np.concatenate([restrict, take_c @ restrict, line_table(3, 32) @ restrict])
    extend = padded(triple(prolong, prolong, prolong), 128, 32)
    flat = np.kron(prolong, prolong)
    flat = np.concatenate([flat, np.repeat(flat[24:25], 7, axis=0)])
    face_extend = np.zeros((192, 96))
    for face in range(6):
        face_extend[32 * face : 32 * face + 32, 16 * face : 16 * face + 9] = flat
    face_pick = np.zeros((96, 192))
    for face in range(6):
        for row in range(16):
            a, b = divmod(min(row, 8), 3)
            face_pick[16 * face + row, 32 * face + 10 * a + 2 * b] = 1.0
    return {
        "take": two(np.concatenate([take, line_table(5, 128), pick])),
        "volume": three(volume_table(5, 128)),
        "give": two(-FINE_FACE * np.concatenate([take @ give, give])),
        "restrict": three(restrict),
        "restrict_give": three(-FINE_FACE * restrict @ give),
        "volume_c": two(np.concatenate([volume_table(3, 32), take_c])),
        "give_c": two(-COARSE_FACE * np.concatenate([take_c @ give_c, give_c])),
        "extend": three(extend),
        "face_extend": three(face_extend),
        "lines": two(line_faces(5, 32)),
        "lines_c": two(line_faces(3, 16)),
        "pick_face": two(face_pick),
    }


def dot(matrix, field):
    return jnp.dot(matrix, field, preferred_element_type=F32)


def split(value):
    high = value.astype(BF16)
    low = (value - high.astype(F32)).astype(BF16)
    return high, low


def lanes(var):
    return slice(128 * var, 128 * var + 128)


def rows_of(step, size=16):
    return pl.ds(pl.multiple_of(step * size, size), size)


def load(ref, rows):
    return [ref[rows, lanes(v)] for v in range(5)]


def store(ref, rows, values):
    for v in range(5):
        ref[rows, lanes(v)] = values[v]


def store_split(ref, step, height, values, pieces):
    for v in range(5):
        parts = split(values[v])
        for piece in range(pieces):
            ref[rows_of(step + piece * (height // 16)), lanes(v)] = parts[piece % 2]


def pull_all(cot, state):
    w = state[:3]
    enthalpy = state[3]
    crossed = [w[0] * c[1] + w[1] * c[2] + w[2] * c[3] + enthalpy * c[4] for c in cot]
    ends = [w[d] * cot[d][4] for d in range(3)]
    energy = ends[0] + ends[1] + ends[2]
    total = 0.4 * (cot[0][1] + cot[1][2] + cot[2][3] + energy)
    half_square = 0.5 * (w[0] * w[0] + w[1] * w[1] + w[2] * w[2])
    first = half_square * total - (w[0] * crossed[0] + w[1] * crossed[1] + w[2] * crossed[2])
    middle = []
    for j in range(3):
        drift = w[0] * cot[0][1 + j] + w[1] * cot[1][1 + j] + w[2] * cot[2][1 + j]
        middle.append(drift + cot[j][0] + crossed[j] - w[j] * total)
    return [first, *middle, total + energy]


def pull_face(jump, state, speed, normal, pick, sign):
    w = state[:3]
    crossed = w[0] * jump[1] + w[1] * jump[2] + w[2] * jump[3] + state[3] * jump[4]
    end = speed * jump[4]
    total = 0.4 * (normal + end)
    half_square = 0.5 * (w[0] * w[0] + w[1] * w[1] + w[2] * w[2])
    turned = jump[0] + crossed
    out = [half_square * total - speed * crossed]
    for j in range(3):
        out.append(speed * jump[1 + j] - w[j] * total + pick[j] * turned)
    out.append(total + end)
    top = jnp.abs(speed) + state[4]
    return [sign * out[v] + top * jump[v] for v in range(5)]


def apply_blocks(blocks, values):
    result = []
    for a in range(5):
        total = blocks[a] * values[0]
        for b in range(1, 5):
            total = total + blocks[b * 5 + a] * values[b]
        result.append(total)
    return result


def kernel(start_h, source_h, density_h, velocity_h, pressure_h, shift_h, inverse_h, *rest):
    tables_h, rest = rest[:12], rest[12:]
    out_h, rest = rest[0], rest[1:]
    (start_r, source_r, density_r, velocity_r, pressure_r, shift_r, inverse_r), rest = rest[:7], rest[7:]
    tables_r, rest = rest[:12], rest[12:]
    (
        take, volume, give, restrict, restrict_give, volume_c, give_c, extend, face_extend,
        lines, lines_c, pick_face,
    ) = tables_r
    (
        field, source, state, base, split_n, cot,
        face_state, start_face, face_field, jump, split_f, compact, own,
        near_state, near, across, line_field, split_l, near_blocks, block_row, edges, signs, signs_c,
        state_c, field_c, base_c, split_c, split_cf, cot_c, jump_c, compact_c, own_c,
        near_state_c, near_c, across_c, face_c,
        blocks, shift, out_r,
    ), rest = rest[:39], rest[39:]
    kinds = []
    for _ in range(5):
        kinds.append((rest[:6], rest[6:12]))
        rest = rest[12:]
    fine_u, fine_t, fine_w, coarse_u, coarse_w = kinds
    send_lines, recv_lines, in_sems, out_sem, send_sems, recv_sems, send_line_sems, recv_line_sems = rest

    place = [lax.axis_index(axis) for axis in AXES]
    size = [lax.axis_size(axis) for axis in AXES]
    has = [place[f // 2] > 0 if f % 2 == 0 else place[f // 2] < size[f // 2] - 1 for f in range(6)]

    def partner(f):
        target = list(place)
        target[f // 2] = target[f // 2] + (1 if f % 2 else -1)
        return tuple(target)

    both = [has[2 * i + s] & has[2 * j + t] for i, j, s, t in LINES]

    def line_partner(line):
        i, j, s, t = LINES[line]
        target = list(place)
        target[i] = target[i] + 2 * s - 1
        target[j] = target[j] + 2 * t - 1
        return tuple(target)

    barrier = pltpu.get_barrier_semaphore()
    for f in range(6):
        @pl.when(has[f])
        def _(f=f):
            pl.semaphore_signal(barrier, inc=1, device_id=partner(f), device_id_type=MESH)
    for line in range(12):
        @pl.when(both[line])
        def _(line=line):
            pl.semaphore_signal(barrier, inc=1, device_id=line_partner(line), device_id_type=MESH)

    field[120:128, :] = jnp.zeros((8, 640), F32)
    source[120:128, :] = jnp.zeros((8, 640), F32)
    order = [
        (start_h, start_r), (tables_h[0], take), (velocity_h, velocity_r), (density_h, density_r),
        (pressure_h, pressure_r), (tables_h[1], volume), (source_h, source_r), (shift_h, shift_r),
        (inverse_h, inverse_r), (tables_h[2], give),
    ] + [(tables_h[n], tables_r[n]) for n in range(3, 12)]
    inward = [pltpu.make_async_copy(a, b, in_sems.at[n]) for n, (a, b) in enumerate(order)]
    for copy in inward:
        copy.start()

    def lane_place(rows, dim):
        lane = lax.broadcasted_iota(jnp.int32, (rows, 128), 1)
        return (lane // STRIDES[dim]) % COUNTS[dim]

    def gather_faces(source_ref, offset, rows, whole, target):
        sub = lax.broadcasted_iota(jnp.int32, (8, 128), 0)

        def one(f, _):
            top = offset + f * rows
            last = source_ref[pl.ds(pl.multiple_of(top + whole, 8), 8), lanes(0)]
            for v in range(5):
                target[f, whole * v : whole * v + whole, :] = source_ref[
                    pl.ds(pl.multiple_of(top, 8), whole), lanes(v)
                ]
                if v:
                    here = source_ref[pl.ds(pl.multiple_of(top + whole, 8), 8), lanes(v)]
                    last = jnp.where(sub == v, here, last)
            target[f, 5 * whole : 5 * whole + 8, :] = last
            return 0

        lax.fori_loop(0, 6, one, 0)

    def scatter_faces(source_ref, rows, whole, target):
        def one(f, _):
            top = f * rows
            for v in range(5):
                target[pl.ds(pl.multiple_of(top, 8), whole), lanes(v)] = source_ref[
                    f, whole * v : whole * v + whole, :
                ]
                target[pl.ds(pl.multiple_of(top + whole, 8), 8), lanes(v)] = jnp.broadcast_to(
                    source_ref[f, pl.ds(5 * whole + v, 1), :], (8, 128)
                )
            return 0

        lax.fori_loop(0, 6, one, 0)

    def turn(value, amount):
        amount %= 128
        return pltpu.roll(value, amount, 1) if amount else value

    def copies(kind):
        sends, receives = kinds[kind]
        return [
            pltpu.make_async_remote_copy(
                src_ref=sends[f],
                dst_ref=receives[f ^ 1],
                send_sem=send_sems.at[kind, f],
                recv_sem=recv_sems.at[kind, f ^ 1],
                device_id=partner(f),
                device_id_type=MESH,
            )
            for f in range(6)
        ]

    def line_copies(level):
        return [
            pltpu.make_async_remote_copy(
                src_ref=send_lines.at[level, line],
                dst_ref=recv_lines.at[level, line ^ 3],
                send_sem=send_line_sems.at[level, line],
                recv_sem=recv_line_sems.at[level, line ^ 3],
                device_id=line_partner(line),
                device_id_type=MESH,
            )
            for line in range(12)
        ]

    remote = [copies(kind) for kind in range(5)]
    remote_lines = [line_copies(level) for level in range(2)]

    def pack(kind, read, height, top=0, slots=None):
        for f in range(6):
            dim, side = divmod(f, 2)
            count, stride = COUNTS[dim], STRIDES[dim]
            target = kinds[kind][0][f]
            slot = target.shape[0] if slots is None else slots[dim]
            where = lane_place(slot, dim)
            packed = None
            for g in range(height // slot):
                block = turn(read(f, g * slot, slot), (g - side * (count - 1)) * stride)
                packed = block if packed is None else jnp.where(where == g, block, packed)
            first = top if slots is None else top[dim]
            target[first : first + slot, :] = packed

    def pack_lines(level, source_ref, offset):
        for line, (i, j, s, t) in enumerate(LINES):
            where = lane_place(8, j)
            packed = None
            for v in range(5):
                block = source_ref[offset + 8 * line : offset + 8 * line + 8, lanes(v)]
                block = turn(block, (v - t * (COUNTS[j] - 1)) * STRIDES[j])
                packed = block if packed is None else jnp.where(where == v, block, packed)
            send_lines[level, line] = packed

    def start(kind):
        for f in range(6):
            @pl.when(has[f])
            def _(f=f):
                remote[kind][f].start()

    def start_lines(level):
        for line in range(12):
            @pl.when(both[line])
            def _(line=line):
                remote_lines[level][line].start()

    def unpack(kind, f, height, write, sign=1.0, top=0, slots=None):
        dim, side = divmod(f, 2)
        count, stride = COUNTS[dim], STRIDES[dim]
        received = kinds[kind][1][f]
        slot = received.shape[0] if slots is None else slots[dim]
        first = top if slots is None else top[dim]
        edge = jnp.where(lane_place(slot, dim) == side * (count - 1), sign, 0.0)

        @pl.when(has[f])
        def _():
            packed = received[first : first + slot, :]
            for g in range(height // slot):
                write(f, g * slot, slot, edge * turn(packed, (side * (count - 1) - g) * stride))

        @pl.when(jnp.logical_not(has[f]))
        def _():
            write(f, 0, height, jnp.zeros((height, 128), F32))

    def arrive(kind, f):
        @pl.when(has[f])
        def _():
            remote[kind][f ^ 1].wait_recv()

    def receive(kind, target, sign):
        def write(f, first, slot, value):
            target[f, first : first + slot, :] = value

        for f in range(6):
            arrive(kind, f)
            unpack(kind, f, target.shape[1], write, sign)

    def receive_lines(level, target):
        for line, (i, j, s, t) in enumerate(LINES):
            edge = (lane_place(8, i) == s * (COUNTS[i] - 1)) & (lane_place(8, j) == t * (COUNTS[j] - 1))
            here = slice(8 * line, 8 * line + 8)

            @pl.when(both[line])
            def _():
                remote_lines[level][line ^ 3].wait_recv()
                packed = recv_lines[level, line]
                for v in range(5):
                    amount = (t * (COUNTS[j] - 1) - v) * STRIDES[j] + (2 * s - 1) * (COUNTS[i] - 1) * STRIDES[i]
                    target[here, lanes(v)] = jnp.where(edge, turn(packed, amount), 0.0)

            @pl.when(jnp.logical_not(both[line]))
            def _():
                target[here, :] = jnp.zeros((8, 640), F32)

    def own_part(faces, result):
        for f in range(6):
            dim, side = divmod(f, 2)
            count, stride = COUNTS[dim], STRIDES[dim]
            inside = lane_place(faces.shape[1], dim) != side * (count - 1)
            other = turn(faces[f ^ 1], -stride if side else stride)
            result[f] = faces[f] - jnp.where(inside, other, 0.0)

    def face_pull(step, values, state_ref, offset, per_face):
        f = lax.div(step, per_face)
        d = lax.div(f, 2)
        sign = (2 * (f - 2 * d) - 1).astype(F32)
        pick = [(d == j).astype(F32) for j in range(3)]
        rows = rows_of(step + offset)
        local = load(state_ref, rows)
        speed = state_ref[rows, pl.ds(pl.multiple_of(d * 128, 128), 128)]
        normal = pick[0] * values[1] + pick[1] * values[2] + pick[2] * values[3]
        return pull_face(values, local, speed, normal, pick, sign)

    def neighbour(rows, face, mine, offset, near_s, across_ref, sign_ref, near_ref, target):
        per_face = rows // 16
        for d in range(3):
            p, q = [n for n in range(3) if n != d]

            def one(step, _, d=d, p=p, q=q):
                side = lax.div(step, per_face)
                f = 2 * d + side
                at = step + 2 * d * per_face
                here = rows_of(at)
                local = load(near_s, here)
                top = [jnp.abs(local[n]) + local[4] for n in range(3)]
                edge = edges[f]
                own_side = load(mine, rows_of(at + offset))
                jumps = [None] * 3
                jumps[d] = [-edge * value for value in own_side]
                jumps[p] = load(across_ref, here)
                jumps[q] = load(across_ref, rows_of(at + 6 * per_face))
                part = rows_of(step - side * per_face)
                sign = [None] * 3
                sign[d] = (1 - 2 * side).astype(F32)
                sign[p], sign[q] = sign_ref[0, part, :], sign_ref[1, part, :]
                pulled = pull_all([[sign[n] * value for value in jumps[n]] for n in range(3)], local)
                for n in range(3):
                    pulled = [pulled[v] + top[n] * jumps[n][v] for v in range(5)]
                inverse = [near_blocks[f, pl.ds(n, 1), :] for n in range(25)]
                change = apply_blocks(inverse, pulled)
                old = load(near_ref, here)
                jumps_now = load(target, here)
                store(target, here, [jumps_now[v] - (old[v] - face * change[v]) for v in range(5)])
                return 0

            lax.fori_loop(0, 2 * per_face, one, 0)

    def block_rows():
        return [blocks[n] for n in range(25)]

    for f in range(6):
        dim, side = divmod(f, 2)
        edges[f] = (lane_place(16, dim) == side * (COUNTS[dim] - 1)).astype(F32)
    for ref, rows, count in ((signs, 32, 5), (signs_c, 16, 3)):
        row = jnp.minimum(lax.broadcasted_iota(jnp.int32, (rows, 128), 0), count * count - 1)
        for n, at in enumerate((row // count, row % count)):
            ref[n] = jnp.where(at == 0, -1.0, jnp.where(at == count - 1, 1.0, 0.0))
    block_row[...] = jnp.zeros((32, 128), F32)
    inward[0].wait()
    for v in range(5):
        field[0:125, lanes(v)] = start_r[v]

    def split_field(step, _):
        store_split(split_n, step, 128, load(field, rows_of(step)), 3)
        return 0

    lax.fori_loop(0, 8, split_field, 0)
    inward[1].wait()
    start_face[...] = dot(take[0:192, :], split_n[0:256, :])
    line_field[...] = dot(take[192:288, :], split_n[0:256, :])
    gather_faces(start_face, 0, 32, 24, compact)
    pack(0, lambda f, first, slot: compact[f, first : first + slot, :], 128)
    pack_lines(0, line_field, 0)
    own_part(compact, own)
    scatter_faces(own, 32, 24, jump)

    for n in (2, 3, 4):
        inward[n].wait()
    state[120:128, :] = jnp.zeros((8, 640), F32)
    for part in ((0, 64), (64, 125)):
        here = slice(*part)
        w = [velocity_r[d, here, :] for d in range(3)]
        sound_2 = 1.4 * pressure_r[here, :] / density_r[here, :]
        for d in range(3):
            state[here, lanes(d)] = w[d]
        state[here, lanes(3)] = 2.5 * sound_2 + 0.5 * (w[0] * w[0] + w[1] * w[1] + w[2] * w[2])
        state[here, lanes(4)] = jnp.sqrt(sound_2)

    def split_state(step, _):
        store_split(split_f, step, 128, load(state, rows_of(step)), 2)
        return 0

    lax.fori_loop(0, 8, split_state, 0)
    face_state[...] = dot(take[0:192, :], split_f[0:256, :])
    state_c[0:32, :] = dot(take[288:320, :], split_f[0:256, :])

    for n in (7, 8):
        inward[n].wait()
    spread = (
        lax.broadcasted_iota(jnp.int32, (8, 128), 1) % 8 == lax.broadcasted_iota(jnp.int32, (8, 128), 0)
    ).astype(F32)

    def to_lanes(value, count):
        wide = jnp.dot(
            value.reshape(16 * count, 8), spread,
            precision=lax.Precision.HIGHEST, preferred_element_type=F32,
        ).reshape(count, 16, 128)
        row = lax.broadcasted_iota(jnp.int32, (count, 16, 128), 1)
        lane = lax.broadcasted_iota(jnp.int32, (count, 16, 128), 2)
        kept = jnp.where(lane // 8 == row, wide, 0.0)
        return jnp.broadcast_to(jnp.sum(kept, axis=1, keepdims=True), (count, 16, 128))

    shift[...] = to_lanes(shift_r[...], 1)[0]
    blocks[...] = OMEGA * to_lanes(inverse_r[...], 25)

    for n in range(25):
        block_row[n : n + 1, :] = blocks[n, 0:1, :]
    gather_faces(face_state, 0, 32, 24, compact)
    slots, tops = (64, 16, 16), (0, 0, 0)
    pack(1, lambda f, first, slot: compact[f, first : first + slot, :], 128, tops, slots)
    block_slots, block_tops = (16, 8, 8), (64, 16, 16)
    pack(1, lambda f, first, slot: block_row[first : first + slot, :], 32, block_tops, block_slots)

    inward[5].wait()
    inward[6].wait()
    for v in range(5):
        source[0:125, lanes(v)] = source_r[v]

    def residual(step, height, cot_ref, values, right, state_ref):
        rows = rows_of(step)
        cots = [load(cot_ref, rows_of(step + d * (height // 16))) for d in range(3)]
        pulled = pull_all(cots, load(state_ref, rows))
        return [right[v] - shift[...] * values[v] - pulled[v] for v in range(5)]

    def smooth_volume(step, _, keep_split):
        rows = rows_of(step)
        values = load(field, rows)
        resid = residual(step, 128, cot, values, load(source, rows), state)
        change = apply_blocks(block_rows(), resid)
        values = [values[v] + change[v] for v in range(5)]
        store(base, rows, values)
        if keep_split:
            store_split(split_n, step, 128, values, 2)
        return 0

    cot[...] = dot(volume[...], split_n[...])
    lax.fori_loop(0, 8, lambda s, c: smooth_volume(s, c, True), 0)
    pl.semaphore_wait(barrier, sum(h.astype(jnp.int32) for h in has + both))
    start(0)
    start(1)
    start_lines(0)
    face_field[...] = dot(take[0:192, :], split_n[0:256, :])

    def smooth_faces(step, _):
        values = face_pull(step, load(jump, rows_of(step)), face_state, 0, 2)
        store_split(split_f, step, 192, apply_blocks(block_rows(), values), 2)
        return 0

    lax.fori_loop(0, 12, smooth_faces, 0)
    inward[9].wait()
    face_field[...] += dot(give[0:192, :], split_f[0:384, :])
    gather_faces(face_field, 0, 32, 24, compact)
    pack(2, lambda f, first, slot: compact[f, first : first + slot, :], 128)
    start(2)
    base[...] += dot(give[192:320, :], split_f[0:384, :])
    for n in range(10, 19):
        inward[n].wait()

    def split_faces(step, ref):
        store_split(split_f, step, 192, load(ref, rows_of(step)), 2)

    def split_face_state(step, _):
        split_faces(step, face_state)
        return 0

    lax.fori_loop(0, 12, split_face_state, 0)
    state_c[32:128, :] = dot(pick_face[...], split_f[0:384, :])

    receive(0, compact, -1.0)
    scatter_faces(compact, 32, 24, jump)
    lax.fori_loop(0, 12, smooth_faces, 0)
    face_field[...] += dot(give[0:192, :], split_f[0:384, :])
    field[...] = base[...] + dot(give[192:320, :], split_f[0:384, :])
    gather_faces(face_field, 0, 32, 24, compact)
    own_part(compact, own)
    scatter_faces(own, 32, 24, jump)
    lax.fori_loop(0, 8, split_field, 0)
    cot[...] = dot(volume[...], split_n[...])

    def residual_volume(step, _):
        rows = rows_of(step)
        resid = residual(step, 128, cot, load(field, rows), load(source, rows), state)
        store_split(split_n, step, 128, resid, 3)
        return 0

    lax.fori_loop(0, 8, residual_volume, 0)
    field_c[...] = dot(restrict[...], split_n[...])

    def write_state(f, first, slot, value):
        compact[f, first : first + slot, :] = value

    def write_blocks(f, first, slot, value):
        near_blocks[f, first : first + slot, :] = value

    for f in range(6):
        arrive(1, f)
        unpack(1, f, 128, write_state, 1.0, tops, slots)
        unpack(1, f, 32, write_blocks, 1.0, block_tops, block_slots)
    scatter_faces(compact, 32, 24, near_state)
    receive_lines(0, line_field)

    def split_lines(step, _):
        store_split(split_l, step, 96, load(line_field, rows_of(step)), 2)
        return 0

    lax.fori_loop(0, 6, split_lines, 0)
    across[...] = dot(lines[...], split_l[...])
    receive(2, compact, 1.0)
    scatter_faces(compact, 32, 24, near)
    neighbour(32, FINE_FACE, start_face, 0, near_state, across, signs, near, jump)

    def residual_faces(step, _):
        values = face_pull(step, load(jump, rows_of(step)), face_state, 0, 2)
        store_split(split_f, step, 192, values, 3)
        return 0

    lax.fori_loop(0, 12, residual_faces, 0)
    field_c[...] += dot(restrict_give[...], split_f[...])

    def coarse_first(step, _):
        rows = rows_of(step)
        store(base_c, rows, apply_blocks(block_rows(), load(field_c, rows)))
        return 0

    lax.fori_loop(0, 14, coarse_first, 0)
    gather_faces(base_c, 32, 16, 8, compact_c)
    pack(3, lambda f, first, slot: compact_c[f, first : first + slot, :], 48)
    start(3)
    pack_lines(1, base_c, 128)
    start_lines(1)
    own_part(compact_c, own_c)
    scatter_faces(own_c, 16, 8, jump_c)

    def split_coarse(step, _):
        store_split(split_c, step, 32, load(base_c, rows_of(step)), 2)
        return 0

    lax.fori_loop(0, 2, split_coarse, 0)
    cot_c[...] = dot(volume_c[0:96, :], split_c[0:64, :])

    def coarse_volume(step, _):
        rows = rows_of(step)
        values = load(base_c, rows)
        resid = residual(step, 32, cot_c, values, load(field_c, rows), state_c)
        change = apply_blocks(block_rows(), resid)
        values = [values[v] + change[v] for v in range(5)]
        store(field_c, rows, values)
        store_split(split_c, step, 32, values, 2)
        return 0

    lax.fori_loop(0, 2, coarse_volume, 0)
    face_c[...] = dot(volume_c[96:192, :], split_c[0:64, :])

    def coarse_faces(step, _):
        values = face_pull(step, load(jump_c, rows_of(step)), state_c, 2, 1)
        store_split(split_cf, step, 96, apply_blocks(block_rows(), values), 2)
        return 0

    lax.fori_loop(0, 6, coarse_faces, 0)
    face_c[...] += dot(give_c[0:96, :], split_cf[0:192, :])
    gather_faces(face_c, 0, 16, 8, compact_c)
    pack(4, lambda f, first, slot: compact_c[f, first : first + slot, :], 48)
    start(4)
    field_c[0:32, :] += dot(give_c[96:128, :], split_cf[0:192, :])

    def split_near(step, _):
        split_faces(step, near_state)
        return 0

    lax.fori_loop(0, 12, split_near, 0)
    near_state_c[...] = dot(pick_face[...], split_f[0:384, :])

    receive(3, compact_c, -1.0)
    scatter_faces(compact_c, 16, 8, jump_c)
    lax.fori_loop(0, 6, coarse_faces, 0)
    face_c[...] += dot(give_c[0:96, :], split_cf[0:192, :])
    field_c[0:32, :] += dot(give_c[96:128, :], split_cf[0:192, :])
    gather_faces(face_c, 0, 16, 8, compact_c)
    own_part(compact_c, own_c)
    scatter_faces(own_c, 16, 8, jump_c)

    def split_coarse_3(step, _):
        store_split(split_c, step, 32, load(field_c, rows_of(step)), 3)
        return 0

    lax.fori_loop(0, 2, split_coarse_3, 0)
    field[...] += dot(extend[...], split_c[...])
    lax.fori_loop(0, 8, split_field, 0)
    cot[...] = dot(volume[...], split_n[...])
    lax.fori_loop(0, 8, lambda s, c: smooth_volume(s, c, False), 0)
    receive_lines(1, line_field)
    lax.fori_loop(0, 6, split_lines, 0)
    across_c[...] = dot(lines_c[...], split_l[...])
    receive(4, compact_c, 1.0)
    scatter_faces(compact_c, 16, 8, near_c)
    neighbour(16, COARSE_FACE, base_c, 2, near_state_c, across_c, signs_c, near_c, jump_c)

    def split_jump(step, _):
        store_split(split_cf, step, 96, load(jump_c, rows_of(step)), 3)
        return 0

    lax.fori_loop(0, 6, split_jump, 0)
    jump[...] += dot(face_extend[...], split_cf[...])
    lax.fori_loop(0, 12, smooth_faces, 0)
    base[...] += dot(give[192:320, :], split_f[0:384, :])
    for v in range(5):
        out_r[v] = base[0:125, lanes(v)]
    outward = pltpu.make_async_copy(out_r, out_h, out_sem)
    outward.start()
    for kind in range(5):
        for f in range(6):
            @pl.when(has[f])
            def _(kind=kind, f=f):
                remote[kind][f].wait_send()
    for level in range(2):
        for line in range(12):
            @pl.when(both[line])
            def _(level=level, line=line):
                remote_lines[level][line].wait_send()
    outward.wait()


def body(*args):
    constants = [jnp.asarray(table) for table in tables().values()]
    vmem = pltpu.VMEM
    raw = [vmem(a.shape, a.dtype) for a in args]
    held = [vmem(t.shape, t.dtype) for t in constants]
    work = [
        vmem((128, 640), F32), vmem((128, 640), F32), vmem((128, 640), F32), vmem((128, 640), F32),
        vmem((384, 640), BF16), vmem((384, 640), F32),
        vmem((192, 640), F32), vmem((192, 640), F32), vmem((192, 640), F32), vmem((192, 640), F32),
        vmem((576, 640), BF16), vmem((6, 128, 128), F32), vmem((6, 128, 128), F32),
        vmem((192, 640), F32), vmem((192, 640), F32), vmem((384, 640), F32), vmem((96, 640), F32),
        vmem((192, 640), BF16), vmem((6, 32, 128), F32), vmem((32, 128), F32), vmem((6, 16, 128), F32),
        vmem((2, 32, 128), F32), vmem((2, 16, 128), F32),
        vmem((128, 640), F32), vmem((224, 640), F32), vmem((224, 640), F32), vmem((96, 640), BF16),
        vmem((288, 640), BF16), vmem((96, 640), F32), vmem((96, 640), F32),
        vmem((6, 48, 128), F32), vmem((6, 48, 128), F32),
        vmem((96, 640), F32), vmem((96, 640), F32), vmem((192, 640), F32), vmem((96, 640), F32),
        vmem((25, 16, 128), F32), vmem((16, 128), F32), vmem(args[0].shape, F32),
    ]
    fine = [vmem((rows, 128), F32) for rows in (64, 64, 16, 16, 16, 16)]
    static = [vmem((rows, 128), F32) for rows in (80, 80, 24, 24, 24, 24)]
    coarse = [vmem((rows, 128), F32) for rows in (24, 24, 8, 8, 8, 8)]
    kinds = [*fine, *fine, *static, *static, *fine, *fine, *coarse, *coarse, *coarse, *coarse]
    sems = [
        pltpu.SemaphoreType.DMA((19,)),
        pltpu.SemaphoreType.DMA,
        pltpu.SemaphoreType.DMA((5, 6)),
        pltpu.SemaphoreType.DMA((5, 6)),
        pltpu.SemaphoreType.DMA((2, 12)),
        pltpu.SemaphoreType.DMA((2, 12)),
    ]
    anywhere = pl.BlockSpec(memory_space=pl.ANY)
    return pl.pallas_call(
        kernel,
        out_shape=jax.ShapeDtypeStruct(args[0].shape, F32),
        in_specs=[anywhere] * (len(args) + len(constants)),
        out_specs=anywhere,
        scratch_shapes=raw + held + work + kinds + [vmem((2, 12, 8, 128), F32)] * 2 + sems,
        compiler_params=pltpu.CompilerParams(
            collective_id=0, has_side_effects=True, vmem_limit_bytes=60 * 1024 * 1024
        ),
    )(*args, *constants)


def solution(mesh):
    in_specs = (
        P(None, None, AXES),
        P(None, None, AXES),
        P(None, AXES),
        P(None, None, AXES),
        P(None, AXES),
        P(*AXES),
        P(None, None, *AXES),
    )
    return jax.shard_map(
        body, mesh=mesh, in_specs=in_specs, out_specs=P(None, None, AXES), check_vma=False
    )
```

```python
import itertools

import jax
import jax.numpy as jnp
import ml_dtypes
import numpy as np
from jax import lax
from jax.experimental import pallas as pl
from jax.experimental.pallas import tpu as pltpu
from jax.sharding import PartitionSpec as P

OMEGA = 0.7
METRIC = 0.25
FINE_FACE = 0.5 * 0.25 / 0.1
COARSE_FACE = 0.5 * 0.25 * 3.0
MESH = pl.DeviceIdType.MESH
AXES = ("gx", "gy", "gz")
COUNTS = (2, 8, 8)
STRIDES = (64, 8, 1)
LINES = [(i, j, s, t) for i, j in ((0, 1), (0, 2), (1, 2)) for s in range(2) for t in range(2)]
F32 = jnp.float32
BF16 = jnp.bfloat16


def diff_table(nodes):
    count = len(nodes)
    weights = np.array(
        [1.0 / np.prod([nodes[j] - nodes[k] for k in range(count) if k != j]) for j in range(count)]
    )
    table = np.zeros((count, count))
    for i in range(count):
        for j in range(count):
            if i != j:
                table[i, j] = weights[j] / weights[i] / (nodes[i] - nodes[j])
        table[i, i] = -np.sum(table[i])
    return table.astype(np.float32).astype(np.float64)


def fine_points():
    return np.array([-1.0, -np.sqrt(3.0 / 7.0), 0.0, np.sqrt(3.0 / 7.0), 1.0])


def interp_table():
    points = fine_points()
    table = np.stack(
        [points * (points - 1.0) / 2.0, 1.0 - points**2, points * (points + 1.0) / 2.0], axis=1
    )
    return table.astype(np.float32).astype(np.float64)


def triple(a, b, c):
    return np.kron(np.kron(a, b), c)


def padded(matrix, rows, columns):
    result = np.zeros((rows, columns))
    result[: matrix.shape[0], : matrix.shape[1]] = matrix
    return result


def face_tables(count, rows, width):
    take = np.zeros((6 * rows, width))
    give = np.zeros((width, 6 * rows))
    for dim in range(3):
        for side in range(2):
            face = 2 * dim + side
            for row in range(rows):
                a, b = divmod(min(row, count * count - 1), count)
                place = [a, b]
                place.insert(dim, side * (count - 1))
                node = (place[0] * count + place[1]) * count + place[2]
                take[face * rows + row, node] = 1.0
                if row < count * count:
                    give[node, face * rows + row] = 1.0
    return take, give


def line_table(count, width):
    take = np.zeros((96, width))
    for line, (i, j, s, t) in enumerate(LINES):
        for node in range(count):
            place = [node] * 3
            place[i], place[j] = s * (count - 1), t * (count - 1)
            take[8 * line + node, (place[0] * count + place[1]) * count + place[2]] = 1.0
    return take


def line_faces(count, rows):
    result = np.zeros((2, 6 * rows, 96))
    for dim in range(3):
        for side in range(2):
            for row in range(rows):
                pair = divmod(min(row, count * count - 1), count)
                others = [d for d in range(3) if d != dim]
                for n in range(2):
                    if pair[n] % (count - 1) == 0:
                        sides = {dim: side, others[n]: pair[n] // (count - 1)}
                        i, j = sorted(sides)
                        line = LINES.index((i, j, sides[i], sides[j]))
                        result[n, (2 * dim + side) * rows + row, 8 * line + pair[1 - n]] = -1.0
    return result.reshape(12 * rows, 96)


def volume_table(count, width):
    table = diff_table(fine_points() if count == 5 else np.array([-1.0, 0.0, 1.0]))
    unit = np.eye(count)
    parts = []
    for dim in range(3):
        mats = [unit, unit, unit]
        mats[dim] = -METRIC * table.T
        parts.append(padded(triple(*mats), width, width))
    return np.concatenate(parts)


def two(matrix):
    high = matrix.astype(ml_dtypes.bfloat16)
    return np.concatenate([high, high], axis=1)


def three(matrix):
    high = matrix.astype(ml_dtypes.bfloat16)
    low = (matrix - high.astype(np.float64)).astype(ml_dtypes.bfloat16)
    return np.concatenate([high, high, low], axis=1)


def tables():
    prolong = interp_table()
    take, give = face_tables(5, 32, 128)
    take_c, give_c = face_tables(3, 16, 32)
    pick = np.zeros((32, 128))
    for n, (a, b, c) in enumerate(itertools.product(range(3), repeat=3)):
        pick[n, (2 * a * 5 + 2 * b) * 5 + 2 * c] = 1.0
    restrict = padded(triple(prolong.T, prolong.T, prolong.T), 32, 128)
    restrict = np.concatenate([restrict, take_c @ restrict, line_table(3, 32) @ restrict])
    extend = padded(triple(prolong, prolong, prolong), 128, 32)
    flat = np.kron(prolong, prolong)
    flat = np.concatenate([flat, np.repeat(flat[24:25], 7, axis=0)])
    face_extend = np.zeros((192, 96))
    for face in range(6):
        face_extend[32 * face : 32 * face + 32, 16 * face : 16 * face + 9] = flat
    face_pick = np.zeros((96, 192))
    for face in range(6):
        for row in range(16):
            a, b = divmod(min(row, 8), 3)
            face_pick[16 * face + row, 32 * face + 10 * a + 2 * b] = 1.0
    return {
        "take": two(np.concatenate([take, line_table(5, 128), pick])),
        "volume": three(volume_table(5, 128)),
        "give": two(-FINE_FACE * np.concatenate([take @ give, give])),
        "restrict": three(restrict),
        "restrict_give": three(-FINE_FACE * restrict @ give),
        "volume_c": two(np.concatenate([volume_table(3, 32), take_c])),
        "give_c": two(-COARSE_FACE * np.concatenate([take_c @ give_c, give_c])),
        "extend": three(extend),
        "face_extend": three(face_extend),
        "lines": two(line_faces(5, 32)),
        "lines_c": two(line_faces(3, 16)),
        "pick_face": two(face_pick),
    }


def dot(matrix, field):
    return jnp.dot(matrix, field, preferred_element_type=F32)


def split(value):
    high = value.astype(BF16)
    low = (value - high.astype(F32)).astype(BF16)
    return high, low


def lanes(var):
    return slice(128 * var, 128 * var + 128)


def steps(count, one, carry):
    for step in range(count):
        one(step, carry)


def rows_of(step, size=16):
    return slice(step * size, step * size + size)


def load(ref, rows):
    return [ref[rows, lanes(v)] for v in range(5)]


def store(ref, rows, values):
    for v in range(5):
        ref[rows, lanes(v)] = values[v]


def store_split(ref, step, height, values, pieces):
    for v in range(5):
        parts = split(values[v])
        for piece in range(pieces):
            ref[rows_of(step + piece * (height // 16)), lanes(v)] = parts[piece % 2]


def pull_all(cot, state):
    w = state[:3]
    enthalpy = state[3]
    crossed = [w[0] * c[1] + w[1] * c[2] + w[2] * c[3] + enthalpy * c[4] for c in cot]
    ends = [w[d] * cot[d][4] for d in range(3)]
    energy = ends[0] + ends[1] + ends[2]
    total = 0.4 * (cot[0][1] + cot[1][2] + cot[2][3] + energy)
    half_square = 0.5 * (w[0] * w[0] + w[1] * w[1] + w[2] * w[2])
    first = half_square * total - (w[0] * crossed[0] + w[1] * crossed[1] + w[2] * crossed[2])
    middle = []
    for j in range(3):
        drift = w[0] * cot[0][1 + j] + w[1] * cot[1][1 + j] + w[2] * cot[2][1 + j]
        middle.append(drift + cot[j][0] + crossed[j] - w[j] * total)
    return [first, *middle, total + energy]


def pull_face(jump, state, d, sign):
    w = state[:3]
    crossed = w[0] * jump[1] + w[1] * jump[2] + w[2] * jump[3] + state[3] * jump[4]
    end = w[d] * jump[4]
    total = 0.4 * (jump[1 + d] + end)
    half_square = 0.5 * (w[0] * w[0] + w[1] * w[1] + w[2] * w[2])
    out = [half_square * total - w[d] * crossed]
    for j in range(3):
        out.append(w[d] * jump[1 + j] - w[j] * total)
    out[1 + d] = out[1 + d] + (jump[0] + crossed)
    out.append(total + end)
    top = jnp.abs(w[d]) + state[4]
    if sign > 0:
        return [top * jump[v] + out[v] for v in range(5)]
    return [top * jump[v] - out[v] for v in range(5)]


def apply_blocks(blocks, values):
    result = []
    for a in range(5):
        total = blocks[a] * values[0]
        for b in range(1, 5):
            total = total + blocks[b * 5 + a] * values[b]
        result.append(total)
    return result


def kernel(start_h, source_h, density_h, velocity_h, pressure_h, shift_h, inverse_h, *rest):
    tables_h, rest = rest[:12], rest[12:]
    out_h, rest = rest[0], rest[1:]
    (start_r, source_r, density_r, velocity_r, pressure_r, shift_r, inverse_r), rest = rest[:7], rest[7:]
    tables_r, rest = rest[:12], rest[12:]
    (
        take, volume, give, restrict, restrict_give, volume_c, give_c, extend, face_extend,
        lines, lines_c, pick_face,
    ) = tables_r
    (
        field, source, state, base, split_n, cot,
        face_state, start_face, face_field, jump, split_f, compact, own,
        near_state, across, line_field, split_l, near_blocks, block_row, edges, signs, signs_c,
        state_c, field_c, base_c, split_c, split_cf, cot_c, jump_c, compact_c, own_c,
        near_state_c, across_c, face_c,
        blocks, shift,
    ), rest = rest[:36], rest[36:]
    kinds = []
    for _ in range(5):
        kinds.append((rest[:6], rest[6:12]))
        rest = rest[12:]
    fine_u, fine_t, fine_w, coarse_u, coarse_w = kinds
    send_lines, recv_lines, in_sems, send_sems, recv_sems, send_line_sems, recv_line_sems = rest

    place = [lax.axis_index(axis) for axis in AXES]
    size = [lax.axis_size(axis) for axis in AXES]
    has = [place[f // 2] > 0 if f % 2 == 0 else place[f // 2] < size[f // 2] - 1 for f in range(6)]

    def partner(f):
        target = list(place)
        target[f // 2] = target[f // 2] + (1 if f % 2 else -1)
        return tuple(target)

    both = [has[2 * i + s] & has[2 * j + t] for i, j, s, t in LINES]

    def line_partner(line):
        i, j, s, t = LINES[line]
        target = list(place)
        target[i] = target[i] + 2 * s - 1
        target[j] = target[j] + 2 * t - 1
        return tuple(target)

    barrier = pltpu.get_barrier_semaphore()
    for f in range(6):
        @pl.when(has[f])
        def _(f=f):
            pl.semaphore_signal(barrier, inc=1, device_id=partner(f), device_id_type=MESH)
    for line in range(12):
        @pl.when(both[line])
        def _(line=line):
            pl.semaphore_signal(barrier, inc=1, device_id=line_partner(line), device_id_type=MESH)

    field[120:128, :] = jnp.zeros((8, 640), F32)
    source[120:128, :] = jnp.zeros((8, 640), F32)
    order = [
        (start_h, start_r), (tables_h[0], take), (velocity_h, velocity_r), (density_h, density_r),
        (pressure_h, pressure_r), (tables_h[1], volume), (source_h, source_r), (shift_h, shift_r),
        (inverse_h, inverse_r), (tables_h[2], give),
    ] + [(tables_h[n], tables_r[n]) for n in range(3, 12)]
    inward = [pltpu.make_async_copy(a, b, in_sems.at[n]) for n, (a, b) in enumerate(order)]
    for copy in inward:
        copy.start()

    def lane_place(rows, dim):
        lane = lax.broadcasted_iota(jnp.int32, (rows, 128), 1)
        return (lane // STRIDES[dim]) % COUNTS[dim]

    def gather_faces(source_ref, offset, rows, whole, target):
        sub = lax.broadcasted_iota(jnp.int32, (8, 128), 0)

        def one(f, _):
            top = offset + f * rows
            last = source_ref[slice(top + whole, top + whole + 8), lanes(0)]
            for v in range(5):
                target[f, whole * v : whole * v + whole, :] = source_ref[
                    slice(top, top + whole), lanes(v)
                ]
                if v:
                    here = source_ref[slice(top + whole, top + whole + 8), lanes(v)]
                    last = jnp.where(sub == v, here, last)
            target[f, 5 * whole : 5 * whole + 8, :] = last
            return 0

        steps(6, one, 0)

    def scatter_faces(source_ref, rows, whole, target, add=False):
        def put(here, v, value):
            target[here, lanes(v)] = target[here, lanes(v)] + value if add else value

        def one(f, _):
            top = f * rows
            for v in range(5):
                put(slice(top, top + whole), v, source_ref[f, whole * v : whole * v + whole, :])
                last = source_ref[f, 5 * whole + v : 5 * whole + v + 1, :]
                put(slice(top + whole, top + whole + 8), v, jnp.broadcast_to(last, (8, 128)))
            return 0

        steps(6, one, 0)

    def turn(value, amount):
        amount %= 128
        return pltpu.roll(value, amount, 1) if amount else value

    def copies(kind):
        sends, receives = kinds[kind]
        return [
            pltpu.make_async_remote_copy(
                src_ref=sends[f],
                dst_ref=receives[f ^ 1],
                send_sem=send_sems.at[kind, f],
                recv_sem=recv_sems.at[kind, f ^ 1],
                device_id=partner(f),
                device_id_type=MESH,
            )
            for f in range(6)
        ]

    def line_copies(level):
        return [
            pltpu.make_async_remote_copy(
                src_ref=send_lines.at[level, line],
                dst_ref=recv_lines.at[level, line ^ 3],
                send_sem=send_line_sems.at[level, line],
                recv_sem=recv_line_sems.at[level, line ^ 3],
                device_id=line_partner(line),
                device_id_type=MESH,
            )
            for line in range(12)
        ]

    remote = [copies(kind) for kind in range(5)]
    remote_lines = [line_copies(level) for level in range(2)]

    def pack(kind, read, height, top=0, slots=None):
        for f in range(6):
            dim, side = divmod(f, 2)
            count, stride = COUNTS[dim], STRIDES[dim]
            target = kinds[kind][0][f]
            slot = target.shape[0] if slots is None else slots[dim]
            where = lane_place(slot, dim)
            packed = None
            for g in range(height // slot):
                block = turn(read(f, g * slot, slot), (g - side * (count - 1)) * stride)
                packed = block if packed is None else jnp.where(where == g, block, packed)
            first = top if slots is None else top[dim]
            target[first : first + slot, :] = packed

    def pack_lines(level, source_ref, offset):
        for line, (i, j, s, t) in enumerate(LINES):
            where = lane_place(8, j)
            packed = None
            for v in range(5):
                block = source_ref[offset + 8 * line : offset + 8 * line + 8, lanes(v)]
                block = turn(block, (v - t * (COUNTS[j] - 1)) * STRIDES[j])
                packed = block if packed is None else jnp.where(where == v, block, packed)
            send_lines[level, line] = packed

    def start(kind):
        for f in range(6):
            @pl.when(has[f])
            def _(f=f):
                remote[kind][f].start()

    def start_lines(level):
        for line in range(12):
            @pl.when(both[line])
            def _(line=line):
                remote_lines[level][line].start()

    def unpack(kind, f, height, write, sign=1.0, top=0, slots=None):
        dim, side = divmod(f, 2)
        count, stride = COUNTS[dim], STRIDES[dim]
        received = kinds[kind][1][f]
        slot = received.shape[0] if slots is None else slots[dim]
        first = top if slots is None else top[dim]
        edge = jnp.where(lane_place(slot, dim) == side * (count - 1), sign, 0.0)

        @pl.when(has[f])
        def _():
            packed = received[first : first + slot, :]
            for g in range(height // slot):
                write(f, g * slot, slot, edge * turn(packed, (side * (count - 1) - g) * stride))

        @pl.when(jnp.logical_not(has[f]))
        def _():
            write(f, 0, height, jnp.zeros((height, 128), F32))

    def arrive(kind, f):
        @pl.when(has[f])
        def _():
            remote[kind][f ^ 1].wait_recv()

    def receive(kind, target, sign):
        def write(f, first, slot, value):
            target[f, first : first + slot, :] = value

        for f in range(6):
            arrive(kind, f)
            unpack(kind, f, target.shape[1], write, sign)

    def receive_lines(level, target):
        for line, (i, j, s, t) in enumerate(LINES):
            edge = (lane_place(8, i) == s * (COUNTS[i] - 1)) & (lane_place(8, j) == t * (COUNTS[j] - 1))
            here = slice(8 * line, 8 * line + 8)

            @pl.when(both[line])
            def _():
                remote_lines[level][line ^ 3].wait_recv()
                packed = recv_lines[level, line]
                for v in range(5):
                    amount = (t * (COUNTS[j] - 1) - v) * STRIDES[j] + (2 * s - 1) * (COUNTS[i] - 1) * STRIDES[i]
                    target[here, lanes(v)] = jnp.where(edge, turn(packed, amount), 0.0)

            @pl.when(jnp.logical_not(both[line]))
            def _():
                target[here, :] = jnp.zeros((8, 640), F32)

    def own_part(faces, result):
        for f in range(6):
            dim, side = divmod(f, 2)
            count, stride = COUNTS[dim], STRIDES[dim]
            inside = lane_place(faces.shape[1], dim) != side * (count - 1)
            other = turn(faces[f ^ 1], -stride if side else stride)
            result[f] = faces[f] - jnp.where(inside, other, 0.0)

    def face_pull(step, values, state_ref, offset, per_face):
        d, side = divmod(step // per_face, 2)
        return pull_face(values, load(state_ref, rows_of(step + offset)), d, 2 * side - 1)

    def neighbour(rows, face, mine, offset, near_s, across_ref, sign_ref, target):
        per_face = rows // 16
        for d in range(3):
            p, q = [n for n in range(3) if n != d]

            def one(step, _, d=d, p=p, q=q):
                side = step // per_face
                f = 2 * d + side
                at = step + 2 * d * per_face
                here = rows_of(at)
                local = load(near_s, here)
                top = [jnp.abs(local[n]) + local[4] for n in range(3)]
                edge = edges[f]
                own_side = load(mine, rows_of(at + offset))
                jumps = [None] * 3
                jumps[d] = [-edge * value for value in own_side]
                jumps[p] = load(across_ref, here)
                jumps[q] = load(across_ref, rows_of(at + 6 * per_face))
                part = rows_of(step - side * per_face)
                sign = [None] * 3
                sign[d] = 1.0 - 2.0 * side
                sign[p], sign[q] = sign_ref[0, part, :], sign_ref[1, part, :]
                pulled = pull_all([[sign[n] * value for value in jumps[n]] for n in range(3)], local)
                for n in range(3):
                    pulled = [pulled[v] + top[n] * jumps[n][v] for v in range(5)]
                inverse = [near_blocks[f, n : n + 1, :] for n in range(25)]
                change = apply_blocks(inverse, pulled)
                jumps_now = load(target, here)
                store(target, here, [jumps_now[v] + face * change[v] for v in range(5)])
                return 0

            steps(2 * per_face, one, 0)

    def block_rows():
        return [blocks[n] for n in range(25)]

    for f in range(6):
        dim, side = divmod(f, 2)
        edges[f] = (lane_place(16, dim) == side * (COUNTS[dim] - 1)).astype(F32)
    for ref, rows, count in ((signs, 32, 5), (signs_c, 16, 3)):
        row = jnp.minimum(lax.broadcasted_iota(jnp.int32, (rows, 128), 0), count * count - 1)
        for n, at in enumerate((row // count, row % count)):
            ref[n] = jnp.where(at == 0, -1.0, jnp.where(at == count - 1, 1.0, 0.0))
    block_row[...] = jnp.zeros((32, 128), F32)
    inward[0].wait()
    for v in range(5):
        field[0:125, lanes(v)] = start_r[v]

    def split_field(step, _):
        store_split(split_n, step, 128, load(field, rows_of(step)), 3)
        return 0

    steps(8, split_field, 0)
    inward[1].wait()
    start_face[...] = dot(take[0:192, :], split_n[0:256, :])
    line_field[...] = dot(take[192:288, :], split_n[0:256, :])
    gather_faces(start_face, 0, 32, 24, compact)
    pack(0, lambda f, first, slot: compact[f, first : first + slot, :], 128)
    pack_lines(0, line_field, 0)
    own_part(compact, own)
    scatter_faces(own, 32, 24, jump)

    for n in (2, 3, 4):
        inward[n].wait()
    state[120:128, :] = jnp.zeros((8, 640), F32)
    for part in ((0, 64), (64, 125)):
        here = slice(*part)
        w = [velocity_r[d, here, :] for d in range(3)]
        sound_2 = 1.4 * pressure_r[here, :] / density_r[here, :]
        for d in range(3):
            state[here, lanes(d)] = w[d]
        state[here, lanes(3)] = 2.5 * sound_2 + 0.5 * (w[0] * w[0] + w[1] * w[1] + w[2] * w[2])
        state[here, lanes(4)] = jnp.sqrt(sound_2)

    def split_state(step, _):
        store_split(split_f, step, 128, load(state, rows_of(step)), 2)
        return 0

    steps(8, split_state, 0)
    face_state[...] = dot(take[0:192, :], split_f[0:256, :])
    state_c[0:32, :] = dot(take[288:320, :], split_f[0:256, :])

    for n in (7, 8):
        inward[n].wait()
    spread = (
        lax.broadcasted_iota(jnp.int32, (8, 128), 1) % 8 == lax.broadcasted_iota(jnp.int32, (8, 128), 0)
    ).astype(F32)

    def to_lanes(value, count):
        wide = jnp.dot(
            value.reshape(16 * count, 8), spread,
            precision=lax.Precision.HIGHEST, preferred_element_type=F32,
        ).reshape(count, 16, 128)
        row = lax.broadcasted_iota(jnp.int32, (count, 16, 128), 1)
        lane = lax.broadcasted_iota(jnp.int32, (count, 16, 128), 2)
        kept = jnp.where(lane // 8 == row, wide, 0.0)
        return jnp.broadcast_to(jnp.sum(kept, axis=1, keepdims=True), (count, 16, 128))

    shift[...] = to_lanes(shift_r[...], 1)[0]
    blocks[...] = OMEGA * to_lanes(inverse_r[...], 25)

    for n in range(25):
        block_row[n : n + 1, :] = blocks[n, 0:1, :]
    gather_faces(face_state, 0, 32, 24, compact)
    slots, tops = (64, 16, 16), (0, 0, 0)
    pack(1, lambda f, first, slot: compact[f, first : first + slot, :], 128, tops, slots)
    block_slots, block_tops = (16, 8, 8), (64, 16, 16)
    pack(1, lambda f, first, slot: block_row[first : first + slot, :], 32, block_tops, block_slots)

    inward[5].wait()
    inward[6].wait()
    for v in range(5):
        source[0:125, lanes(v)] = source_r[v]

    def residual(step, height, cot_ref, values, right, state_ref):
        rows = rows_of(step)
        cots = [load(cot_ref, rows_of(step + d * (height // 16))) for d in range(3)]
        pulled = pull_all(cots, load(state_ref, rows))
        return [right[v] - shift[...] * values[v] - pulled[v] for v in range(5)]

    def smooth_volume(step, _, keep_split):
        rows = rows_of(step)
        values = load(field, rows)
        resid = residual(step, 128, cot, values, load(source, rows), state)
        change = apply_blocks(block_rows(), resid)
        values = [values[v] + change[v] for v in range(5)]
        store(base, rows, values)
        if keep_split:
            store_split(split_n, step, 128, values, 2)
        return 0

    cot[...] = dot(volume[...], split_n[...])
    steps(8, lambda s, c: smooth_volume(s, c, True), 0)
    pl.semaphore_wait(barrier, sum(h.astype(jnp.int32) for h in has + both))
    start(0)
    start(1)
    start_lines(0)
    face_field[...] = dot(take[0:192, :], split_n[0:256, :])

    def smooth_faces(step, _):
        values = face_pull(step, load(jump, rows_of(step)), face_state, 0, 2)
        store_split(split_f, step, 192, apply_blocks(block_rows(), values), 2)
        return 0

    steps(12, smooth_faces, 0)
    inward[9].wait()
    face_field[...] += dot(give[0:192, :], split_f[0:384, :])
    gather_faces(face_field, 0, 32, 24, compact)
    pack(2, lambda f, first, slot: compact[f, first : first + slot, :], 128)
    start(2)
    base[...] += dot(give[192:320, :], split_f[0:384, :])
    for n in range(10, 19):
        inward[n].wait()

    def split_faces(step, ref):
        store_split(split_f, step, 192, load(ref, rows_of(step)), 2)

    def split_face_state(step, _):
        split_faces(step, face_state)
        return 0

    steps(12, split_face_state, 0)
    state_c[32:128, :] = dot(pick_face[...], split_f[0:384, :])

    receive(0, compact, -1.0)
    scatter_faces(compact, 32, 24, jump)
    steps(12, smooth_faces, 0)
    face_field[...] += dot(give[0:192, :], split_f[0:384, :])
    field[...] = base[...] + dot(give[192:320, :], split_f[0:384, :])
    gather_faces(face_field, 0, 32, 24, compact)
    own_part(compact, own)
    scatter_faces(own, 32, 24, jump)
    steps(8, split_field, 0)
    cot[...] = dot(volume[...], split_n[...])

    def residual_volume(step, _):
        rows = rows_of(step)
        resid = residual(step, 128, cot, load(field, rows), load(source, rows), state)
        store_split(split_n, step, 128, resid, 3)
        return 0

    steps(8, residual_volume, 0)
    field_c[...] = dot(restrict[...], split_n[...])

    def write_state(f, first, slot, value):
        compact[f, first : first + slot, :] = value

    def write_blocks(f, first, slot, value):
        near_blocks[f, first : first + slot, :] = value

    for f in range(6):
        arrive(1, f)
        unpack(1, f, 128, write_state, 1.0, tops, slots)
        unpack(1, f, 32, write_blocks, 1.0, block_tops, block_slots)
    scatter_faces(compact, 32, 24, near_state)
    receive_lines(0, line_field)

    def split_lines(step, _):
        store_split(split_l, step, 96, load(line_field, rows_of(step)), 2)
        return 0

    steps(6, split_lines, 0)
    across[...] = dot(lines[...], split_l[...])
    neighbour(32, FINE_FACE, start_face, 0, near_state, across, signs, jump)
    receive(2, compact, -1.0)
    scatter_faces(compact, 32, 24, jump, True)

    def residual_faces(step, _):
        values = face_pull(step, load(jump, rows_of(step)), face_state, 0, 2)
        store_split(split_f, step, 192, values, 3)
        return 0

    steps(12, residual_faces, 0)
    field_c[...] += dot(restrict_give[...], split_f[...])

    def coarse_first(step, _):
        rows = rows_of(step)
        store(base_c, rows, apply_blocks(block_rows(), load(field_c, rows)))
        return 0

    steps(14, coarse_first, 0)
    gather_faces(base_c, 32, 16, 8, compact_c)
    pack(3, lambda f, first, slot: compact_c[f, first : first + slot, :], 48)
    start(3)
    pack_lines(1, base_c, 128)
    start_lines(1)
    own_part(compact_c, own_c)
    scatter_faces(own_c, 16, 8, jump_c)

    def split_coarse(step, _):
        store_split(split_c, step, 32, load(base_c, rows_of(step)), 2)
        return 0

    steps(2, split_coarse, 0)
    cot_c[...] = dot(volume_c[0:96, :], split_c[0:64, :])

    def coarse_volume(step, _):
        rows = rows_of(step)
        values = load(base_c, rows)
        resid = residual(step, 32, cot_c, values, load(field_c, rows), state_c)
        change = apply_blocks(block_rows(), resid)
        values = [values[v] + change[v] for v in range(5)]
        store(field_c, rows, values)
        store_split(split_c, step, 32, values, 2)
        return 0

    steps(2, coarse_volume, 0)
    face_c[...] = dot(volume_c[96:192, :], split_c[0:64, :])

    def coarse_faces(step, _):
        values = face_pull(step, load(jump_c, rows_of(step)), state_c, 2, 1)
        store_split(split_cf, step, 96, apply_blocks(block_rows(), values), 2)
        return 0

    steps(6, coarse_faces, 0)
    face_c[...] += dot(give_c[0:96, :], split_cf[0:192, :])
    gather_faces(face_c, 0, 16, 8, compact_c)
    pack(4, lambda f, first, slot: compact_c[f, first : first + slot, :], 48)
    start(4)
    field_c[0:32, :] += dot(give_c[96:128, :], split_cf[0:192, :])

    def split_near(step, _):
        split_faces(step, near_state)
        return 0

    steps(12, split_near, 0)
    near_state_c[...] = dot(pick_face[...], split_f[0:384, :])

    receive(3, compact_c, -1.0)
    scatter_faces(compact_c, 16, 8, jump_c)
    steps(6, coarse_faces, 0)
    face_c[...] += dot(give_c[0:96, :], split_cf[0:192, :])
    field_c[0:32, :] += dot(give_c[96:128, :], split_cf[0:192, :])
    gather_faces(face_c, 0, 16, 8, compact_c)
    own_part(compact_c, own_c)
    scatter_faces(own_c, 16, 8, jump_c)

    def split_coarse_3(step, _):
        store_split(split_c, step, 32, load(field_c, rows_of(step)), 3)
        return 0

    steps(2, split_coarse_3, 0)
    field[...] += dot(extend[...], split_c[...])
    steps(8, split_field, 0)
    cot[...] = dot(volume[...], split_n[...])
    steps(8, lambda s, c: smooth_volume(s, c, False), 0)
    receive_lines(1, line_field)
    steps(6, split_lines, 0)
    across_c[...] = dot(lines_c[...], split_l[...])
    neighbour(16, COARSE_FACE, base_c, 2, near_state_c, across_c, signs_c, jump_c)
    receive(4, compact_c, -1.0)
    scatter_faces(compact_c, 16, 8, jump_c, True)

    def split_jump(step, _):
        store_split(split_cf, step, 96, load(jump_c, rows_of(step)), 3)
        return 0

    steps(6, split_jump, 0)
    jump[...] += dot(face_extend[...], split_cf[...])
    steps(12, smooth_faces, 0)
    base[...] += dot(give[192:320, :], split_f[0:384, :])
    for v in range(5):
        out_h[v] = base[0:125, lanes(v)]
    for kind in range(5):
        for f in range(6):
            @pl.when(has[f])
            def _(kind=kind, f=f):
                remote[kind][f].wait_send()
    for level in range(2):
        for line in range(12):
            @pl.when(both[line])
            def _(level=level, line=line):
                remote_lines[level][line].wait_send()


def body(*args):
    constants = [jnp.asarray(table) for table in tables().values()]
    vmem = pltpu.VMEM
    raw = [vmem(a.shape, a.dtype) for a in args]
    held = [vmem(t.shape, t.dtype) for t in constants]
    work = [
        vmem((128, 640), F32), vmem((128, 640), F32), vmem((128, 640), F32), vmem((128, 640), F32),
        vmem((384, 640), BF16), vmem((384, 640), F32),
        vmem((192, 640), F32), vmem((192, 640), F32), vmem((192, 640), F32), vmem((192, 640), F32),
        vmem((576, 640), BF16), vmem((6, 128, 128), F32), vmem((6, 128, 128), F32),
        vmem((192, 640), F32), vmem((384, 640), F32), vmem((96, 640), F32),
        vmem((192, 640), BF16), vmem((6, 32, 128), F32), vmem((32, 128), F32), vmem((6, 16, 128), F32),
        vmem((2, 32, 128), F32), vmem((2, 16, 128), F32),
        vmem((128, 640), F32), vmem((224, 640), F32), vmem((224, 640), F32), vmem((96, 640), BF16),
        vmem((288, 640), BF16), vmem((96, 640), F32), vmem((96, 640), F32),
        vmem((6, 48, 128), F32), vmem((6, 48, 128), F32),
        vmem((96, 640), F32), vmem((192, 640), F32), vmem((96, 640), F32),
        vmem((25, 16, 128), F32), vmem((16, 128), F32),
    ]
    fine = [vmem((rows, 128), F32) for rows in (64, 64, 16, 16, 16, 16)]
    static = [vmem((rows, 128), F32) for rows in (80, 80, 24, 24, 24, 24)]
    coarse = [vmem((rows, 128), F32) for rows in (24, 24, 8, 8, 8, 8)]
    kinds = [*fine, *fine, *static, *static, *fine, *fine, *coarse, *coarse, *coarse, *coarse]
    sems = [
        pltpu.SemaphoreType.DMA((19,)),
        pltpu.SemaphoreType.DMA((5, 6)),
        pltpu.SemaphoreType.DMA((5, 6)),
        pltpu.SemaphoreType.DMA((2, 12)),
        pltpu.SemaphoreType.DMA((2, 12)),
    ]
    anywhere = pl.BlockSpec(memory_space=pl.ANY)
    return pl.pallas_call(
        kernel,
        out_shape=pltpu.VMEM(args[0].shape, F32),
        in_specs=[anywhere] * (len(args) + len(constants)),
        out_specs=pl.BlockSpec(memory_space=pltpu.VMEM),
        scratch_shapes=raw + held + work + kinds + [vmem((2, 12, 8, 128), F32)] * 2 + sems,
        compiler_params=pltpu.CompilerParams(
            collective_id=0, has_side_effects=True, vmem_limit_bytes=60 * 1024 * 1024
        ),
    )(*args, *constants)


def solution(mesh):
    in_specs = (
        P(None, None, AXES),
        P(None, None, AXES),
        P(None, AXES),
        P(None, None, AXES),
        P(None, AXES),
        P(*AXES),
        P(None, None, *AXES),
    )
    return jax.shard_map(
        body, mesh=mesh, in_specs=in_specs, out_specs=P(None, None, AXES), check_vma=False
    )
```

```python
import itertools

import jax
import jax.numpy as jnp
import ml_dtypes
import numpy as np
from jax import lax
from jax.experimental import pallas as pl
from jax.experimental.pallas import tpu as pltpu
from jax.sharding import PartitionSpec as P

OMEGA = 0.7
METRIC = 0.25
FINE_FACE = 0.5 * 0.25 / 0.1
COARSE_FACE = 0.5 * 0.25 * 3.0
MESH = pl.DeviceIdType.MESH
AXES = ("gx", "gy", "gz")
COUNTS = (2, 8, 8)
STRIDES = (64, 8, 1)
LINES = [(i, j, s, t) for i, j in ((0, 1), (0, 2), (1, 2)) for s in range(2) for t in range(2)]
F32 = jnp.float32
BF16 = jnp.bfloat16


def diff_table(nodes):
    count = len(nodes)
    weights = np.array(
        [1.0 / np.prod([nodes[j] - nodes[k] for k in range(count) if k != j]) for j in range(count)]
    )
    table = np.zeros((count, count))
    for i in range(count):
        for j in range(count):
            if i != j:
                table[i, j] = weights[j] / weights[i] / (nodes[i] - nodes[j])
        table[i, i] = -np.sum(table[i])
    return table.astype(np.float32).astype(np.float64)


def fine_points():
    return np.array([-1.0, -np.sqrt(3.0 / 7.0), 0.0, np.sqrt(3.0 / 7.0), 1.0])


def interp_table():
    points = fine_points()
    table = np.stack(
        [points * (points - 1.0) / 2.0, 1.0 - points**2, points * (points + 1.0) / 2.0], axis=1
    )
    return table.astype(np.float32).astype(np.float64)


def triple(a, b, c):
    return np.kron(np.kron(a, b), c)


def padded(matrix, rows, columns):
    result = np.zeros((rows, columns))
    result[: matrix.shape[0], : matrix.shape[1]] = matrix
    return result


def face_tables(count, rows, width):
    take = np.zeros((6 * rows, width))
    give = np.zeros((width, 6 * rows))
    for dim in range(3):
        for side in range(2):
            face = 2 * dim + side
            for row in range(rows):
                a, b = divmod(min(row, count * count - 1), count)
                place = [a, b]
                place.insert(dim, side * (count - 1))
                node = (place[0] * count + place[1]) * count + place[2]
                take[face * rows + row, node] = 1.0
                if row < count * count:
                    give[node, face * rows + row] = 1.0
    return take, give


def line_table(count, width):
    take = np.zeros((96, width))
    for line, (i, j, s, t) in enumerate(LINES):
        for node in range(count):
            place = [node] * 3
            place[i], place[j] = s * (count - 1), t * (count - 1)
            take[8 * line + node, (place[0] * count + place[1]) * count + place[2]] = 1.0
    return take


def line_faces(count, rows):
    result = np.zeros((2, 6 * rows, 96))
    for dim in range(3):
        for side in range(2):
            for row in range(rows):
                pair = divmod(min(row, count * count - 1), count)
                others = [d for d in range(3) if d != dim]
                for n in range(2):
                    if pair[n] % (count - 1) == 0:
                        sides = {dim: side, others[n]: pair[n] // (count - 1)}
                        i, j = sorted(sides)
                        line = LINES.index((i, j, sides[i], sides[j]))
                        result[n, (2 * dim + side) * rows + row, 8 * line + pair[1 - n]] = -1.0
    return result.reshape(12 * rows, 96)


def volume_table(count, width):
    table = diff_table(fine_points() if count == 5 else np.array([-1.0, 0.0, 1.0]))
    unit = np.eye(count)
    parts = []
    for dim in range(3):
        mats = [unit, unit, unit]
        mats[dim] = -METRIC * table.T
        parts.append(padded(triple(*mats), width, width))
    return np.concatenate(parts)


def two(matrix):
    high = matrix.astype(ml_dtypes.bfloat16)
    return np.concatenate([high, high], axis=1)


def three(matrix):
    high = matrix.astype(ml_dtypes.bfloat16)
    low = (matrix - high.astype(np.float64)).astype(ml_dtypes.bfloat16)
    return np.concatenate([high, high, low], axis=1)


def tables():
    prolong = interp_table()
    take, give = face_tables(5, 32, 128)
    take_c, give_c = face_tables(3, 16, 32)
    pick = np.zeros((32, 128))
    for n, (a, b, c) in enumerate(itertools.product(range(3), repeat=3)):
        pick[n, (2 * a * 5 + 2 * b) * 5 + 2 * c] = 1.0
    restrict = padded(triple(prolong.T, prolong.T, prolong.T), 32, 128)
    restrict = np.concatenate([restrict, take_c @ restrict, line_table(3, 32) @ restrict])
    extend = padded(triple(prolong, prolong, prolong), 128, 32)
    flat = np.kron(prolong, prolong)
    flat = np.concatenate([flat, np.repeat(flat[24:25], 7, axis=0)])
    face_extend = np.zeros((192, 96))
    for face in range(6):
        face_extend[32 * face : 32 * face + 32, 16 * face : 16 * face + 9] = flat
    correct = -COARSE_FACE * give_c
    face_pick = np.zeros((96, 192))
    for face in range(6):
        for row in range(16):
            a, b = divmod(min(row, 8), 3)
            face_pick[16 * face + row, 32 * face + 10 * a + 2 * b] = 1.0
    return {
        "take": two(np.concatenate([take, line_table(5, 128), pick])),
        "volume": three(volume_table(5, 128)),
        "give": two(-FINE_FACE * np.concatenate([take @ give, give])),
        "restrict": three(restrict),
        "restrict_give": three(-FINE_FACE * restrict @ give),
        "volume_c": two(np.concatenate([volume_table(3, 32), take_c])),
        "give_c": two(-COARSE_FACE * np.concatenate([take_c @ give_c, give_c])),
        "extend": three(extend),
        "face_extend": three(face_extend),
        "chain": three(np.concatenate([take_c @ correct, extend @ correct, volume_table(5, 128) @ extend @ correct])),
        "lines": two(line_faces(5, 32)),
        "lines_c": two(line_faces(3, 16)),
        "pick_face": two(face_pick),
    }


def dot(matrix, field):
    return jnp.dot(matrix, field, preferred_element_type=F32)


def split(value):
    high = value.astype(BF16)
    low = (value - high.astype(F32)).astype(BF16)
    return high, low


def lanes(var):
    return slice(128 * var, 128 * var + 128)


def steps(count, one, carry):
    for step in range(count):
        one(step, carry)


def rows_of(step, size=16):
    return slice(step * size, step * size + size)


def load(ref, rows):
    return [ref[rows, lanes(v)] for v in range(5)]


def store(ref, rows, values):
    for v in range(5):
        ref[rows, lanes(v)] = values[v]


def store_split(ref, step, height, values, pieces):
    for v in range(5):
        parts = split(values[v])
        for piece in range(pieces):
            ref[rows_of(step + piece * (height // 16)), lanes(v)] = parts[piece % 2]


def pull_all(cot, state):
    w = state[:3]
    enthalpy = state[3]
    crossed = [w[0] * c[1] + w[1] * c[2] + w[2] * c[3] + enthalpy * c[4] for c in cot]
    ends = [w[d] * cot[d][4] for d in range(3)]
    energy = ends[0] + ends[1] + ends[2]
    total = 0.4 * (cot[0][1] + cot[1][2] + cot[2][3] + energy)
    half_square = 0.5 * (w[0] * w[0] + w[1] * w[1] + w[2] * w[2])
    first = half_square * total - (w[0] * crossed[0] + w[1] * crossed[1] + w[2] * crossed[2])
    middle = []
    for j in range(3):
        drift = w[0] * cot[0][1 + j] + w[1] * cot[1][1 + j] + w[2] * cot[2][1 + j]
        middle.append(drift + cot[j][0] + crossed[j] - w[j] * total)
    return [first, *middle, total + energy]


def pull_face(jump, state, d, sign):
    w = state[:3]
    crossed = w[0] * jump[1] + w[1] * jump[2] + w[2] * jump[3] + state[3] * jump[4]
    end = w[d] * jump[4]
    total = 0.4 * (jump[1 + d] + end)
    half_square = 0.5 * (w[0] * w[0] + w[1] * w[1] + w[2] * w[2])
    out = [half_square * total - w[d] * crossed]
    for j in range(3):
        out.append(w[d] * jump[1 + j] - w[j] * total)
    out[1 + d] = out[1 + d] + (jump[0] + crossed)
    out.append(total + end)
    top = jnp.abs(w[d]) + state[4]
    if sign > 0:
        return [top * jump[v] + out[v] for v in range(5)]
    return [top * jump[v] - out[v] for v in range(5)]


def apply_blocks(blocks, values):
    result = []
    for a in range(5):
        total = blocks[a] * values[0]
        for b in range(1, 5):
            total = total + blocks[b * 5 + a] * values[b]
        result.append(total)
    return result


def kernel(start_h, source_h, density_h, velocity_h, pressure_h, shift_h, inverse_h, *rest):
    tables_h, rest = rest[:13], rest[13:]
    out_h, rest = rest[0], rest[1:]
    (start_r, source_r, density_r, velocity_r, pressure_r, shift_r, inverse_r), rest = rest[:7], rest[7:]
    tables_r, rest = rest[:13], rest[13:]
    (
        take, volume, give, restrict, restrict_give, volume_c, give_c, extend, face_extend,
        chain, lines, lines_c, pick_face,
    ) = tables_r
    (
        field, source, state, base, split_n, cot,
        face_state, start_face, face_field, jump, split_f, compact, own,
        near_state, across, line_field, split_l, near_blocks, block_row, edges, signs, signs_c,
        state_c, field_c, base_c, split_c, split_cf, cot_c, jump_c, compact_c, own_c,
        near_state_c, near_c, across_c, face_c,
        blocks, shift,
    ), rest = rest[:37], rest[37:]
    kinds = []
    for _ in range(5):
        kinds.append((rest[:6], rest[6:12]))
        rest = rest[12:]
    fine_u, fine_t, fine_w, coarse_u, coarse_w = kinds
    send_lines, recv_lines, in_sems, send_sems, recv_sems, send_line_sems, recv_line_sems = rest

    place = [lax.axis_index(axis) for axis in AXES]
    size = [lax.axis_size(axis) for axis in AXES]
    has = [place[f // 2] > 0 if f % 2 == 0 else place[f // 2] < size[f // 2] - 1 for f in range(6)]

    def partner(f):
        target = list(place)
        target[f // 2] = target[f // 2] + (1 if f % 2 else -1)
        return tuple(target)

    both = [has[2 * i + s] & has[2 * j + t] for i, j, s, t in LINES]

    def line_partner(line):
        i, j, s, t = LINES[line]
        target = list(place)
        target[i] = target[i] + 2 * s - 1
        target[j] = target[j] + 2 * t - 1
        return tuple(target)

    barrier = pltpu.get_barrier_semaphore()
    for f in range(6):
        @pl.when(has[f])
        def _(f=f):
            pl.semaphore_signal(barrier, inc=1, device_id=partner(f), device_id_type=MESH)
    for line in range(12):
        @pl.when(both[line])
        def _(line=line):
            pl.semaphore_signal(barrier, inc=1, device_id=line_partner(line), device_id_type=MESH)

    field[120:128, :] = jnp.zeros((8, 640), F32)
    source[120:128, :] = jnp.zeros((8, 640), F32)
    order = [
        (start_h, start_r), (tables_h[0], take), (velocity_h, velocity_r), (density_h, density_r),
        (pressure_h, pressure_r), (tables_h[1], volume), (source_h, source_r), (shift_h, shift_r),
        (inverse_h, inverse_r), (tables_h[2], give),
    ] + [(tables_h[n], tables_r[n]) for n in range(3, 13)]
    inward = [pltpu.make_async_copy(a, b, in_sems.at[n]) for n, (a, b) in enumerate(order)]
    for n in (0, 1, 2, 3, 4, 8, 7, 5, 6, *range(9, len(inward))):
        inward[n].start()

    def lane_place(rows, dim):
        lane = lax.broadcasted_iota(jnp.int32, (rows, 128), 1)
        return (lane // STRIDES[dim]) % COUNTS[dim]

    def gather_faces(source_ref, offset, rows, whole, target):
        sub = lax.broadcasted_iota(jnp.int32, (8, 128), 0)

        def one(f, _):
            top = offset + f * rows
            last = source_ref[slice(top + whole, top + whole + 8), lanes(0)]
            for v in range(5):
                target[f, whole * v : whole * v + whole, :] = source_ref[
                    slice(top, top + whole), lanes(v)
                ]
                if v:
                    here = source_ref[slice(top + whole, top + whole + 8), lanes(v)]
                    last = jnp.where(sub == v, here, last)
            target[f, 5 * whole : 5 * whole + 8, :] = last
            return 0

        steps(6, one, 0)

    def scatter_faces(source_ref, rows, whole, target, add=None):
        def put(here, v, value):
            target[here, lanes(v)] = value if add is None else add[here, lanes(v)] + value

        def one(f, _):
            top = f * rows
            for v in range(5):
                put(slice(top, top + whole), v, source_ref[f, whole * v : whole * v + whole, :])
                last = source_ref[f, 5 * whole + v : 5 * whole + v + 1, :]
                put(slice(top + whole, top + whole + 8), v, jnp.broadcast_to(last, (8, 128)))
            return 0

        steps(6, one, 0)

    def turn(value, amount):
        amount %= 128
        return pltpu.roll(value, amount, 1) if amount else value

    def copies(kind):
        sends, receives = kinds[kind]
        return [
            pltpu.make_async_remote_copy(
                src_ref=sends[f],
                dst_ref=receives[f ^ 1],
                send_sem=send_sems.at[kind, f],
                recv_sem=recv_sems.at[kind, f ^ 1],
                device_id=partner(f),
                device_id_type=MESH,
            )
            for f in range(6)
        ]

    def line_copies(level):
        return [
            pltpu.make_async_remote_copy(
                src_ref=send_lines.at[level, line],
                dst_ref=recv_lines.at[level, line ^ 3],
                send_sem=send_line_sems.at[level, line],
                recv_sem=recv_line_sems.at[level, line ^ 3],
                device_id=line_partner(line),
                device_id_type=MESH,
            )
            for line in range(12)
        ]

    remote = [copies(kind) for kind in range(5)]
    remote_lines = [line_copies(level) for level in range(2)]

    def pack(kind, read, height, top=0, slots=None):
        for f in range(6):
            dim, side = divmod(f, 2)
            count, stride = COUNTS[dim], STRIDES[dim]
            target = kinds[kind][0][f]
            slot = target.shape[0] if slots is None else slots[dim]
            where = lane_place(slot, dim)
            packed = None
            for g in range(height // slot):
                block = turn(read(f, g * slot, slot), (g - side * (count - 1)) * stride)
                packed = block if packed is None else jnp.where(where == g, block, packed)
            first = top if slots is None else top[dim]
            target[first : first + slot, :] = packed

    def pack_lines(level, source_ref, offset):
        for line, (i, j, s, t) in enumerate(LINES):
            where = lane_place(8, j)
            packed = None
            for v in range(5):
                block = source_ref[offset + 8 * line : offset + 8 * line + 8, lanes(v)]
                block = turn(block, (v - t * (COUNTS[j] - 1)) * STRIDES[j])
                packed = block if packed is None else jnp.where(where == v, block, packed)
            send_lines[level, line] = packed

    def start(kind):
        for f in range(6):
            @pl.when(has[f])
            def _(f=f):
                remote[kind][f].start()

    def start_lines(level):
        for line in range(12):
            @pl.when(both[line])
            def _(line=line):
                remote_lines[level][line].start()

    def unpack(kind, f, height, write, sign=1.0, top=0, slots=None):
        dim, side = divmod(f, 2)
        count, stride = COUNTS[dim], STRIDES[dim]
        received = kinds[kind][1][f]
        slot = received.shape[0] if slots is None else slots[dim]
        first = top if slots is None else top[dim]
        edge = jnp.where(lane_place(slot, dim) == side * (count - 1), sign, 0.0)

        @pl.when(has[f])
        def _():
            packed = received[first : first + slot, :]
            for g in range(height // slot):
                write(f, g * slot, slot, edge * turn(packed, (side * (count - 1) - g) * stride))

        @pl.when(jnp.logical_not(has[f]))
        def _():
            write(f, 0, height, jnp.zeros((height, 128), F32))

    def arrive(kind, f):
        @pl.when(has[f])
        def _():
            remote[kind][f ^ 1].wait_recv()

    def receive(kind, target, sign):
        def write(f, first, slot, value):
            target[f, first : first + slot, :] = value

        for f in range(6):
            arrive(kind, f)
            unpack(kind, f, target.shape[1], write, sign)

    def receive_lines(level, target):
        for line, (i, j, s, t) in enumerate(LINES):
            edge = (lane_place(8, i) == s * (COUNTS[i] - 1)) & (lane_place(8, j) == t * (COUNTS[j] - 1))
            here = slice(8 * line, 8 * line + 8)

            @pl.when(both[line])
            def _():
                remote_lines[level][line ^ 3].wait_recv()
                packed = recv_lines[level, line]
                for v in range(5):
                    amount = (t * (COUNTS[j] - 1) - v) * STRIDES[j] + (2 * s - 1) * (COUNTS[i] - 1) * STRIDES[i]
                    target[here, lanes(v)] = jnp.where(edge, turn(packed, amount), 0.0)

            @pl.when(jnp.logical_not(both[line]))
            def _():
                target[here, :] = jnp.zeros((8, 640), F32)

    def own_part(faces, result):
        for f in range(6):
            dim, side = divmod(f, 2)
            count, stride = COUNTS[dim], STRIDES[dim]
            inside = lane_place(faces.shape[1], dim) != side * (count - 1)
            other = turn(faces[f ^ 1], -stride if side else stride)
            result[f] = faces[f] - jnp.where(inside, other, 0.0)

    def face_pull(step, values, state_ref, offset, per_face):
        d, side = divmod(step // per_face, 2)
        return pull_face(values, load(state_ref, rows_of(step + offset)), d, 2 * side - 1)

    def neighbour(rows, face, mine, offset, near_s, across_ref, sign_ref, target, add):
        per_face = rows // 16
        for d in range(3):
            p, q = [n for n in range(3) if n != d]

            def one(step, _, d=d, p=p, q=q):
                side = step // per_face
                f = 2 * d + side
                at = step + 2 * d * per_face
                here = rows_of(at)
                local = load(near_s, here)
                top = [jnp.abs(local[n]) + local[4] for n in range(3)]
                edge = edges[f]
                own_side = load(mine, rows_of(at + offset))
                jumps = [None] * 3
                jumps[d] = [-edge * value for value in own_side]
                jumps[p] = load(across_ref, here)
                jumps[q] = load(across_ref, rows_of(at + 6 * per_face))
                part = rows_of(step - side * per_face)
                sign = [None] * 3
                sign[d] = 1.0 - 2.0 * side
                sign[p], sign[q] = sign_ref[0, part, :], sign_ref[1, part, :]
                pulled = pull_all([[sign[n] * value for value in jumps[n]] for n in range(3)], local)
                for n in range(3):
                    pulled = [pulled[v] + top[n] * jumps[n][v] for v in range(5)]
                inverse = [near_blocks[f, n : n + 1, :] for n in range(25)]
                change = apply_blocks(inverse, pulled)
                change = [face * value for value in change]
                if add:
                    change = [old + value for old, value in zip(load(target, here), change)]
                store(target, here, change)
                return 0

            steps(2 * per_face, one, 0)

    def block_rows():
        return [blocks[n] for n in range(25)]

    for f in range(6):
        dim, side = divmod(f, 2)
        edges[f] = (lane_place(16, dim) == side * (COUNTS[dim] - 1)).astype(F32)
    for ref, rows, count in ((signs, 32, 5), (signs_c, 16, 3)):
        row = jnp.minimum(lax.broadcasted_iota(jnp.int32, (rows, 128), 0), count * count - 1)
        for n, at in enumerate((row // count, row % count)):
            ref[n] = jnp.where(at == 0, -1.0, jnp.where(at == count - 1, 1.0, 0.0))
    block_row[...] = jnp.zeros((32, 128), F32)
    inward[0].wait()
    for v in range(5):
        field[0:125, lanes(v)] = start_r[v]

    def split_field(step, _):
        store_split(split_n, step, 128, load(field, rows_of(step)), 3)
        return 0

    steps(8, split_field, 0)
    inward[1].wait()
    start_face[...] = dot(take[0:192, :], split_n[0:256, :])
    line_field[...] = dot(take[192:288, :], split_n[0:256, :])
    gather_faces(start_face, 0, 32, 24, compact)
    pack(0, lambda f, first, slot: compact[f, first : first + slot, :], 128)
    pack_lines(0, line_field, 0)
    own_part(compact, own)
    scatter_faces(own, 32, 24, jump)

    for n in (2, 3, 4):
        inward[n].wait()
    state[120:128, :] = jnp.zeros((8, 640), F32)
    for part in ((0, 64), (64, 125)):
        here = slice(*part)
        w = [velocity_r[d, here, :] for d in range(3)]
        sound_2 = 1.4 * pressure_r[here, :] / density_r[here, :]
        for d in range(3):
            state[here, lanes(d)] = w[d]
        state[here, lanes(3)] = 2.5 * sound_2 + 0.5 * (w[0] * w[0] + w[1] * w[1] + w[2] * w[2])
        state[here, lanes(4)] = jnp.sqrt(sound_2)

    def split_state(step, _):
        store_split(split_f, step, 128, load(state, rows_of(step)), 2)
        return 0

    steps(8, split_state, 0)
    face_state[...] = dot(take[0:192, :], split_f[0:256, :])
    state_c[0:32, :] = dot(take[288:320, :], split_f[0:256, :])

    for n in (7, 8):
        inward[n].wait()
    spread = (
        lax.broadcasted_iota(jnp.int32, (8, 128), 1) % 8 == lax.broadcasted_iota(jnp.int32, (8, 128), 0)
    ).astype(F32)

    def to_lanes(value, count):
        wide = jnp.dot(
            value.reshape(16 * count, 8), spread,
            precision=lax.Precision.HIGHEST, preferred_element_type=F32,
        ).reshape(count, 16, 128)
        row = lax.broadcasted_iota(jnp.int32, (count, 16, 128), 1)
        lane = lax.broadcasted_iota(jnp.int32, (count, 16, 128), 2)
        kept = jnp.where(lane // 8 == row, wide, 0.0)
        return jnp.broadcast_to(jnp.sum(kept, axis=1, keepdims=True), (count, 16, 128))

    shift[...] = to_lanes(shift_r[...], 1)[0]
    blocks[...] = OMEGA * to_lanes(inverse_r[...], 25)

    for n in range(25):
        block_row[n : n + 1, :] = blocks[n, 0:1, :]
    gather_faces(face_state, 0, 32, 24, compact)
    slots, tops = (64, 16, 16), (0, 0, 0)
    pack(1, lambda f, first, slot: compact[f, first : first + slot, :], 128, tops, slots)
    block_slots, block_tops = (16, 8, 8), (64, 16, 16)
    pack(1, lambda f, first, slot: block_row[first : first + slot, :], 32, block_tops, block_slots)

    pl.semaphore_wait(barrier, sum(h.astype(jnp.int32) for h in has + both))
    start(0)
    start(1)
    start_lines(0)

    inward[5].wait()
    inward[6].wait()
    for v in range(5):
        source[0:125, lanes(v)] = source_r[v]

    def residual(step, height, cot_ref, values, right, state_ref):
        rows = rows_of(step)
        cots = [load(cot_ref, rows_of(step + d * (height // 16))) for d in range(3)]
        pulled = pull_all(cots, load(state_ref, rows))
        return [right[v] - shift[...] * values[v] - pulled[v] for v in range(5)]

    def smooth_volume(step, _, keep_split):
        rows = rows_of(step)
        values = load(field, rows)
        resid = residual(step, 128, cot, values, load(source, rows), state)
        change = apply_blocks(block_rows(), resid)
        values = [values[v] + change[v] for v in range(5)]
        store(base, rows, values)
        if keep_split:
            store_split(split_n, step, 128, values, 2)
        return 0

    cot[...] = dot(volume[...], split_n[...])
    steps(8, lambda s, c: smooth_volume(s, c, True), 0)
    face_field[...] = dot(take[0:192, :], split_n[0:256, :])

    def smooth_faces(step, _):
        values = face_pull(step, load(jump, rows_of(step)), face_state, 0, 2)
        store_split(split_f, step, 192, apply_blocks(block_rows(), values), 2)
        return 0

    steps(12, smooth_faces, 0)
    inward[9].wait()
    face_field[...] += dot(give[0:192, :], split_f[0:384, :])
    gather_faces(face_field, 0, 32, 24, compact)
    pack(2, lambda f, first, slot: compact[f, first : first + slot, :], 128)
    start(2)
    base[...] += dot(give[192:320, :], split_f[0:384, :])
    for n in range(10, 20):
        inward[n].wait()

    def split_faces(step, ref):
        store_split(split_f, step, 192, load(ref, rows_of(step)), 2)

    def split_face_state(step, _):
        split_faces(step, face_state)
        return 0

    steps(12, split_face_state, 0)
    state_c[32:128, :] = dot(pick_face[...], split_f[0:384, :])

    receive(0, compact, -1.0)
    scatter_faces(compact, 32, 24, jump)
    steps(12, smooth_faces, 0)
    face_field[...] += dot(give[0:192, :], split_f[0:384, :])
    field[...] = base[...] + dot(give[192:320, :], split_f[0:384, :])
    gather_faces(face_field, 0, 32, 24, compact)
    own_part(compact, own)
    scatter_faces(own, 32, 24, jump)
    steps(8, split_field, 0)
    cot[...] = dot(volume[...], split_n[...])

    def residual_volume(step, _):
        rows = rows_of(step)
        resid = residual(step, 128, cot, load(field, rows), load(source, rows), state)
        store_split(split_n, step, 128, resid, 3)
        return 0

    steps(8, residual_volume, 0)
    field_c[...] = dot(restrict[...], split_n[...])

    def write_state(f, first, slot, value):
        compact[f, first : first + slot, :] = value

    def write_blocks(f, first, slot, value):
        near_blocks[f, first : first + slot, :] = value

    for f in range(6):
        arrive(1, f)
        unpack(1, f, 128, write_state, 1.0, tops, slots)
        unpack(1, f, 32, write_blocks, 1.0, block_tops, block_slots)
    scatter_faces(compact, 32, 24, near_state)
    receive_lines(0, line_field)

    def split_lines(step, _):
        store_split(split_l, step, 96, load(line_field, rows_of(step)), 2)
        return 0

    steps(6, split_lines, 0)
    across[...] = dot(lines[...], split_l[...])
    neighbour(32, FINE_FACE, start_face, 0, near_state, across, signs, jump, True)
    receive(2, compact, -1.0)
    scatter_faces(compact, 32, 24, jump, jump)

    def residual_faces(step, _):
        values = face_pull(step, load(jump, rows_of(step)), face_state, 0, 2)
        store_split(split_f, step, 192, values, 3)
        return 0

    steps(12, residual_faces, 0)
    field_c[...] += dot(restrict_give[...], split_f[...])

    def coarse_first(step, _):
        rows = rows_of(step)
        store(base_c, rows, apply_blocks(block_rows(), load(field_c, rows)))
        return 0

    steps(14, coarse_first, 0)
    gather_faces(base_c, 32, 16, 8, compact_c)
    pack(3, lambda f, first, slot: compact_c[f, first : first + slot, :], 48)
    start(3)
    pack_lines(1, base_c, 128)
    start_lines(1)
    own_part(compact_c, own_c)
    scatter_faces(own_c, 16, 8, jump_c)

    def split_coarse(step, _):
        store_split(split_c, step, 32, load(base_c, rows_of(step)), 2)
        return 0

    steps(2, split_coarse, 0)
    cot_c[...] = dot(volume_c[0:96, :], split_c[0:64, :])

    def coarse_volume(step, _):
        rows = rows_of(step)
        values = load(base_c, rows)
        resid = residual(step, 32, cot_c, values, load(field_c, rows), state_c)
        change = apply_blocks(block_rows(), resid)
        values = [values[v] + change[v] for v in range(5)]
        store(field_c, rows, values)
        store_split(split_c, step, 32, values, 2)
        return 0

    steps(2, coarse_volume, 0)
    face_c[...] = dot(volume_c[96:192, :], split_c[0:64, :])

    def coarse_faces(step, _):
        values = face_pull(step, load(jump_c, rows_of(step)), state_c, 2, 1)
        store_split(split_cf, step, 96, apply_blocks(block_rows(), values), 2)
        return 0

    steps(6, coarse_faces, 0)
    face_c[...] += dot(give_c[0:96, :], split_cf[0:192, :])
    gather_faces(face_c, 0, 16, 8, compact_c)
    pack(4, lambda f, first, slot: compact_c[f, first : first + slot, :], 48)
    start(4)
    field_c[0:32, :] += dot(give_c[96:128, :], split_cf[0:192, :])

    def split_near(step, _):
        split_faces(step, near_state)
        return 0

    steps(12, split_near, 0)
    near_state_c[...] = dot(pick_face[...], split_f[0:384, :])

    def split_coarse_3(step, _):
        store_split(split_c, step, 32, load(field_c, rows_of(step)), 3)
        return 0

    steps(2, split_coarse_3, 0)
    field[...] += dot(extend[...], split_c[...])
    steps(8, split_field, 0)
    cot[...] = dot(volume[...], split_n[...])
    receive_lines(1, line_field)
    steps(6, split_lines, 0)
    across_c[...] = dot(lines_c[...], split_l[...])
    neighbour(16, COARSE_FACE, base_c, 2, near_state_c, across_c, signs_c, near_c, False)

    def coarse_rest(step, _):
        values = face_pull(step, load(jump_c, rows_of(step)), state_c, 2, 1)
        store_split(split_cf, step, 96, apply_blocks(block_rows(), values), 3)
        return 0

    receive(3, compact_c, -1.0)
    scatter_faces(compact_c, 16, 8, jump_c)
    steps(6, coarse_rest, 0)
    face_c[...] += dot(chain[0:96, :], split_cf[...])
    gather_faces(face_c, 0, 16, 8, compact_c)
    own_part(compact_c, own_c)
    scatter_faces(own_c, 16, 8, jump_c, near_c)
    field[...] += dot(chain[96:224, :], split_cf[...])
    cot[...] += dot(chain[224:608, :], split_cf[...])
    steps(8, lambda s, c: smooth_volume(s, c, False), 0)
    receive(4, compact_c, -1.0)
    scatter_faces(compact_c, 16, 8, jump_c, jump_c)

    def split_jump(step, _):
        store_split(split_cf, step, 96, load(jump_c, rows_of(step)), 3)
        return 0

    steps(6, split_jump, 0)
    jump[...] += dot(face_extend[...], split_cf[...])
    steps(12, smooth_faces, 0)
    base[...] += dot(give[192:320, :], split_f[0:384, :])
    for v in range(5):
        out_h[v] = base[0:125, lanes(v)]
    for kind in range(5):
        for f in range(6):
            @pl.when(has[f])
            def _(kind=kind, f=f):
                remote[kind][f].wait_send()
    for level in range(2):
        for line in range(12):
            @pl.when(both[line])
            def _(level=level, line=line):
                remote_lines[level][line].wait_send()


def body(*args):
    constants = [jnp.asarray(table) for table in tables().values()]
    vmem = pltpu.VMEM
    raw = [vmem(a.shape, a.dtype) for a in args]
    held = [vmem(t.shape, t.dtype) for t in constants]
    work = [
        vmem((128, 640), F32), vmem((128, 640), F32), vmem((128, 640), F32), vmem((128, 640), F32),
        vmem((384, 640), BF16), vmem((384, 640), F32),
        vmem((192, 640), F32), vmem((192, 640), F32), vmem((192, 640), F32), vmem((192, 640), F32),
        vmem((576, 640), BF16), vmem((6, 128, 128), F32), vmem((6, 128, 128), F32),
        vmem((192, 640), F32), vmem((384, 640), F32), vmem((96, 640), F32),
        vmem((192, 640), BF16), vmem((6, 32, 128), F32), vmem((32, 128), F32), vmem((6, 16, 128), F32),
        vmem((2, 32, 128), F32), vmem((2, 16, 128), F32),
        vmem((128, 640), F32), vmem((224, 640), F32), vmem((224, 640), F32), vmem((96, 640), BF16),
        vmem((288, 640), BF16), vmem((96, 640), F32), vmem((96, 640), F32),
        vmem((6, 48, 128), F32), vmem((6, 48, 128), F32),
        vmem((96, 640), F32), vmem((96, 640), F32), vmem((192, 640), F32), vmem((96, 640), F32),
        vmem((25, 16, 128), F32), vmem((16, 128), F32),
    ]
    fine = [vmem((rows, 128), F32) for rows in (64, 64, 16, 16, 16, 16)]
    static = [vmem((rows, 128), F32) for rows in (80, 80, 24, 24, 24, 24)]
    coarse = [vmem((rows, 128), F32) for rows in (24, 24, 8, 8, 8, 8)]
    kinds = [*fine, *fine, *static, *static, *fine, *fine, *coarse, *coarse, *coarse, *coarse]
    sems = [
        pltpu.SemaphoreType.DMA((20,)),
        pltpu.SemaphoreType.DMA((5, 6)),
        pltpu.SemaphoreType.DMA((5, 6)),
        pltpu.SemaphoreType.DMA((2, 12)),
        pltpu.SemaphoreType.DMA((2, 12)),
    ]
    anywhere = pl.BlockSpec(memory_space=pl.ANY)
    return pl.pallas_call(
        kernel,
        out_shape=pltpu.VMEM(args[0].shape, F32),
        in_specs=[anywhere] * (len(args) + len(constants)),
        out_specs=pl.BlockSpec(memory_space=pltpu.VMEM),
        scratch_shapes=raw + held + work + kinds + [vmem((2, 12, 8, 128), F32)] * 2 + sems,
        compiler_params=pltpu.CompilerParams(
            collective_id=0, has_side_effects=True, vmem_limit_bytes=60 * 1024 * 1024
        ),
    )(*args, *constants)


def solution(mesh):
    in_specs = (
        P(None, None, AXES),
        P(None, None, AXES),
        P(None, AXES),
        P(None, None, AXES),
        P(None, AXES),
        P(*AXES),
        P(None, None, *AXES),
    )
    return jax.shard_map(
        body, mesh=mesh, in_specs=in_specs, out_specs=P(None, None, AXES), check_vma=False
    )
```

```python
import itertools

import jax
import jax.numpy as jnp
import ml_dtypes
import numpy as np
from jax import lax
from jax.experimental import pallas as pl
from jax.experimental.pallas import tpu as pltpu
from jax.sharding import PartitionSpec as P

OMEGA = 0.7
METRIC = 0.25
FINE_FACE = 0.5 * 0.25 / 0.1
COARSE_FACE = 0.5 * 0.25 * 3.0
MESH = pl.DeviceIdType.MESH
AXES = ("gx", "gy", "gz")
COUNTS = (2, 8, 8)
STRIDES = (64, 8, 1)
LINES = [(i, j, s, t) for i, j in ((0, 1), (0, 2), (1, 2)) for s in range(2) for t in range(2)]
F32 = jnp.float32
BF16 = jnp.bfloat16


def diff_table(nodes):
    count = len(nodes)
    weights = np.array(
        [1.0 / np.prod([nodes[j] - nodes[k] for k in range(count) if k != j]) for j in range(count)]
    )
    table = np.zeros((count, count))
    for i in range(count):
        for j in range(count):
            if i != j:
                table[i, j] = weights[j] / weights[i] / (nodes[i] - nodes[j])
        table[i, i] = -np.sum(table[i])
    return table.astype(np.float32).astype(np.float64)


def fine_points():
    return np.array([-1.0, -np.sqrt(3.0 / 7.0), 0.0, np.sqrt(3.0 / 7.0), 1.0])


def interp_table():
    points = fine_points()
    table = np.stack(
        [points * (points - 1.0) / 2.0, 1.0 - points**2, points * (points + 1.0) / 2.0], axis=1
    )
    return table.astype(np.float32).astype(np.float64)


def triple(a, b, c):
    return np.kron(np.kron(a, b), c)


def padded(matrix, rows, columns):
    result = np.zeros((rows, columns))
    result[: matrix.shape[0], : matrix.shape[1]] = matrix
    return result


def face_tables(count, rows, width):
    take = np.zeros((6 * rows, width))
    give = np.zeros((width, 6 * rows))
    for dim in range(3):
        for side in range(2):
            face = 2 * dim + side
            for row in range(rows):
                a, b = divmod(min(row, count * count - 1), count)
                place = [a, b]
                place.insert(dim, side * (count - 1))
                node = (place[0] * count + place[1]) * count + place[2]
                take[face * rows + row, node] = 1.0
                if row < count * count:
                    give[node, face * rows + row] = 1.0
    return take, give


def line_table(count, width):
    take = np.zeros((96, width))
    for line, (i, j, s, t) in enumerate(LINES):
        for node in range(count):
            place = [node] * 3
            place[i], place[j] = s * (count - 1), t * (count - 1)
            take[8 * line + node, (place[0] * count + place[1]) * count + place[2]] = 1.0
    return take


def line_faces(count, rows):
    result = np.zeros((2, 6 * rows, 96))
    for dim in range(3):
        for side in range(2):
            for row in range(rows):
                pair = divmod(min(row, count * count - 1), count)
                others = [d for d in range(3) if d != dim]
                for n in range(2):
                    if pair[n] % (count - 1) == 0:
                        sides = {dim: side, others[n]: pair[n] // (count - 1)}
                        i, j = sorted(sides)
                        line = LINES.index((i, j, sides[i], sides[j]))
                        result[n, (2 * dim + side) * rows + row, 8 * line + pair[1 - n]] = -1.0
    return result.reshape(12 * rows, 96)


def volume_table(count, width):
    table = diff_table(fine_points() if count == 5 else np.array([-1.0, 0.0, 1.0]))
    unit = np.eye(count)
    parts = []
    for dim in range(3):
        mats = [unit, unit, unit]
        mats[dim] = -METRIC * table.T
        parts.append(padded(triple(*mats), width, width))
    return np.concatenate(parts)


def two(matrix):
    high = matrix.astype(ml_dtypes.bfloat16)
    return np.concatenate([high, high], axis=1)


def three(matrix):
    high = matrix.astype(ml_dtypes.bfloat16)
    low = (matrix - high.astype(np.float64)).astype(ml_dtypes.bfloat16)
    return np.concatenate([high, high, low], axis=1)


def tables():
    prolong = interp_table()
    take, give = face_tables(5, 32, 128)
    take_c, give_c = face_tables(3, 16, 32)
    pick = np.zeros((32, 128))
    for n, (a, b, c) in enumerate(itertools.product(range(3), repeat=3)):
        pick[n, (2 * a * 5 + 2 * b) * 5 + 2 * c] = 1.0
    restrict = padded(triple(prolong.T, prolong.T, prolong.T), 32, 128)
    restrict = np.concatenate([restrict, take_c @ restrict, line_table(3, 32) @ restrict])
    extend = padded(triple(prolong, prolong, prolong), 128, 32)
    flat = np.kron(prolong, prolong)
    flat = np.concatenate([flat, np.repeat(flat[24:25], 7, axis=0)])
    face_extend = np.zeros((192, 96))
    for face in range(6):
        face_extend[32 * face : 32 * face + 32, 16 * face : 16 * face + 9] = flat
    correct = -COARSE_FACE * give_c
    face_pick = np.zeros((96, 192))
    for face in range(6):
        for row in range(16):
            a, b = divmod(min(row, 8), 3)
            face_pick[16 * face + row, 32 * face + 10 * a + 2 * b] = 1.0
    return {
        "take": two(np.concatenate([take, line_table(5, 128), pick])),
        "volume": three(volume_table(5, 128)),
        "give": two(-FINE_FACE * np.concatenate([take @ give, give])),
        "restrict": three(restrict),
        "restrict_give": three(-FINE_FACE * restrict @ give),
        "volume_c": two(np.concatenate([volume_table(3, 32), take_c])),
        "give_c": two(-COARSE_FACE * np.concatenate([take_c @ give_c, give_c])),
        "extend": three(extend),
        "face_extend": three(face_extend),
        "chain": three(np.concatenate([take_c @ correct, extend @ correct, volume_table(5, 128) @ extend @ correct])),
        "lines": two(line_faces(5, 32)),
        "lines_c": two(line_faces(3, 16)),
        "pick_face": two(face_pick),
    }


def dot(matrix, field):
    return jnp.dot(matrix, field, preferred_element_type=F32)


def split(value):
    high = value.astype(BF16)
    low = (value - high.astype(F32)).astype(BF16)
    return high, low


def lanes(var):
    return slice(128 * var, 128 * var + 128)


def steps(count, one, carry):
    for step in range(count):
        one(step, carry)


def rows_of(step, size=16):
    return slice(step * size, step * size + size)


def load(ref, rows):
    return [ref[rows, lanes(v)] for v in range(5)]


def store(ref, rows, values):
    for v in range(5):
        ref[rows, lanes(v)] = values[v]


def store_split(ref, step, height, values, pieces):
    for v in range(5):
        parts = split(values[v])
        for piece in range(pieces):
            ref[rows_of(step + piece * (height // 16)), lanes(v)] = parts[piece % 2]


def pull_all(cot, state):
    w = state[:3]
    enthalpy = state[3]
    crossed = [w[0] * c[1] + w[1] * c[2] + w[2] * c[3] + enthalpy * c[4] for c in cot]
    ends = [w[d] * cot[d][4] for d in range(3)]
    energy = ends[0] + ends[1] + ends[2]
    total = 0.4 * (cot[0][1] + cot[1][2] + cot[2][3] + energy)
    half_square = 0.5 * (w[0] * w[0] + w[1] * w[1] + w[2] * w[2])
    first = half_square * total - (w[0] * crossed[0] + w[1] * crossed[1] + w[2] * crossed[2])
    middle = []
    for j in range(3):
        drift = w[0] * cot[0][1 + j] + w[1] * cot[1][1 + j] + w[2] * cot[2][1 + j]
        middle.append(drift + cot[j][0] + crossed[j] - w[j] * total)
    return [first, *middle, total + energy]


def pull_face(jump, state, d, sign):
    w = state[:3]
    crossed = w[0] * jump[1] + w[1] * jump[2] + w[2] * jump[3] + state[3] * jump[4]
    end = w[d] * jump[4]
    total = 0.4 * (jump[1 + d] + end)
    half_square = 0.5 * (w[0] * w[0] + w[1] * w[1] + w[2] * w[2])
    out = [half_square * total - w[d] * crossed]
    for j in range(3):
        out.append(w[d] * jump[1 + j] - w[j] * total)
    out[1 + d] = out[1 + d] + (jump[0] + crossed)
    out.append(total + end)
    top = jnp.abs(w[d]) + state[4]
    if sign > 0:
        return [top * jump[v] + out[v] for v in range(5)]
    return [top * jump[v] - out[v] for v in range(5)]


def apply_blocks(blocks, values):
    result = []
    for a in range(5):
        total = blocks[a] * values[0]
        for b in range(1, 5):
            total = total + blocks[b * 5 + a] * values[b]
        result.append(total)
    return result


def kernel(start_h, source_h, density_h, velocity_h, pressure_h, shift_h, inverse_h, *rest):
    tables_h, rest = rest[:13], rest[13:]
    out_h, rest = rest[0], rest[1:]
    (start_r, source_r, density_r, velocity_r, pressure_r, shift_r, inverse_r), rest = rest[:7], rest[7:]
    tables_r, rest = rest[:13], rest[13:]
    (
        take, volume, give, restrict, restrict_give, volume_c, give_c, extend, face_extend,
        chain, lines, lines_c, pick_face,
    ) = tables_r
    (
        field, source, state, base, split_n, cot,
        face_state, start_face, face_field, jump, split_f, compact, own,
        near_state, across, line_field, split_l, near_blocks, block_row, edges, signs, signs_c,
        state_c, field_c, base_c, split_c, split_cf, cot_c, jump_c, compact_c, own_c,
        near_state_c, near_c, across_c, face_c,
        blocks, shift,
    ), rest = rest[:37], rest[37:]
    kinds = []
    for _ in range(5):
        kinds.append((rest[:6], rest[6:12]))
        rest = rest[12:]
    fine_u, fine_t, fine_w, coarse_u, coarse_w = kinds
    send_lines, recv_lines, in_sems, send_sems, recv_sems, send_line_sems, recv_line_sems = rest

    place = [lax.axis_index(axis) for axis in AXES]
    size = [lax.axis_size(axis) for axis in AXES]
    has = [place[f // 2] > 0 if f % 2 == 0 else place[f // 2] < size[f // 2] - 1 for f in range(6)]

    def partner(f):
        target = list(place)
        target[f // 2] = target[f // 2] + (1 if f % 2 else -1)
        return tuple(target)

    both = [has[2 * i + s] & has[2 * j + t] for i, j, s, t in LINES]

    def line_partner(line):
        i, j, s, t = LINES[line]
        target = list(place)
        target[i] = target[i] + 2 * s - 1
        target[j] = target[j] + 2 * t - 1
        return tuple(target)

    barrier = pltpu.get_barrier_semaphore()
    for f in range(6):
        @pl.when(has[f])
        def _(f=f):
            pl.semaphore_signal(barrier, inc=1, device_id=partner(f), device_id_type=MESH)
    for line in range(12):
        @pl.when(both[line])
        def _(line=line):
            pl.semaphore_signal(barrier, inc=1, device_id=line_partner(line), device_id_type=MESH)

    field[120:128, :] = jnp.zeros((8, 640), F32)
    source[120:128, :] = jnp.zeros((8, 640), F32)
    order = [
        (start_h, start_r), (tables_h[0], take), (velocity_h, velocity_r), (density_h, density_r),
        (pressure_h, pressure_r), (tables_h[1], volume), (source_h, source_r), (shift_h, shift_r),
        (inverse_h, inverse_r), (tables_h[2], give),
    ] + [(tables_h[n], tables_r[n]) for n in range(3, 13)]
    inward = [pltpu.make_async_copy(a, b, in_sems.at[n]) for n, (a, b) in enumerate(order)]
    for n in (0, 1, 2, 3, 4, 8, 7, 5, 6, *range(9, len(inward))):
        inward[n].start()

    def lane_place(rows, dim):
        lane = lax.broadcasted_iota(jnp.int32, (rows, 128), 1)
        return (lane // STRIDES[dim]) % COUNTS[dim]

    def gather_faces(source_ref, offset, rows, whole, target):
        sub = lax.broadcasted_iota(jnp.int32, (8, 128), 0)

        def one(f, _):
            top = offset + f * rows
            last = source_ref[slice(top + whole, top + whole + 8), lanes(0)]
            for v in range(5):
                target[f, whole * v : whole * v + whole, :] = source_ref[
                    slice(top, top + whole), lanes(v)
                ]
                if v:
                    here = source_ref[slice(top + whole, top + whole + 8), lanes(v)]
                    last = jnp.where(sub == v, here, last)
            target[f, 5 * whole : 5 * whole + 8, :] = last
            return 0

        steps(6, one, 0)

    def scatter_faces(source_ref, rows, whole, target, add=None, faces=range(6)):
        def put(here, v, value):
            target[here, lanes(v)] = value if add is None else add[here, lanes(v)] + value

        def one(f, _):
            top = f * rows
            for v in range(5):
                put(slice(top, top + whole), v, source_ref[f, whole * v : whole * v + whole, :])
                last = source_ref[f, 5 * whole + v : 5 * whole + v + 1, :]
                put(slice(top + whole, top + whole + 8), v, jnp.broadcast_to(last, (8, 128)))
            return 0

        for f in faces:
            one(f, 0)

    def turn(value, amount):
        amount %= 128
        return pltpu.roll(value, amount, 1) if amount else value

    def copies(kind):
        sends, receives = kinds[kind]
        return [
            pltpu.make_async_remote_copy(
                src_ref=sends[f],
                dst_ref=receives[f ^ 1],
                send_sem=send_sems.at[kind, f],
                recv_sem=recv_sems.at[kind, f ^ 1],
                device_id=partner(f),
                device_id_type=MESH,
            )
            for f in range(6)
        ]

    def line_copies(level):
        return [
            pltpu.make_async_remote_copy(
                src_ref=send_lines.at[level, line],
                dst_ref=recv_lines.at[level, line ^ 3],
                send_sem=send_line_sems.at[level, line],
                recv_sem=recv_line_sems.at[level, line ^ 3],
                device_id=line_partner(line),
                device_id_type=MESH,
            )
            for line in range(12)
        ]

    remote = [copies(kind) for kind in range(5)]
    remote_lines = [line_copies(level) for level in range(2)]

    def pack(kind, read, height, top=0, slots=None, faces=range(6)):
        for f in faces:
            dim, side = divmod(f, 2)
            count, stride = COUNTS[dim], STRIDES[dim]
            target = kinds[kind][0][f]
            slot = target.shape[0] if slots is None else slots[dim]
            where = lane_place(slot, dim)
            packed = None
            for g in range(height // slot):
                block = turn(read(f, g * slot, slot), (g - side * (count - 1)) * stride)
                packed = block if packed is None else jnp.where(where == g, block, packed)
            first = top if slots is None else top[dim]
            target[first : first + slot, :] = packed

    def pack_lines(level, source_ref, offset):
        for line, (i, j, s, t) in enumerate(LINES):
            where = lane_place(8, j)
            packed = None
            for v in range(5):
                block = source_ref[offset + 8 * line : offset + 8 * line + 8, lanes(v)]
                block = turn(block, (v - t * (COUNTS[j] - 1)) * STRIDES[j])
                packed = block if packed is None else jnp.where(where == v, block, packed)
            send_lines[level, line] = packed

    def start(kind, faces=range(6)):
        for f in faces:
            @pl.when(has[f])
            def _(f=f):
                remote[kind][f].start()

    def start_lines(level):
        for line in range(12):
            @pl.when(both[line])
            def _(line=line):
                remote_lines[level][line].start()

    def unpack(kind, f, height, write, sign=1.0, top=0, slots=None):
        dim, side = divmod(f, 2)
        count, stride = COUNTS[dim], STRIDES[dim]
        received = kinds[kind][1][f]
        slot = received.shape[0] if slots is None else slots[dim]
        first = top if slots is None else top[dim]
        edge = jnp.where(lane_place(slot, dim) == side * (count - 1), sign, 0.0)

        @pl.when(has[f])
        def _():
            packed = received[first : first + slot, :]
            for g in range(height // slot):
                write(f, g * slot, slot, edge * turn(packed, (side * (count - 1) - g) * stride))

        @pl.when(jnp.logical_not(has[f]))
        def _():
            write(f, 0, height, jnp.zeros((height, 128), F32))

    def arrive(kind, f):
        @pl.when(has[f])
        def _():
            remote[kind][f ^ 1].wait_recv()

    def receive(kind, target, sign):
        def write(f, first, slot, value):
            target[f, first : first + slot, :] = value

        for f in range(6):
            arrive(kind, f)
            unpack(kind, f, target.shape[1], write, sign)

    def receive_lines(level, target):
        for line, (i, j, s, t) in enumerate(LINES):
            edge = (lane_place(8, i) == s * (COUNTS[i] - 1)) & (lane_place(8, j) == t * (COUNTS[j] - 1))
            here = slice(8 * line, 8 * line + 8)

            @pl.when(both[line])
            def _():
                remote_lines[level][line ^ 3].wait_recv()
                packed = recv_lines[level, line]
                for v in range(5):
                    amount = (t * (COUNTS[j] - 1) - v) * STRIDES[j] + (2 * s - 1) * (COUNTS[i] - 1) * STRIDES[i]
                    target[here, lanes(v)] = jnp.where(edge, turn(packed, amount), 0.0)

            @pl.when(jnp.logical_not(both[line]))
            def _():
                target[here, :] = jnp.zeros((8, 640), F32)

    def own_part(faces, result):
        for f in range(6):
            dim, side = divmod(f, 2)
            count, stride = COUNTS[dim], STRIDES[dim]
            inside = lane_place(faces.shape[1], dim) != side * (count - 1)
            other = turn(faces[f ^ 1], -stride if side else stride)
            result[f] = faces[f] - jnp.where(inside, other, 0.0)

    def face_pull(step, values, state_ref, offset, per_face):
        d, side = divmod(step // per_face, 2)
        return pull_face(values, load(state_ref, rows_of(step + offset)), d, 2 * side - 1)

    def neighbour(rows, face, mine, offset, near_s, across_ref, sign_ref, target, add, dims):
        per_face = rows // 16
        for d in dims:
            p, q = [n for n in range(3) if n != d]

            def one(step, _, d=d, p=p, q=q):
                side = step // per_face
                f = 2 * d + side
                at = step + 2 * d * per_face
                here = rows_of(at)
                local = load(near_s, here)
                top = [jnp.abs(local[n]) + local[4] for n in range(3)]
                edge = edges[f]
                own_side = load(mine, rows_of(at + offset))
                jumps = [None] * 3
                jumps[d] = [-edge * value for value in own_side]
                jumps[p] = load(across_ref, here)
                jumps[q] = load(across_ref, rows_of(at + 6 * per_face))
                part = rows_of(step - side * per_face)
                sign = [None] * 3
                sign[d] = 1.0 - 2.0 * side
                sign[p], sign[q] = sign_ref[0, part, :], sign_ref[1, part, :]
                pulled = pull_all([[sign[n] * value for value in jumps[n]] for n in range(3)], local)
                for n in range(3):
                    pulled = [pulled[v] + top[n] * jumps[n][v] for v in range(5)]
                inverse = [near_blocks[f, n : n + 1, :] for n in range(25)]
                change = apply_blocks(inverse, pulled)
                change = [face * value for value in change]
                if add:
                    change = [old + value for old, value in zip(load(target, here), change)]
                store(target, here, change)
                return 0

            steps(2 * per_face, one, 0)

    def block_rows():
        return [blocks[n] for n in range(25)]

    for f in range(6):
        dim, side = divmod(f, 2)
        edges[f] = (lane_place(16, dim) == side * (COUNTS[dim] - 1)).astype(F32)
    for ref, rows, count in ((signs, 32, 5), (signs_c, 16, 3)):
        row = jnp.minimum(lax.broadcasted_iota(jnp.int32, (rows, 128), 0), count * count - 1)
        for n, at in enumerate((row // count, row % count)):
            ref[n] = jnp.where(at == 0, -1.0, jnp.where(at == count - 1, 1.0, 0.0))
    block_row[...] = jnp.zeros((32, 128), F32)
    inward[0].wait()
    for v in range(5):
        field[0:125, lanes(v)] = start_r[v]

    def split_field(step, _):
        store_split(split_n, step, 128, load(field, rows_of(step)), 3)
        return 0

    steps(8, split_field, 0)
    inward[1].wait()
    start_face[...] = dot(take[0:192, :], split_n[0:256, :])
    line_field[...] = dot(take[192:288, :], split_n[0:256, :])
    gather_faces(start_face, 0, 32, 24, compact)
    pack(0, lambda f, first, slot: compact[f, first : first + slot, :], 128)
    pack_lines(0, line_field, 0)
    own_part(compact, own)
    scatter_faces(own, 32, 24, jump)

    for n in (2, 3, 4):
        inward[n].wait()
    state[120:128, :] = jnp.zeros((8, 640), F32)
    for part in ((0, 64), (64, 125)):
        here = slice(*part)
        w = [velocity_r[d, here, :] for d in range(3)]
        sound_2 = 1.4 * pressure_r[here, :] / density_r[here, :]
        for d in range(3):
            state[here, lanes(d)] = w[d]
        state[here, lanes(3)] = 2.5 * sound_2 + 0.5 * (w[0] * w[0] + w[1] * w[1] + w[2] * w[2])
        state[here, lanes(4)] = jnp.sqrt(sound_2)

    def split_state(step, _):
        store_split(split_f, step, 128, load(state, rows_of(step)), 2)
        return 0

    steps(8, split_state, 0)
    face_state[...] = dot(take[0:192, :], split_f[0:256, :])
    state_c[0:32, :] = dot(take[288:320, :], split_f[0:256, :])

    for n in (7, 8):
        inward[n].wait()
    spread = (
        lax.broadcasted_iota(jnp.int32, (8, 128), 1) % 8 == lax.broadcasted_iota(jnp.int32, (8, 128), 0)
    ).astype(F32)

    def to_lanes(value, count):
        wide = jnp.dot(
            value.reshape(16 * count, 8), spread,
            precision=lax.Precision.HIGHEST, preferred_element_type=F32,
        ).reshape(count, 16, 128)
        row = lax.broadcasted_iota(jnp.int32, (count, 16, 128), 1)
        lane = lax.broadcasted_iota(jnp.int32, (count, 16, 128), 2)
        kept = jnp.where(lane // 8 == row, wide, 0.0)
        return jnp.broadcast_to(jnp.sum(kept, axis=1, keepdims=True), (count, 16, 128))

    shift[...] = to_lanes(shift_r[...], 1)[0]
    blocks[...] = OMEGA * to_lanes(inverse_r[...], 25)

    for n in range(25):
        block_row[n : n + 1, :] = blocks[n, 0:1, :]
    gather_faces(face_state, 0, 32, 24, compact)
    slots, tops = (64, 16, 16), (0, 0, 0)
    pack(1, lambda f, first, slot: compact[f, first : first + slot, :], 128, tops, slots)
    block_slots, block_tops = (16, 8, 8), (64, 16, 16)
    pack(1, lambda f, first, slot: block_row[first : first + slot, :], 32, block_tops, block_slots)

    pl.semaphore_wait(barrier, sum(h.astype(jnp.int32) for h in has + both))
    start(0)
    start(1, (2, 3, 4, 5))
    start_lines(0)

    inward[5].wait()
    inward[6].wait()
    for v in range(5):
        source[0:125, lanes(v)] = source_r[v]

    def residual(step, height, cot_ref, values, right, state_ref):
        rows = rows_of(step)
        cots = [load(cot_ref, rows_of(step + d * (height // 16))) for d in range(3)]
        pulled = pull_all(cots, load(state_ref, rows))
        return [right[v] - shift[...] * values[v] - pulled[v] for v in range(5)]

    def smooth_volume(step, _, keep_split):
        rows = rows_of(step)
        values = load(field, rows)
        resid = residual(step, 128, cot, values, load(source, rows), state)
        change = apply_blocks(block_rows(), resid)
        values = [values[v] + change[v] for v in range(5)]
        store(base, rows, values)
        if keep_split:
            store_split(split_n, step, 128, values, 2)
        return 0

    cot[...] = dot(volume[...], split_n[...])
    steps(8, lambda s, c: smooth_volume(s, c, True), 0)
    face_field[...] = dot(take[0:192, :], split_n[0:256, :])

    def smooth_faces(step, _):
        values = face_pull(step, load(jump, rows_of(step)), face_state, 0, 2)
        store_split(split_f, step, 192, apply_blocks(block_rows(), values), 2)
        return 0

    steps(12, smooth_faces, 0)
    inward[9].wait()
    face_field[...] += dot(give[0:192, :], split_f[0:384, :])
    gather_faces(face_field, 0, 32, 24, compact)
    pack(2, lambda f, first, slot: compact[f, first : first + slot, :], 128, faces=(2, 3, 4, 5))
    start(2, (2, 3, 4, 5))
    base[...] += dot(give[192:320, :], split_f[0:384, :])
    for n in range(10, 20):
        inward[n].wait()

    def split_faces(step, ref):
        store_split(split_f, step, 192, load(ref, rows_of(step)), 2)

    def split_face_state(step, _):
        split_faces(step, face_state)
        return 0

    steps(12, split_face_state, 0)
    state_c[32:128, :] = dot(pick_face[...], split_f[0:384, :])

    receive(0, compact, -1.0)
    scatter_faces(compact, 32, 24, jump)
    steps(12, smooth_faces, 0)
    face_field[...] += dot(give[0:192, :], split_f[0:384, :])
    gather_faces(face_field, 0, 32, 24, compact)
    pack(2, lambda f, first, slot: compact[f, first : first + slot, :], 128, faces=(0, 1))
    start(2, (0, 1))
    start(1, (0, 1))
    field[...] = base[...] + dot(give[192:320, :], split_f[0:384, :])
    own_part(compact, own)
    scatter_faces(own, 32, 24, jump)
    steps(8, split_field, 0)
    cot[...] = dot(volume[...], split_n[...])

    def residual_volume(step, _):
        rows = rows_of(step)
        resid = residual(step, 128, cot, load(field, rows), load(source, rows), state)
        store_split(split_n, step, 128, resid, 3)
        return 0

    steps(8, residual_volume, 0)
    field_c[...] = dot(restrict[...], split_n[...])

    def write_state(f, first, slot, value):
        compact[f, first : first + slot, :] = value

    def write_blocks(f, first, slot, value):
        near_blocks[f, first : first + slot, :] = value

    def receive_state(faces):
        for f in faces:
            arrive(1, f)
            unpack(1, f, 128, write_state, 1.0, tops, slots)
            unpack(1, f, 32, write_blocks, 1.0, block_tops, block_slots)
        scatter_faces(compact, 32, 24, near_state, faces=faces)

    receive_state((2, 3, 4, 5))
    receive_lines(0, line_field)

    def split_lines(step, _):
        store_split(split_l, step, 96, load(line_field, rows_of(step)), 2)
        return 0

    steps(6, split_lines, 0)
    across[...] = dot(lines[...], split_l[...])
    neighbour(32, FINE_FACE, start_face, 0, near_state, across, signs, jump, True, (1, 2))
    receive(2, compact, -1.0)
    scatter_faces(compact, 32, 24, jump, jump)

    def residual_faces(step, _):
        values = face_pull(step, load(jump, rows_of(step)), face_state, 0, 2)
        store_split(split_f, step, 192, values, 3)
        return 0

    steps(12, residual_faces, 0)
    field_c[...] += dot(restrict_give[...], split_f[...])

    def coarse_first(step, _):
        rows = rows_of(step)
        store(base_c, rows, apply_blocks(block_rows(), load(field_c, rows)))
        return 0

    steps(14, coarse_first, 0)
    gather_faces(base_c, 32, 16, 8, compact_c)
    pack(3, lambda f, first, slot: compact_c[f, first : first + slot, :], 48)
    start(3)
    pack_lines(1, base_c, 128)
    start_lines(1)
    own_part(compact_c, own_c)
    scatter_faces(own_c, 16, 8, jump_c)

    def split_coarse(step, _):
        store_split(split_c, step, 32, load(base_c, rows_of(step)), 2)
        return 0

    steps(2, split_coarse, 0)
    cot_c[...] = dot(volume_c[0:96, :], split_c[0:64, :])

    def coarse_volume(step, _):
        rows = rows_of(step)
        values = load(base_c, rows)
        resid = residual(step, 32, cot_c, values, load(field_c, rows), state_c)
        change = apply_blocks(block_rows(), resid)
        values = [values[v] + change[v] for v in range(5)]
        store(field_c, rows, values)
        store_split(split_c, step, 32, values, 2)
        return 0

    steps(2, coarse_volume, 0)
    face_c[...] = dot(volume_c[96:192, :], split_c[0:64, :])

    def coarse_faces(step, _):
        values = face_pull(step, load(jump_c, rows_of(step)), state_c, 2, 1)
        store_split(split_cf, step, 96, apply_blocks(block_rows(), values), 2)
        return 0

    steps(6, coarse_faces, 0)
    face_c[...] += dot(give_c[0:96, :], split_cf[0:192, :])
    gather_faces(face_c, 0, 16, 8, compact_c)
    pack(4, lambda f, first, slot: compact_c[f, first : first + slot, :], 48)
    start(4)
    field_c[0:32, :] += dot(give_c[96:128, :], split_cf[0:192, :])

    receive_state((0, 1))

    def split_near(step, _):
        split_faces(step, near_state)
        return 0

    steps(12, split_near, 0)
    near_state_c[...] = dot(pick_face[...], split_f[0:384, :])

    def split_coarse_3(step, _):
        store_split(split_c, step, 32, load(field_c, rows_of(step)), 3)
        return 0

    steps(2, split_coarse_3, 0)
    field[...] += dot(extend[...], split_c[...])
    steps(8, split_field, 0)
    cot[...] = dot(volume[...], split_n[...])
    receive_lines(1, line_field)
    steps(6, split_lines, 0)
    across_c[...] = dot(lines_c[...], split_l[...])
    neighbour(16, COARSE_FACE, base_c, 2, near_state_c, across_c, signs_c, near_c, False, (0, 1, 2))

    def coarse_rest(step, _):
        values = face_pull(step, load(jump_c, rows_of(step)), state_c, 2, 1)
        store_split(split_cf, step, 96, apply_blocks(block_rows(), values), 3)
        return 0

    receive(3, compact_c, -1.0)
    scatter_faces(compact_c, 16, 8, jump_c)
    steps(6, coarse_rest, 0)
    face_c[...] += dot(chain[0:96, :], split_cf[...])
    gather_faces(face_c, 0, 16, 8, compact_c)
    own_part(compact_c, own_c)
    scatter_faces(own_c, 16, 8, jump_c, near_c)
    field[...] += dot(chain[96:224, :], split_cf[...])
    cot[...] += dot(chain[224:608, :], split_cf[...])
    steps(8, lambda s, c: smooth_volume(s, c, False), 0)
    receive(4, compact_c, -1.0)
    scatter_faces(compact_c, 16, 8, jump_c, jump_c)

    def split_jump(step, _):
        store_split(split_cf, step, 96, load(jump_c, rows_of(step)), 3)
        return 0

    steps(6, split_jump, 0)
    jump[...] += dot(face_extend[...], split_cf[...])
    steps(12, smooth_faces, 0)
    base[...] += dot(give[192:320, :], split_f[0:384, :])
    for v in range(5):
        out_h[v] = base[0:125, lanes(v)]
    for kind in range(5):
        for f in range(6):
            @pl.when(has[f])
            def _(kind=kind, f=f):
                remote[kind][f].wait_send()
    for level in range(2):
        for line in range(12):
            @pl.when(both[line])
            def _(level=level, line=line):
                remote_lines[level][line].wait_send()


def body(*args):
    constants = [jnp.asarray(table) for table in tables().values()]
    vmem = pltpu.VMEM
    raw = [vmem(a.shape, a.dtype) for a in args]
    held = [vmem(t.shape, t.dtype) for t in constants]
    work = [
        vmem((128, 640), F32), vmem((128, 640), F32), vmem((128, 640), F32), vmem((128, 640), F32),
        vmem((384, 640), BF16), vmem((384, 640), F32),
        vmem((192, 640), F32), vmem((192, 640), F32), vmem((192, 640), F32), vmem((192, 640), F32),
        vmem((576, 640), BF16), vmem((6, 128, 128), F32), vmem((6, 128, 128), F32),
        vmem((192, 640), F32), vmem((384, 640), F32), vmem((96, 640), F32),
        vmem((192, 640), BF16), vmem((6, 32, 128), F32), vmem((32, 128), F32), vmem((6, 16, 128), F32),
        vmem((2, 32, 128), F32), vmem((2, 16, 128), F32),
        vmem((128, 640), F32), vmem((224, 640), F32), vmem((224, 640), F32), vmem((96, 640), BF16),
        vmem((288, 640), BF16), vmem((96, 640), F32), vmem((96, 640), F32),
        vmem((6, 48, 128), F32), vmem((6, 48, 128), F32),
        vmem((96, 640), F32), vmem((96, 640), F32), vmem((192, 640), F32), vmem((96, 640), F32),
        vmem((25, 16, 128), F32), vmem((16, 128), F32),
    ]
    fine = [vmem((rows, 128), F32) for rows in (64, 64, 16, 16, 16, 16)]
    static = [vmem((rows, 128), F32) for rows in (80, 80, 24, 24, 24, 24)]
    coarse = [vmem((rows, 128), F32) for rows in (24, 24, 8, 8, 8, 8)]
    kinds = [*fine, *fine, *static, *static, *fine, *fine, *coarse, *coarse, *coarse, *coarse]
    sems = [
        pltpu.SemaphoreType.DMA((20,)),
        pltpu.SemaphoreType.DMA((5, 6)),
        pltpu.SemaphoreType.DMA((5, 6)),
        pltpu.SemaphoreType.DMA((2, 12)),
        pltpu.SemaphoreType.DMA((2, 12)),
    ]
    anywhere = pl.BlockSpec(memory_space=pl.ANY)
    return pl.pallas_call(
        kernel,
        out_shape=pltpu.VMEM(args[0].shape, F32),
        in_specs=[anywhere] * (len(args) + len(constants)),
        out_specs=pl.BlockSpec(memory_space=pltpu.VMEM),
        scratch_shapes=raw + held + work + kinds + [vmem((2, 12, 8, 128), F32)] * 2 + sems,
        compiler_params=pltpu.CompilerParams(
            collective_id=0, has_side_effects=True, vmem_limit_bytes=60 * 1024 * 1024
        ),
    )(*args, *constants)


def solution(mesh):
    in_specs = (
        P(None, None, AXES),
        P(None, None, AXES),
        P(None, AXES),
        P(None, None, AXES),
        P(None, AXES),
        P(*AXES),
        P(None, None, *AXES),
    )
    return jax.shard_map(
        body, mesh=mesh, in_specs=in_specs, out_specs=P(None, None, AXES), check_vma=False
    )
```

```python
import itertools

import jax
import jax.numpy as jnp
import ml_dtypes
import numpy as np
from jax import lax
from jax.experimental import pallas as pl
from jax.experimental.pallas import tpu as pltpu
from jax.sharding import PartitionSpec as P

OMEGA = 0.7
METRIC = 0.25
FINE_FACE = 0.5 * 0.25 / 0.1
COARSE_FACE = 0.5 * 0.25 * 3.0
MESH = pl.DeviceIdType.MESH
AXES = ("gx", "gy", "gz")
COUNTS = (2, 8, 8)
STRIDES = (64, 8, 1)
LINES = [(i, j, s, t) for i, j in ((0, 1), (0, 2), (1, 2)) for s in range(2) for t in range(2)]
F32 = jnp.float32
BF16 = jnp.bfloat16


def diff_table(nodes):
    count = len(nodes)
    weights = np.array(
        [1.0 / np.prod([nodes[j] - nodes[k] for k in range(count) if k != j]) for j in range(count)]
    )
    table = np.zeros((count, count))
    for i in range(count):
        for j in range(count):
            if i != j:
                table[i, j] = weights[j] / weights[i] / (nodes[i] - nodes[j])
        table[i, i] = -np.sum(table[i])
    return table.astype(np.float32).astype(np.float64)


def fine_points():
    return np.array([-1.0, -np.sqrt(3.0 / 7.0), 0.0, np.sqrt(3.0 / 7.0), 1.0])


def interp_table():
    points = fine_points()
    table = np.stack(
        [points * (points - 1.0) / 2.0, 1.0 - points**2, points * (points + 1.0) / 2.0], axis=1
    )
    return table.astype(np.float32).astype(np.float64)


def triple(a, b, c):
    return np.kron(np.kron(a, b), c)


def padded(matrix, rows, columns):
    result = np.zeros((rows, columns))
    result[: matrix.shape[0], : matrix.shape[1]] = matrix
    return result


def face_tables(count, rows, width):
    take = np.zeros((6 * rows, width))
    give = np.zeros((width, 6 * rows))
    for dim in range(3):
        for side in range(2):
            face = 2 * dim + side
            for row in range(rows):
                a, b = divmod(min(row, count * count - 1), count)
                place = [a, b]
                place.insert(dim, side * (count - 1))
                node = (place[0] * count + place[1]) * count + place[2]
                take[face * rows + row, node] = 1.0
                if row < count * count:
                    give[node, face * rows + row] = 1.0
    return take, give


def line_table(count, width):
    take = np.zeros((96, width))
    for line, (i, j, s, t) in enumerate(LINES):
        for node in range(count):
            place = [node] * 3
            place[i], place[j] = s * (count - 1), t * (count - 1)
            take[8 * line + node, (place[0] * count + place[1]) * count + place[2]] = 1.0
    return take


def line_faces(count, rows):
    result = np.zeros((2, 6 * rows, 96))
    for dim in range(3):
        for side in range(2):
            for row in range(rows):
                pair = divmod(min(row, count * count - 1), count)
                others = [d for d in range(3) if d != dim]
                for n in range(2):
                    if pair[n] % (count - 1) == 0:
                        sides = {dim: side, others[n]: pair[n] // (count - 1)}
                        i, j = sorted(sides)
                        line = LINES.index((i, j, sides[i], sides[j]))
                        result[n, (2 * dim + side) * rows + row, 8 * line + pair[1 - n]] = -1.0
    return result.reshape(12 * rows, 96)


def volume_table(count, width):
    table = diff_table(fine_points() if count == 5 else np.array([-1.0, 0.0, 1.0]))
    unit = np.eye(count)
    parts = []
    for dim in range(3):
        mats = [unit, unit, unit]
        mats[dim] = -METRIC * table.T
        parts.append(padded(triple(*mats), width, width))
    return np.concatenate(parts)


def two(matrix):
    high = matrix.astype(ml_dtypes.bfloat16)
    return np.concatenate([high, high], axis=1)


def three(matrix):
    high = matrix.astype(ml_dtypes.bfloat16)
    low = (matrix - high.astype(np.float64)).astype(ml_dtypes.bfloat16)
    return np.concatenate([high, high, low], axis=1)


def tables():
    prolong = interp_table()
    take, give = face_tables(5, 32, 128)
    take_c, give_c = face_tables(3, 16, 32)
    pick = np.zeros((32, 128))
    for n, (a, b, c) in enumerate(itertools.product(range(3), repeat=3)):
        pick[n, (2 * a * 5 + 2 * b) * 5 + 2 * c] = 1.0
    restrict = padded(triple(prolong.T, prolong.T, prolong.T), 32, 128)
    restrict = np.concatenate([restrict, take_c @ restrict, line_table(3, 32) @ restrict])
    extend = padded(triple(prolong, prolong, prolong), 128, 32)
    flat = np.kron(prolong, prolong)
    flat = np.concatenate([flat, np.repeat(flat[24:25], 7, axis=0)])
    face_extend = np.zeros((192, 96))
    for face in range(6):
        face_extend[32 * face : 32 * face + 32, 16 * face : 16 * face + 9] = flat
    correct = -COARSE_FACE * give_c
    face_pick = np.zeros((96, 192))
    for face in range(6):
        for row in range(16):
            a, b = divmod(min(row, 8), 3)
            face_pick[16 * face + row, 32 * face + 10 * a + 2 * b] = 1.0
    return {
        "take": two(np.concatenate([take, line_table(5, 128), pick])),
        "volume": three(volume_table(5, 128)),
        "give": two(-FINE_FACE * np.concatenate([take @ give, give])),
        "restrict": three(restrict),
        "restrict_give": three(-FINE_FACE * restrict @ give),
        "volume_c": two(np.concatenate([volume_table(3, 32), take_c])),
        "give_c": two(-COARSE_FACE * np.concatenate([take_c @ give_c, give_c])),
        "extend": three(extend),
        "face_extend": three(face_extend),
        "chain": three(np.concatenate([take_c @ correct, extend @ correct, volume_table(5, 128) @ extend @ correct])),
        "lines": two(line_faces(5, 32)),
        "lines_c": two(line_faces(3, 16)),
        "pick_face": two(face_pick),
    }


def dot(matrix, field):
    return jnp.dot(matrix, field, preferred_element_type=F32)


def split(value):
    high = value.astype(BF16)
    low = (value - high.astype(F32)).astype(BF16)
    return high, low


def lanes(var):
    return slice(128 * var, 128 * var + 128)


def steps(count, one, carry):
    for step in range(count):
        one(step, carry)


def rows_of(step, size=16):
    return slice(step * size, step * size + size)


def load(ref, rows):
    return [ref[rows, lanes(v)] for v in range(5)]


def store(ref, rows, values):
    for v in range(5):
        ref[rows, lanes(v)] = values[v]


def store_split(ref, step, height, values, pieces):
    for v in range(5):
        parts = split(values[v])
        for piece in range(pieces):
            ref[rows_of(step + piece * (height // 16)), lanes(v)] = parts[piece % 2]


def pull_all(cot, state):
    w = state[:3]
    enthalpy = state[3]
    crossed = [w[0] * c[1] + w[1] * c[2] + w[2] * c[3] + enthalpy * c[4] for c in cot]
    ends = [w[d] * cot[d][4] for d in range(3)]
    energy = ends[0] + ends[1] + ends[2]
    total = 0.4 * (cot[0][1] + cot[1][2] + cot[2][3] + energy)
    half_square = 0.5 * (w[0] * w[0] + w[1] * w[1] + w[2] * w[2])
    first = half_square * total - (w[0] * crossed[0] + w[1] * crossed[1] + w[2] * crossed[2])
    middle = []
    for j in range(3):
        drift = w[0] * cot[0][1 + j] + w[1] * cot[1][1 + j] + w[2] * cot[2][1 + j]
        middle.append(drift + cot[j][0] + crossed[j] - w[j] * total)
    return [first, *middle, total + energy]


def pull_face(jump, state, d, sign):
    w = state[:3]
    crossed = w[0] * jump[1] + w[1] * jump[2] + w[2] * jump[3] + state[3] * jump[4]
    end = w[d] * jump[4]
    total = 0.4 * (jump[1 + d] + end)
    half_square = 0.5 * (w[0] * w[0] + w[1] * w[1] + w[2] * w[2])
    out = [half_square * total - w[d] * crossed]
    for j in range(3):
        out.append(w[d] * jump[1 + j] - w[j] * total)
    out[1 + d] = out[1 + d] + (jump[0] + crossed)
    out.append(total + end)
    top = jnp.abs(w[d]) + state[4]
    if sign > 0:
        return [top * jump[v] + out[v] for v in range(5)]
    return [top * jump[v] - out[v] for v in range(5)]


def apply_blocks(blocks, values):
    result = []
    for a in range(5):
        total = blocks[a] * values[0]
        for b in range(1, 5):
            total = total + blocks[b * 5 + a] * values[b]
        result.append(total)
    return result


def kernel(start_h, source_h, density_h, velocity_h, pressure_h, shift_h, inverse_h, *rest):
    tables_h, rest = rest[:13], rest[13:]
    out_h, rest = rest[0], rest[1:]
    (start_r, source_r, density_r, velocity_r, pressure_r, shift_r, inverse_r), rest = rest[:7], rest[7:]
    tables_r, rest = rest[:13], rest[13:]
    (
        take, volume, give, restrict, restrict_give, volume_c, give_c, extend, face_extend,
        chain, lines, lines_c, pick_face,
    ) = tables_r
    (
        field, source, state, base, split_n, cot,
        face_state, start_face, face_field, jump, split_f, compact, own,
        near_state, across, line_field, split_l, near_blocks, block_row, edges, signs, signs_c,
        state_c, field_c, base_c, split_c, split_cf, cot_c, jump_c, compact_c, own_c,
        near_state_c, near_c, across_c, face_c,
        blocks, shift,
    ), rest = rest[:37], rest[37:]
    kinds = []
    for _ in range(5):
        kinds.append((rest[:6], rest[6:12]))
        rest = rest[12:]
    fine_u, fine_t, fine_w, coarse_u, coarse_w = kinds
    send_lines, recv_lines, in_sems, send_sems, recv_sems, send_line_sems, recv_line_sems = rest

    place = [lax.axis_index(axis) for axis in AXES]
    size = [lax.axis_size(axis) for axis in AXES]
    has = [place[f // 2] > 0 if f % 2 == 0 else place[f // 2] < size[f // 2] - 1 for f in range(6)]

    def partner(f):
        target = list(place)
        target[f // 2] = target[f // 2] + (1 if f % 2 else -1)
        return tuple(target)

    both = [has[2 * i + s] & has[2 * j + t] for i, j, s, t in LINES]

    def line_partner(line):
        i, j, s, t = LINES[line]
        target = list(place)
        target[i] = target[i] + 2 * s - 1
        target[j] = target[j] + 2 * t - 1
        return tuple(target)

    barrier = pltpu.get_barrier_semaphore()
    for f in range(6):
        @pl.when(has[f])
        def _(f=f):
            pl.semaphore_signal(barrier, inc=1, device_id=partner(f), device_id_type=MESH)
    for line in range(12):
        @pl.when(both[line])
        def _(line=line):
            pl.semaphore_signal(barrier, inc=1, device_id=line_partner(line), device_id_type=MESH)

    field[120:128, :] = jnp.zeros((8, 640), F32)
    source[120:128, :] = jnp.zeros((8, 640), F32)
    order = [
        (start_h, start_r), (tables_h[0], take), (velocity_h, velocity_r), (density_h, density_r),
        (pressure_h, pressure_r), (tables_h[1], volume), (source_h, source_r), (shift_h, shift_r),
        (inverse_h, inverse_r), (tables_h[2], give),
    ] + [(tables_h[n], tables_r[n]) for n in range(3, 13)]
    inward = [pltpu.make_async_copy(a, b, in_sems.at[n]) for n, (a, b) in enumerate(order)]
    for n in (0, 1, 2, 3, 4, 8, 7, 5, 6, *range(9, len(inward))):
        inward[n].start()

    def lane_place(rows, dim):
        lane = lax.broadcasted_iota(jnp.int32, (rows, 128), 1)
        return (lane // STRIDES[dim]) % COUNTS[dim]

    def gather_faces(source_ref, offset, rows, whole, target):
        sub = lax.broadcasted_iota(jnp.int32, (8, 128), 0)

        def one(f, _):
            top = offset + f * rows
            last = source_ref[slice(top + whole, top + whole + 8), lanes(0)]
            for v in range(5):
                target[f, whole * v : whole * v + whole, :] = source_ref[
                    slice(top, top + whole), lanes(v)
                ]
                if v:
                    here = source_ref[slice(top + whole, top + whole + 8), lanes(v)]
                    last = jnp.where(sub == v, here, last)
            target[f, 5 * whole : 5 * whole + 8, :] = last
            return 0

        steps(6, one, 0)

    def scatter_faces(source_ref, rows, whole, target, add=None):
        def put(here, v, value):
            target[here, lanes(v)] = value if add is None else add[here, lanes(v)] + value

        def one(f, _):
            top = f * rows
            for v in range(5):
                put(slice(top, top + whole), v, source_ref[f, whole * v : whole * v + whole, :])
                last = source_ref[f, 5 * whole + v : 5 * whole + v + 1, :]
                put(slice(top + whole, top + whole + 8), v, jnp.broadcast_to(last, (8, 128)))
            return 0

        steps(6, one, 0)

    def turn(value, amount):
        amount %= 128
        return pltpu.roll(value, amount, 1) if amount else value

    def copies(kind):
        sends, receives = kinds[kind]
        return [
            pltpu.make_async_remote_copy(
                src_ref=sends[f],
                dst_ref=receives[f ^ 1],
                send_sem=send_sems.at[kind, f],
                recv_sem=recv_sems.at[kind, f ^ 1],
                device_id=partner(f),
                device_id_type=MESH,
            )
            for f in range(6)
        ]

    def line_copies(level):
        return [
            pltpu.make_async_remote_copy(
                src_ref=send_lines.at[level, line],
                dst_ref=recv_lines.at[level, line ^ 3],
                send_sem=send_line_sems.at[level, line],
                recv_sem=recv_line_sems.at[level, line ^ 3],
                device_id=line_partner(line),
                device_id_type=MESH,
            )
            for line in range(12)
        ]

    remote = [copies(kind) for kind in range(5)]
    remote_lines = [line_copies(level) for level in range(2)]

    def pack(kind, read, height, top=0, slots=None):
        for f in range(6):
            dim, side = divmod(f, 2)
            count, stride = COUNTS[dim], STRIDES[dim]
            target = kinds[kind][0][f]
            slot = target.shape[0] if slots is None else slots[dim]
            where = lane_place(slot, dim)
            packed = None
            for g in range(height // slot):
                block = turn(read(f, g * slot, slot), (g - side * (count - 1)) * stride)
                packed = block if packed is None else jnp.where(where == g, block, packed)
            first = top if slots is None else top[dim]
            target[first : first + slot, :] = packed

    def pack_lines(level, source_ref, offset):
        for line, (i, j, s, t) in enumerate(LINES):
            where = lane_place(8, j)
            packed = None
            for v in range(5):
                block = source_ref[offset + 8 * line : offset + 8 * line + 8, lanes(v)]
                block = turn(block, (v - t * (COUNTS[j] - 1)) * STRIDES[j])
                packed = block if packed is None else jnp.where(where == v, block, packed)
            send_lines[level, line] = packed

    def start(kind):
        for f in (2, 3, 4, 5, 0, 1):
            @pl.when(has[f])
            def _(f=f):
                remote[kind][f].start()

    def start_lines(level):
        for line in range(12):
            @pl.when(both[line])
            def _(line=line):
                remote_lines[level][line].start()

    def unpack(kind, f, height, write, sign=1.0, top=0, slots=None):
        dim, side = divmod(f, 2)
        count, stride = COUNTS[dim], STRIDES[dim]
        received = kinds[kind][1][f]
        slot = received.shape[0] if slots is None else slots[dim]
        first = top if slots is None else top[dim]
        edge = jnp.where(lane_place(slot, dim) == side * (count - 1), sign, 0.0)

        @pl.when(has[f])
        def _():
            packed = received[first : first + slot, :]
            for g in range(height // slot):
                write(f, g * slot, slot, edge * turn(packed, (side * (count - 1) - g) * stride))

        @pl.when(jnp.logical_not(has[f]))
        def _():
            write(f, 0, height, jnp.zeros((height, 128), F32))

    def arrive(kind, f):
        @pl.when(has[f])
        def _():
            remote[kind][f ^ 1].wait_recv()

    def receive(kind, target, sign):
        def write(f, first, slot, value):
            target[f, first : first + slot, :] = value

        for f in range(6):
            arrive(kind, f)
            unpack(kind, f, target.shape[1], write, sign)

    def receive_lines(level, target):
        for line, (i, j, s, t) in enumerate(LINES):
            edge = (lane_place(8, i) == s * (COUNTS[i] - 1)) & (lane_place(8, j) == t * (COUNTS[j] - 1))
            here = slice(8 * line, 8 * line + 8)

            @pl.when(both[line])
            def _():
                remote_lines[level][line ^ 3].wait_recv()
                packed = recv_lines[level, line]
                for v in range(5):
                    amount = (t * (COUNTS[j] - 1) - v) * STRIDES[j] + (2 * s - 1) * (COUNTS[i] - 1) * STRIDES[i]
                    target[here, lanes(v)] = jnp.where(edge, turn(packed, amount), 0.0)

            @pl.when(jnp.logical_not(both[line]))
            def _():
                target[here, :] = jnp.zeros((8, 640), F32)

    def own_part(faces, result):
        for f in range(6):
            dim, side = divmod(f, 2)
            count, stride = COUNTS[dim], STRIDES[dim]
            inside = lane_place(faces.shape[1], dim) != side * (count - 1)
            other = turn(faces[f ^ 1], -stride if side else stride)
            result[f] = faces[f] - jnp.where(inside, other, 0.0)

    def face_pull(step, values, state_ref, offset, per_face):
        d, side = divmod(step // per_face, 2)
        return pull_face(values, load(state_ref, rows_of(step + offset)), d, 2 * side - 1)

    def neighbour(rows, face, mine, offset, near_s, across_ref, sign_ref, target, add):
        per_face = rows // 16
        for d in range(3):
            p, q = [n for n in range(3) if n != d]

            def one(step, _, d=d, p=p, q=q):
                side = step // per_face
                f = 2 * d + side
                at = step + 2 * d * per_face
                here = rows_of(at)
                local = load(near_s, here)
                top = [jnp.abs(local[n]) + local[4] for n in range(3)]
                edge = edges[f]
                own_side = load(mine, rows_of(at + offset))
                jumps = [None] * 3
                jumps[d] = [-edge * value for value in own_side]
                jumps[p] = load(across_ref, here)
                jumps[q] = load(across_ref, rows_of(at + 6 * per_face))
                part = rows_of(step - side * per_face)
                sign = [None] * 3
                sign[d] = 1.0 - 2.0 * side
                sign[p], sign[q] = sign_ref[0, part, :], sign_ref[1, part, :]
                pulled = pull_all([[sign[n] * value for value in jumps[n]] for n in range(3)], local)
                for n in range(3):
                    pulled = [pulled[v] + top[n] * jumps[n][v] for v in range(5)]
                inverse = [near_blocks[f, n : n + 1, :] for n in range(25)]
                change = apply_blocks(inverse, pulled)
                change = [face * value for value in change]
                if add:
                    change = [old + value for old, value in zip(load(target, here), change)]
                store(target, here, change)
                return 0

            steps(2 * per_face, one, 0)

    def block_rows():
        return [blocks[n] for n in range(25)]

    for f in range(6):
        dim, side = divmod(f, 2)
        edges[f] = (lane_place(16, dim) == side * (COUNTS[dim] - 1)).astype(F32)
    for ref, rows, count in ((signs, 32, 5), (signs_c, 16, 3)):
        row = jnp.minimum(lax.broadcasted_iota(jnp.int32, (rows, 128), 0), count * count - 1)
        for n, at in enumerate((row // count, row % count)):
            ref[n] = jnp.where(at == 0, -1.0, jnp.where(at == count - 1, 1.0, 0.0))
    block_row[...] = jnp.zeros((32, 128), F32)
    inward[0].wait()
    for v in range(5):
        field[0:125, lanes(v)] = start_r[v]

    def split_field(step, _):
        store_split(split_n, step, 128, load(field, rows_of(step)), 3)
        return 0

    steps(8, split_field, 0)
    inward[1].wait()
    start_face[...] = dot(take[0:192, :], split_n[0:256, :])
    line_field[...] = dot(take[192:288, :], split_n[0:256, :])
    gather_faces(start_face, 0, 32, 24, compact)
    pack(0, lambda f, first, slot: compact[f, first : first + slot, :], 128)
    pack_lines(0, line_field, 0)
    own_part(compact, own)
    scatter_faces(own, 32, 24, jump)

    for n in (2, 3, 4):
        inward[n].wait()
    state[120:128, :] = jnp.zeros((8, 640), F32)
    for part in ((0, 64), (64, 125)):
        here = slice(*part)
        w = [velocity_r[d, here, :] for d in range(3)]
        sound_2 = 1.4 * pressure_r[here, :] / density_r[here, :]
        for d in range(3):
            state[here, lanes(d)] = w[d]
        state[here, lanes(3)] = 2.5 * sound_2 + 0.5 * (w[0] * w[0] + w[1] * w[1] + w[2] * w[2])
        state[here, lanes(4)] = jnp.sqrt(sound_2)

    def split_state(step, _):
        store_split(split_f, step, 128, load(state, rows_of(step)), 2)
        return 0

    steps(8, split_state, 0)
    face_state[...] = dot(take[0:192, :], split_f[0:256, :])
    state_c[0:32, :] = dot(take[288:320, :], split_f[0:256, :])

    for n in (7, 8):
        inward[n].wait()
    spread = (
        lax.broadcasted_iota(jnp.int32, (8, 128), 1) % 8 == lax.broadcasted_iota(jnp.int32, (8, 128), 0)
    ).astype(F32)

    def to_lanes(value, count):
        wide = jnp.dot(
            value.reshape(16 * count, 8), spread,
            precision=lax.Precision.HIGHEST, preferred_element_type=F32,
        ).reshape(count, 16, 128)
        row = lax.broadcasted_iota(jnp.int32, (count, 16, 128), 1)
        lane = lax.broadcasted_iota(jnp.int32, (count, 16, 128), 2)
        kept = jnp.where(lane // 8 == row, wide, 0.0)
        return jnp.broadcast_to(jnp.sum(kept, axis=1, keepdims=True), (count, 16, 128))

    shift[...] = to_lanes(shift_r[...], 1)[0]
    blocks[...] = OMEGA * to_lanes(inverse_r[...], 25)

    for n in range(25):
        block_row[n : n + 1, :] = blocks[n, 0:1, :]
    gather_faces(face_state, 0, 32, 24, compact)
    slots, tops = (64, 16, 16), (0, 0, 0)
    pack(1, lambda f, first, slot: compact[f, first : first + slot, :], 128, tops, slots)
    block_slots, block_tops = (16, 8, 8), (64, 16, 16)
    pack(1, lambda f, first, slot: block_row[first : first + slot, :], 32, block_tops, block_slots)


    inward[5].wait()
    inward[6].wait()
    for v in range(5):
        source[0:125, lanes(v)] = source_r[v]

    def residual(step, height, cot_ref, values, right, state_ref):
        rows = rows_of(step)
        cots = [load(cot_ref, rows_of(step + d * (height // 16))) for d in range(3)]
        pulled = pull_all(cots, load(state_ref, rows))
        return [right[v] - shift[...] * values[v] - pulled[v] for v in range(5)]

    def smooth_volume(step, _, keep_split):
        rows = rows_of(step)
        values = load(field, rows)
        resid = residual(step, 128, cot, values, load(source, rows), state)
        change = apply_blocks(block_rows(), resid)
        values = [values[v] + change[v] for v in range(5)]
        store(base, rows, values)
        if keep_split:
            store_split(split_n, step, 128, values, 2)
        return 0

    cot[...] = dot(volume[...], split_n[...])
    steps(8, lambda s, c: smooth_volume(s, c, True), 0)
    pl.semaphore_wait(barrier, sum(h.astype(jnp.int32) for h in has + both))
    start(0)
    start(1)
    start_lines(0)
    face_field[...] = dot(take[0:192, :], split_n[0:256, :])

    def smooth_faces(step, _):
        values = face_pull(step, load(jump, rows_of(step)), face_state, 0, 2)
        store_split(split_f, step, 192, apply_blocks(block_rows(), values), 2)
        return 0

    steps(12, smooth_faces, 0)
    inward[9].wait()
    face_field[...] += dot(give[0:192, :], split_f[0:384, :])
    gather_faces(face_field, 0, 32, 24, compact)
    pack(2, lambda f, first, slot: compact[f, first : first + slot, :], 128)
    start(2)
    base[...] += dot(give[192:320, :], split_f[0:384, :])
    for n in range(10, 20):
        inward[n].wait()

    def split_faces(step, ref):
        store_split(split_f, step, 192, load(ref, rows_of(step)), 2)

    def split_face_state(step, _):
        split_faces(step, face_state)
        return 0

    steps(12, split_face_state, 0)
    state_c[32:128, :] = dot(pick_face[...], split_f[0:384, :])

    receive(0, compact, -1.0)
    scatter_faces(compact, 32, 24, jump)
    steps(12, smooth_faces, 0)
    face_field[...] += dot(give[0:192, :], split_f[0:384, :])
    field[...] = base[...] + dot(give[192:320, :], split_f[0:384, :])
    gather_faces(face_field, 0, 32, 24, compact)
    own_part(compact, own)
    scatter_faces(own, 32, 24, jump)
    steps(8, split_field, 0)
    cot[...] = dot(volume[...], split_n[...])

    def residual_volume(step, _):
        rows = rows_of(step)
        resid = residual(step, 128, cot, load(field, rows), load(source, rows), state)
        store_split(split_n, step, 128, resid, 3)
        return 0

    steps(8, residual_volume, 0)
    field_c[...] = dot(restrict[...], split_n[...])

    def write_state(f, first, slot, value):
        compact[f, first : first + slot, :] = value

    def write_blocks(f, first, slot, value):
        near_blocks[f, first : first + slot, :] = value

    for f in range(6):
        arrive(1, f)
        unpack(1, f, 128, write_state, 1.0, tops, slots)
        unpack(1, f, 32, write_blocks, 1.0, block_tops, block_slots)
    scatter_faces(compact, 32, 24, near_state)
    receive_lines(0, line_field)

    def split_lines(step, _):
        store_split(split_l, step, 96, load(line_field, rows_of(step)), 2)
        return 0

    steps(6, split_lines, 0)
    across[...] = dot(lines[...], split_l[...])
    neighbour(32, FINE_FACE, start_face, 0, near_state, across, signs, jump, True)
    receive(2, compact, -1.0)
    scatter_faces(compact, 32, 24, jump, jump)

    def residual_faces(step, _):
        values = face_pull(step, load(jump, rows_of(step)), face_state, 0, 2)
        store_split(split_f, step, 192, values, 3)
        return 0

    steps(12, residual_faces, 0)
    field_c[...] += dot(restrict_give[...], split_f[...])

    def coarse_first(step, _):
        rows = rows_of(step)
        store(base_c, rows, apply_blocks(block_rows(), load(field_c, rows)))
        return 0

    steps(14, coarse_first, 0)
    gather_faces(base_c, 32, 16, 8, compact_c)
    pack(3, lambda f, first, slot: compact_c[f, first : first + slot, :], 48)
    start(3)
    pack_lines(1, base_c, 128)
    start_lines(1)
    own_part(compact_c, own_c)
    scatter_faces(own_c, 16, 8, jump_c)

    def split_coarse(step, _):
        store_split(split_c, step, 32, load(base_c, rows_of(step)), 2)
        return 0

    steps(2, split_coarse, 0)
    cot_c[...] = dot(volume_c[0:96, :], split_c[0:64, :])

    def coarse_volume(step, _):
        rows = rows_of(step)
        values = load(base_c, rows)
        resid = residual(step, 32, cot_c, values, load(field_c, rows), state_c)
        change = apply_blocks(block_rows(), resid)
        values = [values[v] + change[v] for v in range(5)]
        store(field_c, rows, values)
        store_split(split_c, step, 32, values, 2)
        return 0

    steps(2, coarse_volume, 0)
    face_c[...] = dot(volume_c[96:192, :], split_c[0:64, :])

    def coarse_faces(step, _):
        values = face_pull(step, load(jump_c, rows_of(step)), state_c, 2, 1)
        store_split(split_cf, step, 96, apply_blocks(block_rows(), values), 2)
        return 0

    steps(6, coarse_faces, 0)
    face_c[...] += dot(give_c[0:96, :], split_cf[0:192, :])
    gather_faces(face_c, 0, 16, 8, compact_c)
    pack(4, lambda f, first, slot: compact_c[f, first : first + slot, :], 48)
    start(4)
    field_c[0:32, :] += dot(give_c[96:128, :], split_cf[0:192, :])

    def split_near(step, _):
        split_faces(step, near_state)
        return 0

    steps(12, split_near, 0)
    near_state_c[...] = dot(pick_face[...], split_f[0:384, :])

    def split_coarse_3(step, _):
        store_split(split_c, step, 32, load(field_c, rows_of(step)), 3)
        return 0

    steps(2, split_coarse_3, 0)
    field[...] += dot(extend[...], split_c[...])
    steps(8, split_field, 0)
    cot[...] = dot(volume[...], split_n[...])
    receive_lines(1, line_field)
    steps(6, split_lines, 0)
    across_c[...] = dot(lines_c[...], split_l[...])
    neighbour(16, COARSE_FACE, base_c, 2, near_state_c, across_c, signs_c, near_c, False)

    def coarse_rest(step, _):
        values = face_pull(step, load(jump_c, rows_of(step)), state_c, 2, 1)
        store_split(split_cf, step, 96, apply_blocks(block_rows(), values), 3)
        return 0

    receive(3, compact_c, -1.0)
    scatter_faces(compact_c, 16, 8, jump_c)
    steps(6, coarse_rest, 0)
    face_c[...] += dot(chain[0:96, :], split_cf[...])
    gather_faces(face_c, 0, 16, 8, compact_c)
    own_part(compact_c, own_c)
    scatter_faces(own_c, 16, 8, jump_c, near_c)
    field[...] += dot(chain[96:224, :], split_cf[...])
    cot[...] += dot(chain[224:608, :], split_cf[...])
    steps(8, lambda s, c: smooth_volume(s, c, False), 0)
    receive(4, compact_c, -1.0)
    scatter_faces(compact_c, 16, 8, jump_c, jump_c)

    def split_jump(step, _):
        store_split(split_cf, step, 96, load(jump_c, rows_of(step)), 3)
        return 0

    steps(6, split_jump, 0)
    jump[...] += dot(face_extend[...], split_cf[...])
    steps(12, smooth_faces, 0)
    base[...] += dot(give[192:320, :], split_f[0:384, :])
    for v in range(5):
        out_h[v] = base[0:125, lanes(v)]
    for kind in range(5):
        for f in range(6):
            @pl.when(has[f])
            def _(kind=kind, f=f):
                remote[kind][f].wait_send()
    for level in range(2):
        for line in range(12):
            @pl.when(both[line])
            def _(level=level, line=line):
                remote_lines[level][line].wait_send()


def body(*args):
    constants = [jnp.asarray(table) for table in tables().values()]
    vmem = pltpu.VMEM
    raw = [vmem(a.shape, a.dtype) for a in args]
    held = [vmem(t.shape, t.dtype) for t in constants]
    work = [
        vmem((128, 640), F32), vmem((128, 640), F32), vmem((128, 640), F32), vmem((128, 640), F32),
        vmem((384, 640), BF16), vmem((384, 640), F32),
        vmem((192, 640), F32), vmem((192, 640), F32), vmem((192, 640), F32), vmem((192, 640), F32),
        vmem((576, 640), BF16), vmem((6, 128, 128), F32), vmem((6, 128, 128), F32),
        vmem((192, 640), F32), vmem((384, 640), F32), vmem((96, 640), F32),
        vmem((192, 640), BF16), vmem((6, 32, 128), F32), vmem((32, 128), F32), vmem((6, 16, 128), F32),
        vmem((2, 32, 128), F32), vmem((2, 16, 128), F32),
        vmem((128, 640), F32), vmem((224, 640), F32), vmem((224, 640), F32), vmem((96, 640), BF16),
        vmem((288, 640), BF16), vmem((96, 640), F32), vmem((96, 640), F32),
        vmem((6, 48, 128), F32), vmem((6, 48, 128), F32),
        vmem((96, 640), F32), vmem((96, 640), F32), vmem((192, 640), F32), vmem((96, 640), F32),
        vmem((25, 16, 128), F32), vmem((16, 128), F32),
    ]
    fine = [vmem((rows, 128), F32) for rows in (64, 64, 16, 16, 16, 16)]
    static = [vmem((rows, 128), F32) for rows in (80, 80, 24, 24, 24, 24)]
    coarse = [vmem((rows, 128), F32) for rows in (24, 24, 8, 8, 8, 8)]
    kinds = [*fine, *fine, *static, *static, *fine, *fine, *coarse, *coarse, *coarse, *coarse]
    sems = [
        pltpu.SemaphoreType.DMA((20,)),
        pltpu.SemaphoreType.DMA((5, 6)),
        pltpu.SemaphoreType.DMA((5, 6)),
        pltpu.SemaphoreType.DMA((2, 12)),
        pltpu.SemaphoreType.DMA((2, 12)),
    ]
    anywhere = pl.BlockSpec(memory_space=pl.ANY)
    return pl.pallas_call(
        kernel,
        out_shape=pltpu.VMEM(args[0].shape, F32),
        in_specs=[anywhere] * (len(args) + len(constants)),
        out_specs=pl.BlockSpec(memory_space=pltpu.VMEM),
        scratch_shapes=raw + held + work + kinds + [vmem((2, 12, 8, 128), F32)] * 2 + sems,
        compiler_params=pltpu.CompilerParams(
            collective_id=0, has_side_effects=True, vmem_limit_bytes=60 * 1024 * 1024
        ),
    )(*args, *constants)


def solution(mesh):
    in_specs = (
        P(None, None, AXES),
        P(None, None, AXES),
        P(None, AXES),
        P(None, None, AXES),
        P(None, AXES),
        P(*AXES),
        P(None, None, *AXES),
    )
    return jax.shard_map(
        body, mesh=mesh, in_specs=in_specs, out_specs=P(None, None, AXES), check_vma=False
    )
```

```python
import itertools

import jax
import jax.numpy as jnp
import ml_dtypes
import numpy as np
from jax import lax
from jax.experimental import pallas as pl
from jax.experimental.pallas import tpu as pltpu
from jax.sharding import PartitionSpec as P

OMEGA = 0.7
METRIC = 0.25
FINE_FACE = 0.5 * 0.25 / 0.1
COARSE_FACE = 0.5 * 0.25 * 3.0
MESH = pl.DeviceIdType.MESH
AXES = ("gx", "gy", "gz")
COUNTS = (2, 8, 8)
STRIDES = (64, 8, 1)
LINES = [(i, j, s, t) for i, j in ((0, 1), (0, 2), (1, 2)) for s in range(2) for t in range(2)]
F32 = jnp.float32
BF16 = jnp.bfloat16


def diff_table(nodes):
    count = len(nodes)
    weights = np.array(
        [1.0 / np.prod([nodes[j] - nodes[k] for k in range(count) if k != j]) for j in range(count)]
    )
    table = np.zeros((count, count))
    for i in range(count):
        for j in range(count):
            if i != j:
                table[i, j] = weights[j] / weights[i] / (nodes[i] - nodes[j])
        table[i, i] = -np.sum(table[i])
    return table.astype(np.float32).astype(np.float64)


def fine_points():
    return np.array([-1.0, -np.sqrt(3.0 / 7.0), 0.0, np.sqrt(3.0 / 7.0), 1.0])


def interp_table():
    points = fine_points()
    table = np.stack(
        [points * (points - 1.0) / 2.0, 1.0 - points**2, points * (points + 1.0) / 2.0], axis=1
    )
    return table.astype(np.float32).astype(np.float64)


def triple(a, b, c):
    return np.kron(np.kron(a, b), c)


def padded(matrix, rows, columns):
    result = np.zeros((rows, columns))
    result[: matrix.shape[0], : matrix.shape[1]] = matrix
    return result


def face_tables(count, rows, width):
    take = np.zeros((6 * rows, width))
    give = np.zeros((width, 6 * rows))
    for dim in range(3):
        for side in range(2):
            face = 2 * dim + side
            for row in range(rows):
                a, b = divmod(min(row, count * count - 1), count)
                place = [a, b]
                place.insert(dim, side * (count - 1))
                node = (place[0] * count + place[1]) * count + place[2]
                take[face * rows + row, node] = 1.0
                if row < count * count:
                    give[node, face * rows + row] = 1.0
    return take, give


def line_table(count, width):
    take = np.zeros((96, width))
    for line, (i, j, s, t) in enumerate(LINES):
        for node in range(count):
            place = [node] * 3
            place[i], place[j] = s * (count - 1), t * (count - 1)
            take[8 * line + node, (place[0] * count + place[1]) * count + place[2]] = 1.0
    return take


def line_faces(count, rows):
    result = np.zeros((2, 6 * rows, 96))
    for dim in range(3):
        for side in range(2):
            for row in range(rows):
                pair = divmod(min(row, count * count - 1), count)
                others = [d for d in range(3) if d != dim]
                for n in range(2):
                    if pair[n] % (count - 1) == 0:
                        sides = {dim: side, others[n]: pair[n] // (count - 1)}
                        i, j = sorted(sides)
                        line = LINES.index((i, j, sides[i], sides[j]))
                        result[n, (2 * dim + side) * rows + row, 8 * line + pair[1 - n]] = -1.0
    return result.reshape(12 * rows, 96)


def volume_table(count, width):
    table = diff_table(fine_points() if count == 5 else np.array([-1.0, 0.0, 1.0]))
    unit = np.eye(count)
    parts = []
    for dim in range(3):
        mats = [unit, unit, unit]
        mats[dim] = -METRIC * table.T
        parts.append(padded(triple(*mats), width, width))
    return np.concatenate(parts)


def two(matrix):
    high = matrix.astype(ml_dtypes.bfloat16)
    return np.concatenate([high, high], axis=1)


def three(matrix):
    high = matrix.astype(ml_dtypes.bfloat16)
    low = (matrix - high.astype(np.float64)).astype(ml_dtypes.bfloat16)
    return np.concatenate([high, high, low], axis=1)


def tables():
    prolong = interp_table()
    take, give = face_tables(5, 32, 128)
    take_c, give_c = face_tables(3, 16, 32)
    pick = np.zeros((32, 128))
    for n, (a, b, c) in enumerate(itertools.product(range(3), repeat=3)):
        pick[n, (2 * a * 5 + 2 * b) * 5 + 2 * c] = 1.0
    restrict = padded(triple(prolong.T, prolong.T, prolong.T), 32, 128)
    restrict = np.concatenate([restrict, take_c @ restrict, line_table(3, 32) @ restrict])
    extend = padded(triple(prolong, prolong, prolong), 128, 32)
    flat = np.kron(prolong, prolong)
    flat = np.concatenate([flat, np.repeat(flat[24:25], 7, axis=0)])
    face_extend = np.zeros((192, 96))
    for face in range(6):
        face_extend[32 * face : 32 * face + 32, 16 * face : 16 * face + 9] = flat
    correct = -COARSE_FACE * give_c
    face_pick = np.zeros((96, 192))
    for face in range(6):
        for row in range(16):
            a, b = divmod(min(row, 8), 3)
            face_pick[16 * face + row, 32 * face + 10 * a + 2 * b] = 1.0
    return {
        "take": two(np.concatenate([take, line_table(5, 128), pick])),
        "volume": three(volume_table(5, 128)),
        "give": two(-FINE_FACE * np.concatenate([take @ give, give])),
        "restrict": three(restrict),
        "restrict_give": three(-FINE_FACE * restrict @ give),
        "volume_c": two(np.concatenate([volume_table(3, 32), take_c])),
        "give_c": two(-COARSE_FACE * np.concatenate([take_c @ give_c, give_c])),
        "extend": three(extend),
        "face_extend": three(face_extend),
        "chain": three(np.concatenate([take_c @ correct, extend @ correct, volume_table(5, 128) @ extend @ correct])),
        "lines": two(line_faces(5, 32)),
        "lines_c": two(line_faces(3, 16)),
        "pick_face": two(face_pick),
    }


def dot(matrix, field):
    return jnp.dot(matrix, field, preferred_element_type=F32)


def split(value):
    high = value.astype(BF16)
    low = (value - high.astype(F32)).astype(BF16)
    return high, low


def lanes(var):
    return slice(128 * var, 128 * var + 128)


def steps(count, one, carry):
    for step in range(count):
        one(step, carry)


def rows_of(step, size=16):
    return slice(step * size, step * size + size)


def load(ref, rows):
    return [ref[rows, lanes(v)] for v in range(5)]


def store(ref, rows, values):
    for v in range(5):
        ref[rows, lanes(v)] = values[v]


def store_split(ref, step, height, values, pieces):
    for v in range(5):
        parts = split(values[v])
        for piece in range(pieces):
            ref[rows_of(step + piece * (height // 16)), lanes(v)] = parts[piece % 2]


def pull_all(cot, state):
    w = state[:3]
    enthalpy = state[3]
    crossed = [w[0] * c[1] + w[1] * c[2] + w[2] * c[3] + enthalpy * c[4] for c in cot]
    ends = [w[d] * cot[d][4] for d in range(3)]
    energy = ends[0] + ends[1] + ends[2]
    total = 0.4 * (cot[0][1] + cot[1][2] + cot[2][3] + energy)
    half_square = 0.5 * (w[0] * w[0] + w[1] * w[1] + w[2] * w[2])
    first = half_square * total - (w[0] * crossed[0] + w[1] * crossed[1] + w[2] * crossed[2])
    middle = []
    for j in range(3):
        drift = w[0] * cot[0][1 + j] + w[1] * cot[1][1 + j] + w[2] * cot[2][1 + j]
        middle.append(drift + cot[j][0] + crossed[j] - w[j] * total)
    return [first, *middle, total + energy]


def pull_face(jump, state, d, sign):
    w = state[:3]
    crossed = w[0] * jump[1] + w[1] * jump[2] + w[2] * jump[3] + state[3] * jump[4]
    end = w[d] * jump[4]
    total = 0.4 * (jump[1 + d] + end)
    half_square = 0.5 * (w[0] * w[0] + w[1] * w[1] + w[2] * w[2])
    out = [half_square * total - w[d] * crossed]
    for j in range(3):
        out.append(w[d] * jump[1 + j] - w[j] * total)
    out[1 + d] = out[1 + d] + (jump[0] + crossed)
    out.append(total + end)
    top = jnp.abs(w[d]) + state[4]
    if sign > 0:
        return [top * jump[v] + out[v] for v in range(5)]
    return [top * jump[v] - out[v] for v in range(5)]


def apply_blocks(blocks, values):
    result = []
    for a in range(5):
        total = blocks[a] * values[0]
        for b in range(1, 5):
            total = total + blocks[b * 5 + a] * values[b]
        result.append(total)
    return result


def kernel(start_h, source_h, density_h, velocity_h, pressure_h, shift_h, inverse_h, *rest):
    tables_h, rest = rest[:13], rest[13:]
    out_h, rest = rest[0], rest[1:]
    (start_r, source_r, density_r, velocity_r, pressure_r, shift_r, inverse_r), rest = rest[:7], rest[7:]
    tables_r, rest = rest[:13], rest[13:]
    (
        take, volume, give, restrict, restrict_give, volume_c, give_c, extend, face_extend,
        chain, lines, lines_c, pick_face,
    ) = tables_r
    (
        field, source, state, base, split_n, cot,
        face_state, start_face, face_field, jump, split_f, compact, own,
        near_state, across, line_field, split_l, near_blocks, block_row, edges, signs, signs_c,
        state_c, field_c, base_c, split_c, split_cf, cot_c, jump_c, compact_c, own_c,
        near_state_c, near_c, across_c, face_c,
        blocks, shift,
    ), rest = rest[:37], rest[37:]
    kinds = []
    for _ in range(5):
        kinds.append((rest[:6], rest[6:12]))
        rest = rest[12:]
    fine_u, fine_t, fine_w, coarse_u, coarse_w = kinds
    send_lines, recv_lines, in_sems, send_sems, recv_sems, send_line_sems, recv_line_sems = rest

    place = [lax.axis_index(axis) for axis in AXES]
    size = [lax.axis_size(axis) for axis in AXES]
    has = [place[f // 2] > 0 if f % 2 == 0 else place[f // 2] < size[f // 2] - 1 for f in range(6)]

    def partner(f):
        target = list(place)
        target[f // 2] = target[f // 2] + (1 if f % 2 else -1)
        return tuple(target)

    both = [has[2 * i + s] & has[2 * j + t] for i, j, s, t in LINES]

    def line_partner(line):
        i, j, s, t = LINES[line]
        target = list(place)
        target[i] = target[i] + 2 * s - 1
        target[j] = target[j] + 2 * t - 1
        return tuple(target)

    barrier = pltpu.get_barrier_semaphore()
    for f in range(6):
        @pl.when(has[f])
        def _(f=f):
            pl.semaphore_signal(barrier, inc=1, device_id=partner(f), device_id_type=MESH)
    for line in range(12):
        @pl.when(both[line])
        def _(line=line):
            pl.semaphore_signal(barrier, inc=1, device_id=line_partner(line), device_id_type=MESH)

    field[120:128, :] = jnp.zeros((8, 640), F32)
    source[120:128, :] = jnp.zeros((8, 640), F32)
    order = [
        (start_h, start_r), (tables_h[0], take), (velocity_h, velocity_r), (density_h, density_r),
        (pressure_h, pressure_r), (tables_h[1], volume), (source_h, source_r), (shift_h, shift_r),
        (inverse_h, inverse_r), (tables_h[2], give),
    ] + [(tables_h[n], tables_r[n]) for n in range(3, 13)]
    inward = [pltpu.make_async_copy(a, b, in_sems.at[n]) for n, (a, b) in enumerate(order)]
    for n in (0, 1, 2, 3, 4, 8, 7, 5, 6, *range(9, len(inward))):
        inward[n].start()

    def lane_place(rows, dim):
        lane = lax.broadcasted_iota(jnp.int32, (rows, 128), 1)
        return (lane // STRIDES[dim]) % COUNTS[dim]

    def gather_faces(source_ref, offset, rows, whole, target):
        sub = lax.broadcasted_iota(jnp.int32, (8, 128), 0)

        def one(f, _):
            top = offset + f * rows
            last = source_ref[slice(top + whole, top + whole + 8), lanes(0)]
            for v in range(5):
                target[f, whole * v : whole * v + whole, :] = source_ref[
                    slice(top, top + whole), lanes(v)
                ]
                if v:
                    here = source_ref[slice(top + whole, top + whole + 8), lanes(v)]
                    last = jnp.where(sub == v, here, last)
            target[f, 5 * whole : 5 * whole + 8, :] = last
            return 0

        steps(6, one, 0)

    def scatter_faces(source_ref, rows, whole, target, add=None, faces=range(6)):
        def put(here, v, value):
            target[here, lanes(v)] = value if add is None else add[here, lanes(v)] + value

        def one(f, _):
            top = f * rows
            for v in range(5):
                put(slice(top, top + whole), v, source_ref[f, whole * v : whole * v + whole, :])
                last = source_ref[f, 5 * whole + v : 5 * whole + v + 1, :]
                put(slice(top + whole, top + whole + 8), v, jnp.broadcast_to(last, (8, 128)))
            return 0

        for f in faces:
            one(f, 0)

    def turn(value, amount):
        amount %= 128
        return pltpu.roll(value, amount, 1) if amount else value

    def copies(kind):
        sends, receives = kinds[kind]
        return [
            pltpu.make_async_remote_copy(
                src_ref=sends[f],
                dst_ref=receives[f ^ 1],
                send_sem=send_sems.at[kind, f],
                recv_sem=recv_sems.at[kind, f ^ 1],
                device_id=partner(f),
                device_id_type=MESH,
            )
            for f in range(6)
        ]

    def line_copies(level):
        return [
            pltpu.make_async_remote_copy(
                src_ref=send_lines.at[level, line],
                dst_ref=recv_lines.at[level, line ^ 3],
                send_sem=send_line_sems.at[level, line],
                recv_sem=recv_line_sems.at[level, line ^ 3],
                device_id=line_partner(line),
                device_id_type=MESH,
            )
            for line in range(12)
        ]

    remote = [copies(kind) for kind in range(5)]
    remote_lines = [line_copies(level) for level in range(2)]

    def pack(kind, read, height, top=0, slots=None, faces=range(6)):
        for f in faces:
            dim, side = divmod(f, 2)
            count, stride = COUNTS[dim], STRIDES[dim]
            target = kinds[kind][0][f]
            slot = target.shape[0] if slots is None else slots[dim]
            where = lane_place(slot, dim)
            packed = None
            for g in range(height // slot):
                block = turn(read(f, g * slot, slot), (g - side * (count - 1)) * stride)
                packed = block if packed is None else jnp.where(where == g, block, packed)
            first = top if slots is None else top[dim]
            target[first : first + slot, :] = packed

    def pack_lines(level, source_ref, offset):
        for line, (i, j, s, t) in enumerate(LINES):
            where = lane_place(8, j)
            packed = None
            for v in range(5):
                block = source_ref[offset + 8 * line : offset + 8 * line + 8, lanes(v)]
                block = turn(block, (v - t * (COUNTS[j] - 1)) * STRIDES[j])
                packed = block if packed is None else jnp.where(where == v, block, packed)
            send_lines[level, line] = packed

    def start(kind, faces=(2, 3, 4, 5, 0, 1)):
        for f in faces:
            @pl.when(has[f])
            def _(f=f):
                remote[kind][f].start()

    def start_lines(level):
        for line in range(12):
            @pl.when(both[line])
            def _(line=line):
                remote_lines[level][line].start()

    def unpack(kind, f, height, write, sign=1.0, top=0, slots=None):
        dim, side = divmod(f, 2)
        count, stride = COUNTS[dim], STRIDES[dim]
        received = kinds[kind][1][f]
        slot = received.shape[0] if slots is None else slots[dim]
        first = top if slots is None else top[dim]
        edge = jnp.where(lane_place(slot, dim) == side * (count - 1), sign, 0.0)

        @pl.when(has[f])
        def _():
            packed = received[first : first + slot, :]
            for g in range(height // slot):
                write(f, g * slot, slot, edge * turn(packed, (side * (count - 1) - g) * stride))

        @pl.when(jnp.logical_not(has[f]))
        def _():
            write(f, 0, height, jnp.zeros((height, 128), F32))

    def arrive(kind, f):
        @pl.when(has[f])
        def _():
            remote[kind][f ^ 1].wait_recv()

    def receive(kind, target, sign):
        def write(f, first, slot, value):
            target[f, first : first + slot, :] = value

        for f in range(6):
            arrive(kind, f)
            unpack(kind, f, target.shape[1], write, sign)

    def receive_lines(level, target):
        for line, (i, j, s, t) in enumerate(LINES):
            edge = (lane_place(8, i) == s * (COUNTS[i] - 1)) & (lane_place(8, j) == t * (COUNTS[j] - 1))
            here = slice(8 * line, 8 * line + 8)

            @pl.when(both[line])
            def _():
                remote_lines[level][line ^ 3].wait_recv()
                packed = recv_lines[level, line]
                for v in range(5):
                    amount = (t * (COUNTS[j] - 1) - v) * STRIDES[j] + (2 * s - 1) * (COUNTS[i] - 1) * STRIDES[i]
                    target[here, lanes(v)] = jnp.where(edge, turn(packed, amount), 0.0)

            @pl.when(jnp.logical_not(both[line]))
            def _():
                target[here, :] = jnp.zeros((8, 640), F32)

    def own_part(faces, result):
        for f in range(6):
            dim, side = divmod(f, 2)
            count, stride = COUNTS[dim], STRIDES[dim]
            inside = lane_place(faces.shape[1], dim) != side * (count - 1)
            other = turn(faces[f ^ 1], -stride if side else stride)
            result[f] = faces[f] - jnp.where(inside, other, 0.0)

    def face_pull(step, values, state_ref, offset, per_face):
        d, side = divmod(step // per_face, 2)
        return pull_face(values, load(state_ref, rows_of(step + offset)), d, 2 * side - 1)

    def neighbour(rows, face, mine, offset, near_s, across_ref, sign_ref, target, add, dims):
        per_face = rows // 16
        for d in dims:
            p, q = [n for n in range(3) if n != d]

            def one(step, _, d=d, p=p, q=q):
                side = step // per_face
                f = 2 * d + side
                at = step + 2 * d * per_face
                here = rows_of(at)
                local = load(near_s, here)
                top = [jnp.abs(local[n]) + local[4] for n in range(3)]
                edge = edges[f]
                own_side = load(mine, rows_of(at + offset))
                jumps = [None] * 3
                jumps[d] = [-edge * value for value in own_side]
                jumps[p] = load(across_ref, here)
                jumps[q] = load(across_ref, rows_of(at + 6 * per_face))
                part = rows_of(step - side * per_face)
                sign = [None] * 3
                sign[d] = 1.0 - 2.0 * side
                sign[p], sign[q] = sign_ref[0, part, :], sign_ref[1, part, :]
                pulled = pull_all([[sign[n] * value for value in jumps[n]] for n in range(3)], local)
                for n in range(3):
                    pulled = [pulled[v] + top[n] * jumps[n][v] for v in range(5)]
                inverse = [near_blocks[f, n : n + 1, :] for n in range(25)]
                change = apply_blocks(inverse, pulled)
                change = [face * value for value in change]
                if add:
                    change = [old + value for old, value in zip(load(target, here), change)]
                store(target, here, change)
                return 0

            steps(2 * per_face, one, 0)

    def block_rows():
        return [blocks[n] for n in range(25)]

    for f in range(6):
        dim, side = divmod(f, 2)
        edges[f] = (lane_place(16, dim) == side * (COUNTS[dim] - 1)).astype(F32)
    for ref, rows, count in ((signs, 32, 5), (signs_c, 16, 3)):
        row = jnp.minimum(lax.broadcasted_iota(jnp.int32, (rows, 128), 0), count * count - 1)
        for n, at in enumerate((row // count, row % count)):
            ref[n] = jnp.where(at == 0, -1.0, jnp.where(at == count - 1, 1.0, 0.0))
    block_row[...] = jnp.zeros((32, 128), F32)
    inward[0].wait()
    for v in range(5):
        field[0:125, lanes(v)] = start_r[v]

    def split_field(step, _):
        store_split(split_n, step, 128, load(field, rows_of(step)), 3)
        return 0

    steps(8, split_field, 0)
    inward[1].wait()
    start_face[...] = dot(take[0:192, :], split_n[0:256, :])
    line_field[...] = dot(take[192:288, :], split_n[0:256, :])
    gather_faces(start_face, 0, 32, 24, compact)
    pack(0, lambda f, first, slot: compact[f, first : first + slot, :], 128)
    pack_lines(0, line_field, 0)
    own_part(compact, own)
    scatter_faces(own, 32, 24, jump)

    for n in (2, 3, 4):
        inward[n].wait()
    state[120:128, :] = jnp.zeros((8, 640), F32)
    for part in ((0, 64), (64, 125)):
        here = slice(*part)
        w = [velocity_r[d, here, :] for d in range(3)]
        sound_2 = 1.4 * pressure_r[here, :] / density_r[here, :]
        for d in range(3):
            state[here, lanes(d)] = w[d]
        state[here, lanes(3)] = 2.5 * sound_2 + 0.5 * (w[0] * w[0] + w[1] * w[1] + w[2] * w[2])
        state[here, lanes(4)] = jnp.sqrt(sound_2)

    def split_state(step, _):
        store_split(split_f, step, 128, load(state, rows_of(step)), 2)
        return 0

    steps(8, split_state, 0)
    face_state[...] = dot(take[0:192, :], split_f[0:256, :])
    state_c[0:32, :] = dot(take[288:320, :], split_f[0:256, :])

    for n in (7, 8):
        inward[n].wait()
    spread = (
        lax.broadcasted_iota(jnp.int32, (8, 128), 1) % 8 == lax.broadcasted_iota(jnp.int32, (8, 128), 0)
    ).astype(F32)

    def to_lanes(value, count):
        wide = jnp.dot(
            value.reshape(16 * count, 8), spread,
            precision=lax.Precision.HIGHEST, preferred_element_type=F32,
        ).reshape(count, 16, 128)
        row = lax.broadcasted_iota(jnp.int32, (count, 16, 128), 1)
        lane = lax.broadcasted_iota(jnp.int32, (count, 16, 128), 2)
        kept = jnp.where(lane // 8 == row, wide, 0.0)
        return jnp.broadcast_to(jnp.sum(kept, axis=1, keepdims=True), (count, 16, 128))

    shift[...] = to_lanes(shift_r[...], 1)[0]
    blocks[...] = OMEGA * to_lanes(inverse_r[...], 25)

    for n in range(25):
        block_row[n : n + 1, :] = blocks[n, 0:1, :]
    gather_faces(face_state, 0, 32, 24, compact)
    slots, tops = (64, 16, 16), (0, 0, 0)
    pack(1, lambda f, first, slot: compact[f, first : first + slot, :], 128, tops, slots)
    block_slots, block_tops = (16, 8, 8), (64, 16, 16)
    pack(1, lambda f, first, slot: block_row[first : first + slot, :], 32, block_tops, block_slots)


    inward[5].wait()
    inward[6].wait()
    for v in range(5):
        source[0:125, lanes(v)] = source_r[v]

    def residual(step, height, cot_ref, values, right, state_ref):
        rows = rows_of(step)
        cots = [load(cot_ref, rows_of(step + d * (height // 16))) for d in range(3)]
        pulled = pull_all(cots, load(state_ref, rows))
        return [right[v] - shift[...] * values[v] - pulled[v] for v in range(5)]

    def smooth_volume(step, _, keep_split):
        rows = rows_of(step)
        values = load(field, rows)
        resid = residual(step, 128, cot, values, load(source, rows), state)
        change = apply_blocks(block_rows(), resid)
        values = [values[v] + change[v] for v in range(5)]
        store(base, rows, values)
        if keep_split:
            store_split(split_n, step, 128, values, 2)
        return 0

    cot[...] = dot(volume[...], split_n[...])
    steps(8, lambda s, c: smooth_volume(s, c, True), 0)
    pl.semaphore_wait(barrier, sum(h.astype(jnp.int32) for h in has + both))
    start(0)
    start(1, (2, 3, 4, 5))
    start_lines(0)
    face_field[...] = dot(take[0:192, :], split_n[0:256, :])

    def smooth_faces(step, _):
        values = face_pull(step, load(jump, rows_of(step)), face_state, 0, 2)
        store_split(split_f, step, 192, apply_blocks(block_rows(), values), 2)
        return 0

    steps(12, smooth_faces, 0)
    inward[9].wait()
    face_field[...] += dot(give[0:192, :], split_f[0:384, :])
    gather_faces(face_field, 0, 32, 24, compact)
    pack(2, lambda f, first, slot: compact[f, first : first + slot, :], 128, faces=(2, 3, 4, 5))
    start(2, (2, 3, 4, 5))
    base[...] += dot(give[192:320, :], split_f[0:384, :])
    for n in range(10, 20):
        inward[n].wait()

    def split_faces(step, ref):
        store_split(split_f, step, 192, load(ref, rows_of(step)), 2)

    def split_face_state(step, _):
        split_faces(step, face_state)
        return 0

    steps(12, split_face_state, 0)
    state_c[32:128, :] = dot(pick_face[...], split_f[0:384, :])

    receive(0, compact, -1.0)
    scatter_faces(compact, 32, 24, jump)
    steps(12, smooth_faces, 0)
    face_field[...] += dot(give[0:192, :], split_f[0:384, :])
    gather_faces(face_field, 0, 32, 24, compact)
    pack(2, lambda f, first, slot: compact[f, first : first + slot, :], 128, faces=(0, 1))
    start(2, (0, 1))
    start(1, (0, 1))
    field[...] = base[...] + dot(give[192:320, :], split_f[0:384, :])
    own_part(compact, own)
    scatter_faces(own, 32, 24, jump)
    steps(8, split_field, 0)
    cot[...] = dot(volume[...], split_n[...])

    def residual_volume(step, _):
        rows = rows_of(step)
        resid = residual(step, 128, cot, load(field, rows), load(source, rows), state)
        store_split(split_n, step, 128, resid, 3)
        return 0

    steps(8, residual_volume, 0)
    field_c[...] = dot(restrict[...], split_n[...])

    def write_state(f, first, slot, value):
        compact[f, first : first + slot, :] = value

    def write_blocks(f, first, slot, value):
        near_blocks[f, first : first + slot, :] = value

    def receive_state(faces):
        for f in faces:
            arrive(1, f)
            unpack(1, f, 128, write_state, 1.0, tops, slots)
            unpack(1, f, 32, write_blocks, 1.0, block_tops, block_slots)
        scatter_faces(compact, 32, 24, near_state, faces=faces)

    receive_state((2, 3, 4, 5))
    receive_lines(0, line_field)

    def split_lines(step, _):
        store_split(split_l, step, 96, load(line_field, rows_of(step)), 2)
        return 0

    steps(6, split_lines, 0)
    across[...] = dot(lines[...], split_l[...])
    neighbour(32, FINE_FACE, start_face, 0, near_state, across, signs, jump, True, (1, 2))
    receive(2, compact, -1.0)
    scatter_faces(compact, 32, 24, jump, jump)

    def residual_faces(step, _):
        values = face_pull(step, load(jump, rows_of(step)), face_state, 0, 2)
        store_split(split_f, step, 192, values, 3)
        return 0

    steps(12, residual_faces, 0)
    field_c[...] += dot(restrict_give[...], split_f[...])

    def coarse_first(step, _):
        rows = rows_of(step)
        store(base_c, rows, apply_blocks(block_rows(), load(field_c, rows)))
        return 0

    steps(14, coarse_first, 0)
    gather_faces(base_c, 32, 16, 8, compact_c)
    pack(3, lambda f, first, slot: compact_c[f, first : first + slot, :], 48)
    start(3)
    pack_lines(1, base_c, 128)
    start_lines(1)
    own_part(compact_c, own_c)
    scatter_faces(own_c, 16, 8, jump_c)

    def split_coarse(step, _):
        store_split(split_c, step, 32, load(base_c, rows_of(step)), 2)
        return 0

    steps(2, split_coarse, 0)
    cot_c[...] = dot(volume_c[0:96, :], split_c[0:64, :])

    def coarse_volume(step, _):
        rows = rows_of(step)
        values = load(base_c, rows)
        resid = residual(step, 32, cot_c, values, load(field_c, rows), state_c)
        change = apply_blocks(block_rows(), resid)
        values = [values[v] + change[v] for v in range(5)]
        store(field_c, rows, values)
        store_split(split_c, step, 32, values, 2)
        return 0

    steps(2, coarse_volume, 0)
    face_c[...] = dot(volume_c[96:192, :], split_c[0:64, :])

    def coarse_faces(step, _):
        values = face_pull(step, load(jump_c, rows_of(step)), state_c, 2, 1)
        store_split(split_cf, step, 96, apply_blocks(block_rows(), values), 2)
        return 0

    steps(6, coarse_faces, 0)
    face_c[...] += dot(give_c[0:96, :], split_cf[0:192, :])
    gather_faces(face_c, 0, 16, 8, compact_c)
    pack(4, lambda f, first, slot: compact_c[f, first : first + slot, :], 48)
    start(4)
    field_c[0:32, :] += dot(give_c[96:128, :], split_cf[0:192, :])

    receive_state((0, 1))

    def split_near(step, _):
        split_faces(step, near_state)
        return 0

    steps(12, split_near, 0)
    near_state_c[...] = dot(pick_face[...], split_f[0:384, :])

    def split_coarse_3(step, _):
        store_split(split_c, step, 32, load(field_c, rows_of(step)), 3)
        return 0

    steps(2, split_coarse_3, 0)
    field[...] += dot(extend[...], split_c[...])
    steps(8, split_field, 0)
    cot[...] = dot(volume[...], split_n[...])
    receive_lines(1, line_field)
    steps(6, split_lines, 0)
    across_c[...] = dot(lines_c[...], split_l[...])
    neighbour(16, COARSE_FACE, base_c, 2, near_state_c, across_c, signs_c, near_c, False, (0, 1, 2))

    def coarse_rest(step, _):
        values = face_pull(step, load(jump_c, rows_of(step)), state_c, 2, 1)
        store_split(split_cf, step, 96, apply_blocks(block_rows(), values), 3)
        return 0

    receive(3, compact_c, -1.0)
    scatter_faces(compact_c, 16, 8, jump_c)
    steps(6, coarse_rest, 0)
    face_c[...] += dot(chain[0:96, :], split_cf[...])
    gather_faces(face_c, 0, 16, 8, compact_c)
    own_part(compact_c, own_c)
    scatter_faces(own_c, 16, 8, jump_c, near_c)
    field[...] += dot(chain[96:224, :], split_cf[...])
    cot[...] += dot(chain[224:608, :], split_cf[...])
    steps(8, lambda s, c: smooth_volume(s, c, False), 0)
    receive(4, compact_c, -1.0)
    scatter_faces(compact_c, 16, 8, jump_c, jump_c)

    def split_jump(step, _):
        store_split(split_cf, step, 96, load(jump_c, rows_of(step)), 3)
        return 0

    steps(6, split_jump, 0)
    jump[...] += dot(face_extend[...], split_cf[...])
    steps(12, smooth_faces, 0)
    base[...] += dot(give[192:320, :], split_f[0:384, :])
    for v in range(5):
        out_h[v] = base[0:125, lanes(v)]
    for kind in range(5):
        for f in range(6):
            @pl.when(has[f])
            def _(kind=kind, f=f):
                remote[kind][f].wait_send()
    for level in range(2):
        for line in range(12):
            @pl.when(both[line])
            def _(level=level, line=line):
                remote_lines[level][line].wait_send()


def body(*args):
    constants = [jnp.asarray(table) for table in tables().values()]
    vmem = pltpu.VMEM
    raw = [vmem(a.shape, a.dtype) for a in args]
    held = [vmem(t.shape, t.dtype) for t in constants]
    work = [
        vmem((128, 640), F32), vmem((128, 640), F32), vmem((128, 640), F32), vmem((128, 640), F32),
        vmem((384, 640), BF16), vmem((384, 640), F32),
        vmem((192, 640), F32), vmem((192, 640), F32), vmem((192, 640), F32), vmem((192, 640), F32),
        vmem((576, 640), BF16), vmem((6, 128, 128), F32), vmem((6, 128, 128), F32),
        vmem((192, 640), F32), vmem((384, 640), F32), vmem((96, 640), F32),
        vmem((192, 640), BF16), vmem((6, 32, 128), F32), vmem((32, 128), F32), vmem((6, 16, 128), F32),
        vmem((2, 32, 128), F32), vmem((2, 16, 128), F32),
        vmem((128, 640), F32), vmem((224, 640), F32), vmem((224, 640), F32), vmem((96, 640), BF16),
        vmem((288, 640), BF16), vmem((96, 640), F32), vmem((96, 640), F32),
        vmem((6, 48, 128), F32), vmem((6, 48, 128), F32),
        vmem((96, 640), F32), vmem((96, 640), F32), vmem((192, 640), F32), vmem((96, 640), F32),
        vmem((25, 16, 128), F32), vmem((16, 128), F32),
    ]
    fine = [vmem((rows, 128), F32) for rows in (64, 64, 16, 16, 16, 16)]
    static = [vmem((rows, 128), F32) for rows in (80, 80, 24, 24, 24, 24)]
    coarse = [vmem((rows, 128), F32) for rows in (24, 24, 8, 8, 8, 8)]
    kinds = [*fine, *fine, *static, *static, *fine, *fine, *coarse, *coarse, *coarse, *coarse]
    sems = [
        pltpu.SemaphoreType.DMA((20,)),
        pltpu.SemaphoreType.DMA((5, 6)),
        pltpu.SemaphoreType.DMA((5, 6)),
        pltpu.SemaphoreType.DMA((2, 12)),
        pltpu.SemaphoreType.DMA((2, 12)),
    ]
    anywhere = pl.BlockSpec(memory_space=pl.ANY)
    return pl.pallas_call(
        kernel,
        out_shape=pltpu.VMEM(args[0].shape, F32),
        in_specs=[anywhere] * (len(args) + len(constants)),
        out_specs=pl.BlockSpec(memory_space=pltpu.VMEM),
        scratch_shapes=raw + held + work + kinds + [vmem((2, 12, 8, 128), F32)] * 2 + sems,
        compiler_params=pltpu.CompilerParams(
            collective_id=0, has_side_effects=True, vmem_limit_bytes=60 * 1024 * 1024
        ),
    )(*args, *constants)


def solution(mesh):
    in_specs = (
        P(None, None, AXES),
        P(None, None, AXES),
        P(None, AXES),
        P(None, None, AXES),
        P(None, AXES),
        P(*AXES),
        P(None, None, *AXES),
    )
    return jax.shard_map(
        body, mesh=mesh, in_specs=in_specs, out_specs=P(None, None, AXES), check_vma=False
    )
```
